32 devices in a mesh: section: 2 (over x), dp: 4 (over z), tensor: 4 (over y, core).
Axes of the slice: x: 2, y: 2, z: 4, core: 2. Of those that a mesh axis runs over, the one named last changes fastest.
Arguments:
- activations: bfloat16 [2, 8, 256, 2048], P('section', 'dp', 'tensor'), may hold values from -6 to 6
- ln_gains: bfloat16 [2, 2, 2048], P('section', None, ('dp', 'tensor')), may hold values from 0.099609375 to 1.8984375
- biases: bfloat16 [2, 4, 2048], P('section', None, ('dp', 'tensor')), may hold values from -2 to 2
- w_qkv: bfloat16 [2, 2048, 3, 2048], P('section', 'dp', None, 'tensor'), may hold values from -0.125 to 0.125
- qv_bias: bfloat16 [2, 2, 16, 128], P('section', None, 'tensor', 'dp'), may hold values from -2 to 2
- w_out: bfloat16 [2, 2048, 2048], P('section', 'tensor', 'dp'), may hold values from -0.375 to 0.375
- w_up: bfloat16 [2, 2048, 8192], P('section', 'dp', 'tensor'), may hold values from -0.125 to 0.125
- up_bias: bfloat16 [2, 64, 128], P('section', 'tensor', 'dp'), may hold values from -2 to 2
- w_down: bfloat16 [2, 8192, 2048], P('section', 'tensor', 'dp'), may hold values from -0.09375 to 0.09375
- prefix: int32 [8], P('dp'), may hold values from 25 to 128
Outputs:
- block_ends: float32 [2, 8, 256, 2048], P('section', 'dp', 'tensor')
- ln_gains_grad: float32 [2, 2, 2048], P('section', None, ('dp', 'tensor'))
- biases_grad: float32 [2, 4, 2048], P('section', None, ('dp', 'tensor'))
- w_qkv_grad: float32 [2, 2048, 3, 2048], P('section', 'dp', None, 'tensor')
- qv_bias_grad: float32 [2, 2, 16, 128], P('section', None, 'tensor', 'dp')
- w_out_grad: float32 [2, 2048, 2048], P('section', 'tensor', 'dp')
- w_up_grad: float32 [2, 2048, 8192], P('section', 'dp', 'tensor')
- up_bias_grad: float32 [2, 64, 128], P('section', 'tensor', 'dp')
- w_down_grad: float32 [2, 8192, 2048], P('section', 'tensor', 'dp')
The draws below stay inside these ranges and needn't reach their ends.
All inputs are finite; a program needn't handle non-finite values.
Results may differ from the reference program's by a relative error of at most 0.02.
Values may be sent and summed in bfloat16 or wider, within the bound.
A program may use at most 192 MiB of HBM per device.

```python
import jax
import jax.numpy as jnp
from jax import lax

D = 2048
H = 16
HD = 128
FF = 8192
LEN = 256
SEQS = 8


def touch_ends(result, own_key, least, high):
    longest = result.shape.index(max(result.shape))
    spots = []
    for shift in (0, 1):
        where = [jax.random.randint(jax.random.fold_in(own_key, axis), (), 0, length) for axis, length in enumerate(result.shape)]
        where[longest] = (where[longest] + shift) % result.shape[longest]
        spots.append(tuple(where))
    return result.at[spots[0]].set(least).at[spots[1]].set(high)


def level_of(own_key, extent, shards, least, high):
    def one(position, parts):
        heights = jax.random.uniform(jax.random.fold_in(jax.random.fold_in(own_key, 6), position), (parts,), jnp.float32, least / len(shards), high / len(shards))
        return jnp.repeat(jnp.exp(heights), extent[position] // parts).reshape((-1,) + (1,) * (len(extent) - position - 1))

    factor_of = one(*shards[0])
    for cut in shards[1:]:
        factor_of = factor_of * one(*cut)
    return factor_of


def scatter_about(stream_key, dims, width, bound, shards=(), held_as=jnp.bfloat16):
    level = level_of(stream_key, dims, shards, -0.22, 0.18) if shards else 1.0
    result = jax.random.normal(stream_key, dims, jnp.float32) * width * level
    return jnp.minimum(jnp.maximum(result, -bound), bound).astype(held_as)


def setup_inputs(seed: int = 0) -> dict:
    streams_of = jax.random.split(jax.random.key(seed), 11)
    activations = scatter_about(streams_of[0], (2, SEQS, LEN, D), 1.0, 6.0, ((0, 2), (1, 4), (2, 4)))
    ln_gains = jnp.clip(1.0 + 0.18 * jax.random.normal(streams_of[1], (2, 2, D), jnp.float32), 0.099609375, 1.8984375).astype(jnp.bfloat16)
    biases = scatter_about(streams_of[2], (2, 4, D), 0.3, 2.0, ((0, 2), (2, 16)))
    w_qkv = scatter_about(streams_of[3], (2, D, 3, D), D ** -0.5, 0.125, ((0, 2), (1, 4), (3, 4)))
    qv_bias = scatter_about(streams_of[4], (2, 2, H, HD), 0.3, 2.0, ((0, 2), (2, 4), (3, 4)))
    w_out = scatter_about(streams_of[5], (2, D, D), (D // 8) ** -0.5, 0.375, ((0, 2), (1, 4), (2, 4)))
    w_up = scatter_about(streams_of[6], (2, D, FF), D ** -0.5, 0.125, ((0, 2), (1, 4), (2, 4)))
    up_bias = scatter_about(streams_of[7], (2, FF // HD, HD), 0.3, 2.0, ((0, 2), (1, 4), (2, 4)))
    w_down = scatter_about(streams_of[8], (2, FF, D), (FF // 2) ** -0.5, 0.09375, ((0, 2), (1, 4), (2, 4)))
    prefix = touch_ends(jax.random.randint(streams_of[9], (SEQS,), LEN // 10, LEN // 2 + 1), jax.random.fold_in(streams_of[9], 1), LEN // 10, (LEN // 2 + 1) - 1).astype(jnp.int32)
    return {"activations": activations, "ln_gains": ln_gains, "biases": biases, "w_qkv": w_qkv, "qv_bias": qv_bias, "w_out": w_out, "w_up": w_up, "up_bias": up_bias, "w_down": w_down, "prefix": prefix}


highest = lax.Precision.HIGHEST

@jax.custom_vjp
def low(v):
    return lax.optimization_barrier(v.astype(jnp.bfloat16)).astype(jnp.float32)

@jax.custom_vjp
def low_back(v):
    return v

def low_keep(v):
    return (low(v), None)

def low_pass(kept, grad):
    return (grad,)

def back_keep(v):
    return (v, None)

def back_low(kept, grad):
    return (low(grad),)
low.defvjp(low_keep, low_pass)
low_back.defvjp(back_keep, back_low)

def layer_norm(hidden, gain, shift_vec):
    centre = hidden - lax.optimization_barrier(jnp.mean(hidden, axis=-1, keepdims=True))
    spread = lax.optimization_barrier(jnp.mean(centre * centre, axis=-1, keepdims=True))
    return centre * lax.rsqrt(spread + 1e-05) * gain + shift_vec

def one_layer(hidden, length, params):
    ln_gains, biases, w_qkv, qv_bias, w_out, w_up, up_bias, w_down = params
    seq_len = hidden.shape[0]
    model_width = hidden.shape[1]
    num_heads = qv_bias.shape[1]
    head_dim = qv_bias.shape[2]
    normed = low(layer_norm(hidden, ln_gains[0], biases[0]))
    proj = jnp.einsum('td,dcf->ctf', normed, w_qkv, precision=highest)
    queries = low(low_back(proj[0] + qv_bias[0].reshape(model_width))).reshape(seq_len, num_heads, head_dim)
    keys_proj = low(low_back(proj[1])).reshape(seq_len, num_heads, head_dim)
    values_proj = low(low_back(proj[2] + qv_bias[1].reshape(model_width))).reshape(seq_len, num_heads, head_dim)
    raw_scores = low_back(jnp.einsum('qhe,khe->hqk', queries, keys_proj, precision=highest))
    positions = jnp.arange(seq_len)
    offsets = (positions[:, None] - positions[None, :]).astype(jnp.float32)
    slopes = jnp.exp2(-8.0 * (jnp.arange(num_heads).astype(jnp.float32) + 1.0) / num_heads)
    allowed = (positions[None, :] <= positions[:, None]) | (positions[None, :] < length)
    scores = raw_scores * head_dim ** (-0.5) - slopes[:, None, None] * offsets
    scores = jnp.where(allowed, scores, -1e+30)
    attention_probs = low(jax.nn.softmax(scores, axis=-1))
    mixed_heads = low(low_back(jnp.einsum('hqk,khe->qhe', attention_probs, values_proj, precision=highest)))
    mixed_heads = mixed_heads.reshape(seq_len, model_width)
    branch = low_back(jnp.dot(mixed_heads, w_out, precision=highest))
    middle = hidden + branch + biases[2]
    second = low(layer_norm(middle, ln_gains[1], biases[1]))
    up_proj = low_back(jnp.dot(second, w_up, precision=highest) + up_bias.reshape(-1))
    activated = low(jax.nn.gelu(up_proj, approximate=True))
    return middle + low_back(jnp.dot(activated, w_down, precision=highest)) + biases[3]

def reference(activations, ln_gains, biases, w_qkv, qv_bias, w_out, w_up, up_bias, w_down, prefix):
    weights = (ln_gains, biases, w_qkv, qv_bias, w_out, w_up, up_bias, w_down)
    weights = tuple((weight.astype(jnp.float32) for weight in weights))

    def scan_step(grad_total, item):
        inputs, cotangent, length = item

        def model(source, params):
            carried = low(low_back(one_layer(source, length, tuple((param[0] for param in params)))))
            return one_layer(carried, length, tuple((param[1] for param in params)))
        output, pullback = jax.vjp(model, inputs.astype(jnp.float32), weights)
        grad_input, grad_weights = pullback(cotangent.astype(jnp.float32))
        grad_total = jax.tree.map(jnp.add, grad_total, grad_weights)
        return (grad_total, (grad_input, output))
    zeros = jax.tree.map(jnp.zeros_like, weights)
    grad_total, (grad_input, output) = lax.scan(scan_step, zeros, (activations[0], activations[1], prefix))
    block_ends = jnp.stack([grad_input, output])
    return (block_ends, grad_total[0], grad_total[1], grad_total[2], grad_total[3], grad_total[4], grad_total[5], grad_total[6], grad_total[7])
```

```python
import jax
import jax.numpy as jnp
from jax import lax
from jax.sharding import PartitionSpec as P

BF = jnp.bfloat16
F32 = jnp.float32


def hop(block, axis, pairs):
    return lax.ppermute(block, axis, pairs)


def swap(block, axis, distance):
    return lax.ppermute(block, axis, [(i, i ^ distance) for i in range(lax.axis_size(axis))])


def after(value, *others):
    return lax.optimization_barrier((value,) + others)[0]


def dslice(block, start, size, axis):
    return lax.dynamic_slice_in_dim(block, start, size, axis)


def layer_norm(hidden, gain, shift_vec):
    centre = hidden - jnp.mean(hidden, axis=-1, keepdims=True)
    spread = jnp.mean(centre * centre, axis=-1, keepdims=True)
    return centre * lax.rsqrt(spread + 1e-05) * gain + shift_vec


def layer_norm_back(hidden, gain, grad):
    centre = hidden - jnp.mean(hidden, axis=-1, keepdims=True)
    spread = jnp.mean(centre * centre, axis=-1, keepdims=True)
    scale = lax.rsqrt(spread + 1e-05)
    unit = centre * scale
    scaled = grad * gain
    inner = jnp.mean(scaled * unit, axis=-1, keepdims=True)
    back = (scaled - jnp.mean(scaled, axis=-1, keepdims=True) - unit * inner) * scale
    return back, jnp.sum(grad * unit, axis=0), jnp.sum(grad, axis=0)


def spread_rows(rows):
    other = swap(rows, "tensor", 2)
    near = swap(rows, "tensor", 1)
    far = swap(other, "tensor", 1)
    return jnp.concatenate([rows, near, other, far], axis=0)


def collect_rows(terms):
    size = terms.shape[0] // 4
    part = terms.reshape(4, size, -1)
    got = swap(jnp.stack([part[1], part[3]]).astype(BF), "tensor", 1).astype(F32)
    away = swap((part[2] + got[1]).astype(BF), "tensor", 2).astype(F32)
    return part[0] + got[0] + away


def spread_pair(rows):
    size = rows.shape[0]
    half = size // 2
    plane = swap(rows, "dp", 1)
    chip = swap(rows, "tensor", 2)
    corner_a = swap(plane[:half], "tensor", 2)
    corner_b = swap(chip[half:], "dp", 1)
    near = swap(rows, "tensor", 1)
    rest = jnp.concatenate([chip, plane, corner_a, corner_b], axis=0)
    far = swap(rest, "tensor", 1)
    return jnp.concatenate([rows, rest, near, far], axis=0)


def collect_pair(terms):
    size = terms.shape[0] // 8
    half = size // 2
    got = swap(terms[4 * size :].astype(BF), "tensor", 1).astype(F32)
    total = terms[: 4 * size] + got
    own, chip, plane, corner = (total[i * size : (i + 1) * size] for i in range(4))
    one = swap(corner[:half].astype(BF), "tensor", 2).astype(F32)
    two = swap(corner[half:].astype(BF), "dp", 1).astype(F32)
    plane = jnp.concatenate([plane[:half] + one, plane[half:]], axis=0)
    chip = jnp.concatenate([chip[:half], chip[half:] + two], axis=0)
    return own + swap(chip.astype(BF), "tensor", 2).astype(F32) + swap(plane.astype(BF), "dp", 1).astype(F32)


def gather_line(pack, layer, is_layer):
    count = lax.axis_size("dp")
    plane = lax.axis_index("dp")
    half = pack.shape[0] // 2
    away = hop(pack[half:], "section", [(layer, 1 - layer)])
    held = jnp.where(is_layer, pack[:half], away)
    right, left = held, held
    rights, lefts = [], []
    for step in range(1, count):
        right = hop(right, "dp", [(i, i + 1) for i in range(step - 1, count - 1)])
        left = hop(left, "dp", [(i + 1, i) for i in range(count - step)])
        rights.append(right)
        lefts.append(left)
    full = jnp.zeros((count,) + pack.shape, pack.dtype)
    full = lax.dynamic_update_slice(full, pack[None], (plane, 0, 0))
    for step in range(1, count):
        block = rights[step - 1] + lefts[count - step - 1]
        home = hop(block, "section", [(1 - layer, layer)])
        both = jnp.concatenate([block, home], axis=0)
        full = lax.dynamic_update_slice(full, both[None], (lax.rem(plane - step + count, count), 0, 0))
    return full


def gather_pair(own, sends, layer, is_layer):
    count = lax.axis_size("dp")
    plane = lax.axis_index("dp")
    half = own.shape[0] // 2
    full = jnp.zeros((count,) + own.shape, own.dtype)
    full = lax.dynamic_update_slice(full, own[None], (plane, 0, 0))
    for distance in range(1, count):
        block = sends[distance & 1]
        away = hop(block[half:], "section", [(layer, 1 - layer)])
        held = jnp.where(is_layer, block[:half], away)
        got = swap(held, "dp", distance)
        home = hop(got, "section", [(1 - layer, layer)])
        both = jnp.concatenate([got, home], axis=0)
        full = lax.dynamic_update_slice(full, both[None], (plane ^ distance, 0, 0))
    return full


def scatter_line(full, layer, is_layer):
    count = lax.axis_size("dp")
    plane = lax.axis_index("dp")
    half = full.shape[1] // 2

    def block(offset):
        return dslice(full, lax.rem(plane + offset, count), 1, 0)[0]

    own = block(0).astype(F32)
    held = {}
    for offset in range(1, count):
        piece = block(offset)
        away = hop(piece[half:], "section", [(layer, 1 - layer)])
        held[offset] = jnp.where(is_layer, piece[:half], away)
    right = left = None
    for step in range(count - 1):
        to_right, to_left = held[count - 1 - step], held[step + 1]
        if right is not None:
            to_right = (to_right.astype(F32) + right.astype(F32)).astype(BF)
            to_left = (to_left.astype(F32) + left.astype(F32)).astype(BF)
        right = hop(to_right, "dp", [(i, i + 1) for i in range(step + 1)])
        left = hop(to_left, "dp", [(i, i - 1) for i in range(count - 1, count - 2 - step, -1)])
    total = right.astype(F32) + left.astype(F32)
    home = hop(total.astype(BF), "section", [(1 - layer, layer)]).astype(F32)
    return own + jnp.concatenate([total, home], axis=0)


def scatter_pair(full, layer, is_layer):
    count = lax.axis_size("dp")
    plane = lax.axis_index("dp")
    half = full.shape[1] // 2
    sums = [None, None]
    for distance in range(1, count):
        piece = dslice(full, plane ^ distance, 1, 0)[0]
        away = hop(piece[half:], "section", [(layer, 1 - layer)])
        held = jnp.where(is_layer, piece[:half], away)
        got = swap(held, "dp", distance).astype(F32)
        odd = distance & 1
        sums[odd] = got if sums[odd] is None else sums[odd] + got
    own = dslice(full, plane, 1, 0)[0].astype(F32)
    results = []
    for part in sums:
        home = hop(part.astype(BF), "section", [(1 - layer, layer)]).astype(F32)
        results.append(jnp.concatenate([part, home], axis=0))
    return own + results[0], results[1]


def score_block(queries, keys, length, slopes, positions):
    raw = jnp.einsum("qhe,khe->hqk", queries, keys, preferred_element_type=F32)
    offsets = (positions[:, None] - positions[None, :]).astype(F32)
    allowed = (positions[None, :] <= positions[:, None]) | (positions[None, :] < length)
    scores = raw * queries.shape[2] ** (-0.5) - slopes[:, None, None] * offsets
    return jnp.where(allowed, scores, -1e30)


def attend(proj, qv_bias, length, slopes, positions):
    heads, size = qv_bias.shape[1:]
    seq_len = proj.shape[0]
    flat = qv_bias.astype(F32).reshape(2, heads * size)
    wide = heads * size
    queries = (proj[:, :wide] + flat[0]).astype(BF).reshape(seq_len, heads, size)
    keys = proj[:, wide : 2 * wide].astype(BF).reshape(seq_len, heads, size)
    values = (proj[:, 2 * wide :] + flat[1]).astype(BF).reshape(seq_len, heads, size)
    scores = score_block(queries, keys, length, slopes, positions)
    peak = jnp.max(scores, axis=-1, keepdims=True)
    expon = jnp.exp(scores - peak)
    total = jnp.sum(expon, axis=-1, keepdims=True)
    probs = (expon / total).astype(BF)
    mixed = jnp.einsum("hqk,khe->qhe", probs, values, preferred_element_type=F32)
    mixed = mixed.astype(BF).reshape(seq_len, wide)
    return mixed, (queries, keys, values, (peak + jnp.log(total))[..., 0])


def attend_back(grad_mixed, kept, length, slopes, positions):
    queries, keys, values, log_total = kept
    seq_len, heads, size = queries.shape
    grad_heads = grad_mixed.reshape(seq_len, heads, size)
    scores = score_block(queries, keys, length, slopes, positions)
    probs = jnp.exp(scores - log_total[..., None])
    grad_probs = jnp.einsum("qhe,khe->hqk", grad_heads, values, preferred_element_type=F32)
    inner = jnp.sum(probs * grad_probs, axis=-1, keepdims=True)
    grad_raw = (probs * (grad_probs - inner) * size ** (-0.5)).astype(BF)
    grad_q = jnp.einsum("hqk,khe->qhe", grad_raw, keys, preferred_element_type=F32).astype(BF)
    grad_k = jnp.einsum("hqk,qhe->khe", grad_raw, queries, preferred_element_type=F32).astype(BF)
    grad_v = jnp.einsum(
        "hqk,qhe->khe", probs.astype(BF), grad_heads, preferred_element_type=F32
    ).astype(BF)
    return jnp.concatenate([g.reshape(seq_len, heads * size) for g in (grad_q, grad_k, grad_v)], axis=1)


def forward(hidden, lengths, weights, gains, shifts, qv_bias, up_bias, slopes, positions):
    w_qkv, w_out, w_up, w_down = weights
    normed, heads, mixed_all, middle, second = [], [], [], [], []
    for seq, rows in enumerate(hidden):
        full = spread_rows(layer_norm(rows, gains[0], shifts[0]).astype(BF))
        proj = jnp.dot(full, w_qkv, preferred_element_type=F32)
        mixed, kept = attend(proj, qv_bias, lengths[seq], slopes, positions)
        branch = jnp.einsum("tf,zfd->tzd", mixed, w_out, preferred_element_type=F32)
        mid = rows + collect_rows(branch.reshape(full.shape)) + shifts[2]
        normed.append(full)
        heads.append(kept)
        mixed_all.append(mixed)
        middle.append(mid)
        second.append(layer_norm(mid, gains[1], shifts[1]).astype(BF))
    second = spread_pair(jnp.concatenate(second, axis=0))
    up = jnp.dot(second, w_up, preferred_element_type=F32) + up_bias
    act = jax.nn.gelu(up, approximate=True).astype(BF)
    branch = jnp.einsum("tf,zfd->tzd", act, w_down, preferred_element_type=F32)
    branch = collect_pair(branch.reshape(second.shape))
    output = jnp.concatenate(middle, axis=0) + branch + shifts[3]
    return output, (hidden, normed, heads, mixed_all, middle, second, up, act)


def backward(grad_out, grad_pair, kept, lengths, weights, gains, slopes, positions, planes):
    hidden, normed, heads, mixed_all, middle, second, up, act = kept
    w_qkv, w_out, w_up, w_down = weights
    width = grad_out.shape[1]
    part = width // planes
    rows = hidden[0].shape[0]
    grad_down_bias = jnp.sum(grad_out, axis=0)
    blocks = grad_pair.reshape(-1, planes, part)
    grad_act = jnp.einsum("tzd,zfd->tf", blocks, w_down, preferred_element_type=F32)
    unused, pull = jax.vjp(lambda v: jax.nn.gelu(v, approximate=True), up)
    grad_up = pull(grad_act)[0].astype(BF)
    grad_second = jnp.einsum("tf,df->td", grad_up, w_up, preferred_element_type=F32)
    grad_w_down = jnp.einsum("tf,tzd->zfd", act, blocks, preferred_element_type=F32).astype(BF)
    grad_w_up = jnp.einsum("td,tf->df", second, grad_up, preferred_element_type=F32).astype(BF)
    grad_up_bias = jnp.sum(grad_up.astype(F32), axis=0)
    grad_second = collect_pair(grad_second)
    back, gain_two, shift_two = layer_norm_back(jnp.concatenate(middle, axis=0), gains[1], grad_second)
    grad_middle = grad_out + back
    grad_out_bias = jnp.sum(grad_middle, axis=0)
    grad_proj_all, grad_mid_all, grad_normed = [], [], []
    for seq in range(len(hidden)):
        full = spread_rows(grad_middle[seq * rows : (seq + 1) * rows].astype(BF))
        mid = full.reshape(-1, planes, part)
        grad_mixed = jnp.einsum("tzd,zfd->tf", mid, w_out, preferred_element_type=F32).astype(BF)
        grad_proj = attend_back(grad_mixed, heads[seq], lengths[seq], slopes, positions)
        term = jnp.einsum("tf,df->td", grad_proj, w_qkv, preferred_element_type=F32)
        grad_normed.append(collect_rows(term))
        grad_proj_all.append(grad_proj)
        grad_mid_all.append(mid)
    grad_proj = jnp.concatenate(grad_proj_all, axis=0)
    grad_w_out = jnp.einsum(
        "tf,tzd->zfd",
        jnp.concatenate(mixed_all, axis=0),
        jnp.concatenate(grad_mid_all, axis=0),
        preferred_element_type=F32,
    ).astype(BF)
    grad_w_qkv = jnp.einsum(
        "td,tf->df", jnp.concatenate(normed, axis=0), grad_proj, preferred_element_type=F32
    ).astype(BF)
    proj_sums = jnp.sum(grad_proj.astype(F32), axis=0)
    back, gain_one, shift_one = layer_norm_back(
        jnp.concatenate(hidden, axis=0), gains[0], jnp.concatenate(grad_normed, axis=0)
    )
    vectors = jnp.stack([gain_one, gain_two, shift_one, shift_two, grad_out_bias, grad_down_bias])
    return (
        grad_middle + back,
        (grad_w_qkv, grad_w_out, grad_w_up, grad_w_down),
        (vectors, proj_sums, grad_up_bias),
    )


def on_device(activations, ln_gains, biases, w_qkv, qv_bias, w_out, w_up, up_bias, w_down, prefix):
    is_first = lax.axis_index("section") == 0
    plane = lax.axis_index("dp")
    place = lax.axis_index("tensor")
    planes = lax.axis_size("dp")
    tensors = lax.axis_size("tensor")
    odd = plane % 2 == 1
    seqs, rows, width = activations.shape[1:]
    heads, size_part = qv_bias.shape[2:]
    size = size_part * planes
    wide = heads * size
    deep = w_qkv.shape[1]
    units = w_up.shape[2]
    half = units // 2
    own = activations[0]

    flat = jnp.concatenate([v.reshape(-1) for v in (ln_gains, biases, qv_bias, up_bias)])
    everyone = lax.all_gather(flat, ("dp", "tensor"), axis=0)
    lane = width // (planes * tensors)
    cut = 6 * lane
    features = everyone[:, :cut].reshape(-1, 6, lane).swapaxes(0, 1).reshape(6, width).astype(F32)
    gains, shifts = features[:2], features[2:]
    mine = everyone.reshape(planes, tensors, -1)
    mine = lax.dynamic_index_in_dim(mine, place, 1, keepdims=False)[:, cut:]
    qv_full = mine[:, : 2 * heads * size_part].reshape(planes, 2, heads, size_part)
    qv_full = qv_full.transpose(1, 2, 0, 3).reshape(2, heads, size)
    up_full = mine[:, 2 * heads * size_part :].reshape(planes, up_bias.shape[1], up_bias.shape[2])
    up_full = up_full.transpose(1, 0, 2).reshape(units).astype(F32)
    up_own = jnp.where(odd, up_full[half:], up_full[:half])

    head_ids = place * heads + jnp.arange(heads)
    slopes = jnp.exp2(-8.0 * (head_ids.astype(F32) + 1.0) / (heads * tensors))
    positions = jnp.concatenate([(place ^ j) * rows + jnp.arange(rows) for j in range(tensors)])

    pack = jnp.concatenate([w_qkv[0].reshape(deep, 3 * wide), w_out[0].reshape(deep, wide)], axis=1)
    up_parts = (w_up[0][:, :half], w_up[0][:, half:])
    down_parts = (w_down[0][:half], w_down[0][half:])
    up_keep = jnp.where(odd, up_parts[1], up_parts[0])
    up_send = jnp.where(odd, up_parts[0], up_parts[1])
    down_keep = jnp.where(odd, down_parts[1], down_parts[0])
    down_send = jnp.where(odd, down_parts[0], down_parts[1])

    def gather(layer, pack, up_keep, up_send, down_keep, down_send):
        is_layer = is_first if layer == 0 else ~is_first
        line = gather_line(pack, layer, is_layer)
        up = gather_pair(up_keep, (up_keep, up_send), layer, is_layer)
        down = gather_pair(down_keep, (down_keep, down_send), layer, is_layer)
        full_out = line[:, :, 3 * wide :].reshape(planes, wide, deep)
        return (
            line[:, :, : 3 * wide].reshape(planes * deep, 3 * wide),
            full_out,
            up.reshape(planes * deep, half),
            down,
        )

    shards = (pack, up_keep, up_send, down_keep, down_send)
    first_weights = gather(0, *shards)
    shards = lax.optimization_barrier((shards, first_weights[3]))[0]
    second_weights = gather(1, *shards)

    common = (gains, shifts, qv_full, up_own, slopes, positions)
    source = [own[s].astype(F32) for s in range(seqs)]
    grad_top = own.reshape(seqs * rows, width)
    grad_top_pair = spread_pair(grad_top)
    output, kept_first = forward(source, prefix, first_weights, *common)
    carried = hop(output.astype(BF), "section", [(0, 1)]).astype(F32)
    source = [carried[s * rows : (s + 1) * rows] for s in range(seqs)]
    output, kept_second = forward(source, prefix, second_weights, *common)

    back_common = (gains, slopes, positions, planes)
    grad_mid, grads_top, sums_top = backward(
        grad_top.astype(F32), grad_top_pair, kept_second, prefix, second_weights, *back_common
    )

    def scatter(layer, grads):
        is_layer = is_first if layer == 0 else ~is_first
        g_qkv, g_out, g_up, g_down = grads
        down = scatter_pair(g_down, layer, is_layer)
        up = scatter_pair(g_up.reshape(planes, deep, half), layer, is_layer)
        line = jnp.concatenate(
            [g_qkv.reshape(planes, deep, 3 * wide), g_out.reshape(planes, deep, wide)], axis=2
        )
        line = scatter_line(line, layer, is_layer)
        return line, up, down

    scattered_top = scatter(1, grads_top)
    returned = hop(grad_mid.astype(BF), "section", [(1, 0)])
    grad_low, grads_low, sums_low = backward(
        returned.astype(F32), spread_pair(returned), kept_first, prefix, first_weights, *back_common
    )
    scattered_low = scatter(0, grads_low)

    line, up, down = jax.tree.map(lambda a, b: jnp.where(is_first, a, b), scattered_low, scattered_top)
    vectors, proj_sums, up_sums = jax.tree.map(lambda a, b: jnp.where(is_first, a, b), sums_low, sums_top)
    up_grad = jnp.where(odd, jnp.concatenate([up[1], up[0]], axis=1), jnp.concatenate(up, axis=1))
    down_grad = jnp.where(odd, jnp.concatenate([down[1], down[0]], axis=0), jnp.concatenate(down, axis=0))

    vec = vectors.reshape(6, planes * tensors, lane).swapaxes(0, 1).reshape(planes * tensors, cut)
    qv_sums = jnp.stack([proj_sums[:wide], proj_sums[2 * wide :]]).reshape(2, heads, planes, size_part)
    qv_sums = qv_sums.transpose(2, 0, 1, 3).reshape(planes, -1)
    zero = jnp.zeros_like(up_sums)
    up_sums = jnp.where(odd, jnp.concatenate([zero, up_sums]), jnp.concatenate([up_sums, zero]))
    up_sums = up_sums.reshape(up_bias.shape[1], planes, up_bias.shape[2]).transpose(1, 0, 2).reshape(planes, -1)
    own_part = jnp.concatenate([qv_sums, up_sums], axis=1)[:, None, :]
    own_part = jnp.where((jnp.arange(tensors) == place)[None, :, None], own_part, 0.0)
    message = jnp.concatenate([vec, own_part.reshape(planes * tensors, -1)], axis=1)
    small = lax.psum_scatter(message, ("dp", "tensor"), scatter_dimension=0, tiled=False)
    mid = cut + 2 * heads * size_part

    ends = jnp.where(is_first, grad_low, output).reshape(seqs, rows, width)
    return (
        ends[None],
        small[: 2 * lane].reshape(1, 2, lane),
        small[2 * lane : cut].reshape(1, 4, lane),
        line[:, : 3 * wide].reshape(1, deep, 3, wide),
        small[cut:mid].reshape(1, 2, heads, size_part),
        line[:, 3 * wide :].reshape(1, wide, deep),
        up_grad[None],
        small[mid:].reshape(1, up_bias.shape[1], up_bias.shape[2]),
        down_grad[None],
    )


def solution(mesh):
    in_specs = (
        P("section", "dp", "tensor", None),
        P("section", None, ("dp", "tensor")),
        P("section", None, ("dp", "tensor")),
        P("section", "dp", None, "tensor"),
        P("section", None, "tensor", "dp"),
        P("section", "tensor", "dp"),
        P("section", "dp", "tensor"),
        P("section", "tensor", "dp"),
        P("section", "tensor", "dp"),
        P("dp"),
    )
    out_specs = (
        P("section", "dp", "tensor", None),
        P("section", None, ("dp", "tensor")),
        P("section", None, ("dp", "tensor")),
        P("section", "dp", None, "tensor"),
        P("section", None, "tensor", "dp"),
        P("section", "tensor", "dp"),
        P("section", "dp", "tensor"),
        P("section", "tensor", "dp"),
        P("section", "tensor", "dp"),
    )
    return jax.shard_map(
        on_device, mesh=mesh, in_specs=in_specs, out_specs=out_specs, check_vma=False
    )
```

```python
import functools

import jax
import jax.numpy as jnp
import numpy as np
from jax import lax
from jax.experimental import pallas as pl
from jax.experimental.pallas import tpu as pltpu
from jax.sharding import PartitionSpec as P

BF = jnp.bfloat16
F32 = jnp.float32


def hop(block, axis, pairs):
    return lax.ppermute(block, axis, pairs)


def swap(block, axis, distance):
    return lax.ppermute(block, axis, [(i, i ^ distance) for i in range(lax.axis_size(axis))])


def after(value, *others):
    return lax.optimization_barrier((value,) + others)[0]


def dslice(block, start, size, axis):
    return lax.dynamic_slice_in_dim(block, start, size, axis)


def layer_norm(hidden, gain, shift_vec):
    centre = hidden - jnp.mean(hidden, axis=-1, keepdims=True)
    spread = jnp.mean(centre * centre, axis=-1, keepdims=True)
    return centre * lax.rsqrt(spread + 1e-05) * gain + shift_vec


def layer_norm_back(hidden, gain, grad):
    centre = hidden - jnp.mean(hidden, axis=-1, keepdims=True)
    spread = jnp.mean(centre * centre, axis=-1, keepdims=True)
    scale = lax.rsqrt(spread + 1e-05)
    unit = centre * scale
    scaled = grad * gain
    inner = jnp.mean(scaled * unit, axis=-1, keepdims=True)
    back = (scaled - jnp.mean(scaled, axis=-1, keepdims=True) - unit * inner) * scale
    return back, jnp.sum(grad * unit, axis=0), jnp.sum(grad, axis=0)


def spread_rows(rows):
    other = swap(rows, "tensor", 2)
    near = swap(rows, "tensor", 1)
    far = swap(other, "tensor", 1)
    return jnp.concatenate([rows, near, other, far], axis=0)


def collect_rows(terms):
    size = terms.shape[0] // 4
    part = terms.reshape(4, size, -1)
    got = swap(jnp.stack([part[1], part[3]]).astype(BF), "tensor", 1).astype(F32)
    away = swap((part[2] + got[1]).astype(BF), "tensor", 2).astype(F32)
    return part[0] + got[0] + away


def spread_pair(rows):
    size = rows.shape[0]
    half = size // 2
    plane = swap(rows, "dp", 1)
    chip = swap(rows, "tensor", 2)
    corner_a = swap(plane[:half], "tensor", 2)
    corner_b = swap(chip[half:], "dp", 1)
    near = swap(rows, "tensor", 1)
    rest = jnp.concatenate([chip, plane, corner_a, corner_b], axis=0)
    far = swap(rest, "tensor", 1)
    return jnp.concatenate([rows, rest, near, far], axis=0)


def collect_pair(terms):
    size = terms.shape[0] // 8
    half = size // 2
    got = swap(terms[4 * size :].astype(BF), "tensor", 1).astype(F32)
    total = terms[: 4 * size] + got
    own, chip, plane, corner = (total[i * size : (i + 1) * size] for i in range(4))
    one = swap(corner[:half].astype(BF), "tensor", 2).astype(F32)
    two = swap(corner[half:].astype(BF), "dp", 1).astype(F32)
    plane = jnp.concatenate([plane[:half] + one, plane[half:]], axis=0)
    chip = jnp.concatenate([chip[:half], chip[half:] + two], axis=0)
    return own + swap(chip.astype(BF), "tensor", 2).astype(F32) + swap(plane.astype(BF), "dp", 1).astype(F32)


def scatter_line(full):
    count = lax.axis_size("dp")
    plane = lax.axis_index("dp")

    def block(offset):
        return dslice(full, lax.rem(plane + offset, count), 1, 0)[0]

    own = block(0).astype(F32)
    right = left = None
    for step in range(count - 1):
        to_right, to_left = block(count - 1 - step), block(step + 1)
        if right is not None:
            to_right = (to_right.astype(F32) + right.astype(F32)).astype(BF)
            to_left = (to_left.astype(F32) + left.astype(F32)).astype(BF)
        right = hop(to_right, "dp", [(i, i + 1) for i in range(step + 1)])
        left = hop(to_left, "dp", [(i, i - 1) for i in range(count - 1, count - 2 - step, -1)])
    return own + right.astype(F32) + left.astype(F32)


def scatter_pair(full):
    count = lax.axis_size("dp")
    plane = lax.axis_index("dp")
    sums = [dslice(full, plane, 1, 0)[0].astype(F32), None]
    for distance in range(1, count):
        piece = dslice(full, plane ^ distance, 1, 0)[0]
        got = swap(piece, "dp", distance).astype(F32)
        odd = distance & 1
        sums[odd] = got if sums[odd] is None else sums[odd] + got
    return sums


MESH = pl.DeviceIdType.MESH
NT = (((1,), (1,)), ((), ()))
TN = (((0,), (0,)), ((), ()))


def dot(a, b, dims=(((1,), (0,)), ((), ()))):
    return lax.dot_general(a, b, dims, preferred_element_type=F32)


def remote(src, dst, send_sem, recv_sem, device):
    return pltpu.make_async_remote_copy(
        src_ref=src, dst_ref=dst, send_sem=send_sem, recv_sem=recv_sem, device_id=device, device_id_type=MESH
    )


def when(condition):
    return True if condition is True else condition


def greet(devices):
    barrier = pltpu.get_barrier_semaphore()
    for device in devices:
        pl.semaphore_signal(barrier, inc=1, device_id=device, device_id_type=MESH)
    pl.semaphore_wait(barrier, len(devices))


def tiles(count, body):
    def step(i, carry):
        body(i)
        return carry

    lax.fori_loop(0, count, step, 0)


def rows_of(i, size):
    return pl.ds(pl.multiple_of(i * size, size), size)


def norm_rows(value, gain, shift_vec):
    centre = value - jnp.mean(value, axis=-1, keepdims=True)
    spread = jnp.mean(centre * centre, axis=-1, keepdims=True)
    return centre * lax.rsqrt(spread + 1e-05) * gain + shift_vec


def spots(base, shape, dim, rows):
    index = lax.broadcasted_iota(jnp.int32, shape, dim)
    return ((index // rows) ^ base) * rows + lax.rem(index, rows)


def gelu_parts(v):
    cube = v * v * v
    inner = np.float32(np.sqrt(2 / np.pi)) * (v + 0.044715 * cube)
    return jnp.tanh(inner)


def masked_scores(raw, slope, length, place, rows, size):
    gap = spots(place, raw.shape, 0, rows) - spots(place, raw.shape, 1, rows)
    open_ = (gap >= 0) | (spots(place, raw.shape, 1, rows) < length)
    scores = raw * np.float32(size ** (-0.5)) - slope * gap.astype(F32)
    return jnp.where(open_, scores, -1e30)


def forward_kernel(
    dims, x_in, vec, qvb, upb, prefix, slopes, wq_in, wo_in, wu_in, wd_in,
    out, wq, wo, wu, wd, x_out, mid_out, nb_out, qkv_out, mix_out, sec_out, up_out, act_out,
    carry, carry_send, hid, mid, nb, qkv, mix, sec, up, act, outv,
    vq, vo, vu, vd, s1, r1, part, sy, ry, part8, sc, rc, s8, r8,
    line_s, line_r, pair_s, pair_r, own_sem, load_sem, keep_sem, carry_s, carry_r,
    ag_s, ag_r, rs_s, rs_r, ag8_s, ag8_r, f8_s, f8_r, c8_s, c8_r, rs8_s, rs8_r,
):
    n, seqs, heads, size, rows, deep, half = dims
    R = seqs * rows
    wide = heads * size
    D = n * deep
    sect, z, t = lax.axis_index("section"), lax.axis_index("dp"), lax.axis_index("tensor")
    me = (sect, z, t)
    core = (sect, z, t ^ 1)
    chip = (sect, z, t ^ 2)
    plane = (sect, z ^ 1, t)
    diag = (sect, z ^ 1, t ^ 2)
    across = (1 - sect, z, t)
    greet([(sect, z ^ k, t) for k in range(1, n)] + [core, chip, diag, across])

    zl = z & 1
    mine = [
        pltpu.make_async_copy(wq_in, wq.at[:, pl.ds(pl.multiple_of(z * deep, deep), deep)], own_sem.at[0]),
        pltpu.make_async_copy(wo_in, wo.at[z], own_sem.at[1]),
        pltpu.make_async_copy(
            wu_in.at[:, pl.ds(pl.multiple_of(zl * half, half), half)],
            wu.at[pl.ds(pl.multiple_of(z * deep, deep), deep)], own_sem.at[2]),
        pltpu.make_async_copy(
            wd_in.at[pl.ds(pl.multiple_of(zl * half, half), half)], wd.at[z], own_sem.at[3]),
    ]

    def slot(a, b):
        if a == 0:
            return wq.at[:, pl.ds(pl.multiple_of(b * deep, deep), deep)]
        return wo.at[b]

    def line(a, side, step, b):
        to = (sect, z + 1 - 2 * side, t)
        src = (wq_in, wo_in)[a] if step == 1 else slot(a, b)
        i = (a * 2 + side) * (n - 1) + step - 1
        return remote(src, slot(a, b), line_s.at[i], line_r.at[i], to)

    def line_send(a, side, step):
        b = z - (step - 1) if side == 0 else z + (step - 1)
        ok = (b >= 0) & (z < n - 1) if side == 0 else (b <= n - 1) & (z > 0)
        return ok, lambda: line(a, side, step, b)

    def line_recv(a, side, step):
        b = z - step if side == 0 else z + step
        ok = (b >= 0) if side == 0 else (b <= n - 1)
        return ok, lambda: line(a, side, step, b)

    def pair(a, k):
        h = (z ^ k) & 1
        to = (sect, z ^ k, t)
        i = a * (n - 1) + k - 1
        if a == 0:
            src = wu_in.at[:, pl.ds(pl.multiple_of(h * half, half), half)]
            dst = wu.at[pl.ds(pl.multiple_of(z * deep, deep), deep)]
        else:
            src = wd_in.at[pl.ds(pl.multiple_of(h * half, half), half)]
            dst = wd.at[z]
        return remote(src, dst, pair_s.at[i], pair_r.at[i], to)

    def pair_recv(a, k):
        i = a * (n - 1) + k - 1
        if a == 0:
            src = wu_in.at[:, pl.ds(0, half)]
            dst = wu.at[pl.ds(pl.multiple_of((z ^ k) * deep, deep), deep)]
        else:
            src = wd_in.at[pl.ds(0, half)]
            dst = wd.at[z ^ k]
        return remote(src, dst, pair_s.at[i], pair_r.at[i], (sect, z ^ k, t))

    for a in range(2):
        for side in range(2):
            ok, make = line_send(a, side, 1)

            @pl.when(ok)
            def _():
                make().start()

    for copy in mine:
        copy.start()

    tile = 32

    def first_norm():
        def body(i):
            sl = rows_of(i, tile)
            v = hid[sl, :].astype(F32)
            nb[0, sl, :] = norm_rows(v, vec[0:1, :], vec[2:3, :]).astype(BF)

        tiles(R // tile, body)

    def ag(i):
        src, to = ((0, core), (0, chip), (2, core))[i]
        dst = (1, 2, 3)[i]
        return remote(nb.at[src], nb.at[dst], ag_s.at[i], ag_r.at[i], to)

    @pl.when(sect == 0)
    def _():
        hid[...] = x_in[...]
        first_norm()
        ag(1).start()
        ag(0).start()
        ag(1).wait_recv()
        ag(2).start()

    for step in range(1, n):
        for a in range(2):
            for side in range(2):
                ok, make = line_recv(a, side, step)

                @pl.when(ok)
                def _():
                    make().wait_recv()

                if step < n - 1:
                    ok, make = line_send(a, side, step + 1)

                    @pl.when(ok)
                    def _():
                        make().start()

        if step == n - 2 or n == 2:
            for a in range(2):
                for k in range(n - 1, 0, -1):
                    pair(a, k).start()

    for copy in mine:
        copy.wait()
    load_q = pltpu.make_async_copy(wq, vq, load_sem.at[0])
    load_o = pltpu.make_async_copy(wo, vo, load_sem.at[1])
    load_q.start()
    load_o.start()

    @pl.when(sect == 1)
    def _():
        remote(carry_send, carry, carry_s, carry_r, across).wait_recv()
        hid[...] = carry[...]
        first_norm()
        ag(1).start()
        ag(0).start()
        ag(1).wait_recv()
        ag(2).start()

    ag(0).wait_recv()
    ag(2).wait_recv()
    load_q.wait()
    load_o.wait()
    keeps = []

    def keep(src, dst):
        copy = pltpu.make_async_copy(src, dst, keep_sem.at[len(keeps)])
        copy.start()
        keeps.append(copy)

    keep(hid, x_out)
    keep(nb, nb_out)

    tn = min(256, wide)
    for c in range(3):
        def body(i):
            j = lax.rem(i, wide // tn)
            b = i // (wide // tn)
            cols = rows_of(j, tn)
            lhs = jnp.concatenate([nb[2 * b], nb[2 * b + 1]], axis=0)
            got = dot(lhs, vq[c, :, cols]) + qvb[c : c + 1, cols]
            got = got.astype(BF)
            qkv[2 * b, :, pl.ds(pl.multiple_of(c * wide + j * tn, tn), tn)] = got[:R]
            qkv[2 * b + 1, :, pl.ds(pl.multiple_of(c * wide + j * tn, tn), tn)] = got[R:]

        tiles(2 * (wide // tn), body)
    keep(qkv, qkv_out)

    def head(i):
        s, h = i // heads, lax.rem(i, heads)
        pos = rows_of(s, rows)

        def part_of(c):
            cols = pl.ds(pl.multiple_of(c * wide + h * size, size), size)
            return jnp.concatenate([qkv[j, pos, cols] for j in range(4)], axis=0)

        raw = dot(part_of(0), part_of(1), NT)
        scores = masked_scores(raw, slopes[h], prefix[s], t, rows, size)
        expon = jnp.exp(scores - jnp.max(scores, axis=-1, keepdims=True))
        probs = (expon / jnp.sum(expon, axis=-1, keepdims=True)).astype(BF)
        got = dot(probs, part_of(2)).astype(BF)
        for j in range(4):
            mix[j, pos, rows_of(h, size)] = got[j * rows : (j + 1) * rows]

    tiles(seqs * heads, head)
    keep(mix, mix_out)

    def project(pair_of, put):
        lhs_blocks = pair_of

        def body(i):
            lhs = jnp.concatenate([mix[lhs_blocks[0]], mix[lhs_blocks[1]]], axis=0)
            got = dot(lhs, vo[i])
            put(rows_of(i, deep), got)

        tiles(n, body)

    def put_send(cols, got):
        s1[0, :, cols] = got[:R].astype(BF)
        s1[1, :, cols] = got[R:].astype(BF)

    def put_part(cols, got):
        part[0, :, cols] = got[:R]
        part[1, :, cols] = got[R:]

    to_core = remote(s1, r1, rs_s.at[0], rs_r.at[0], core)
    to_chip = remote(sy, ry, rs_s.at[1], rs_r.at[1], chip)
    project((3, 1), put_send)
    to_core.start()
    project((2, 0), put_part)
    to_core.wait_recv()

    def add_chip(i):
        sl = rows_of(i, tile)
        sy[sl, :] = (part[0, sl, :] + r1[0, sl, :].astype(F32)).astype(BF)

    tiles(R // tile, add_chip)
    to_chip.start()
    to_chip.wait_recv()

    def middle_body(i):
        sl = rows_of(i, tile)
        v = hid[sl, :].astype(F32) + part[1, sl, :] + r1[1, sl, :].astype(F32)
        v = v + ry[sl, :].astype(F32) + vec[4:5, :]
        mid[sl, :] = v
        sec[0, sl, :] = norm_rows(v, vec[1:2, :], vec[3:4, :]).astype(BF)

    tiles(R // tile, middle_body)
    keep(mid, mid_out)

    targets = (None, chip, plane, diag)

    def ag8(i):
        return remote(sec.at[0], sec.at[i], ag8_s.at[i], ag8_r.at[i], targets[i])

    def forward8(i):
        return remote(sec.at[i], sec.at[4 + i], f8_s.at[i], f8_r.at[i], core)

    def core8(i):
        return remote(sc.at[i], rc.at[i], c8_s.at[i], c8_r.at[i], core)

    def rs8(i):
        return remote(s8.at[i], r8.at[i], rs8_s.at[i], rs8_r.at[i], targets[i])

    order = (0, 2, 1, 3)
    for i in order[1:]:
        ag8(i).start()
    forward8(0).start()

    for a in range(2):
        for k in range(n - 1, 0, -1):
            pair_recv(a, k).wait_recv()
    load_u = pltpu.make_async_copy(wu, vu, load_sem.at[2])
    load_d = pltpu.make_async_copy(wd, vd, load_sem.at[3])
    load_u.start()
    load_d.start()
    load_u.wait()
    load_d.wait()

    tu = min(256, half)

    def group(i):
        if i:
            ag8(i).wait_recv()
            forward8(i).start()
        forward8(i).wait_recv()

        def up_body(j):
            cols = rows_of(j, tu)
            lhs = jnp.concatenate([sec[i], sec[4 + i]], axis=0)
            v = dot(lhs, vu[:, cols]) + upb[:, cols]
            g = (0.5 * v * (1.0 + gelu_parts(v))).astype(BF)
            up[i, :, cols] = v[:R]
            up[4 + i, :, cols] = v[R:]
            act[i, :, cols] = g[:R]
            act[4 + i, :, cols] = g[R:]

        tiles(half // tu, up_body)

        def down_body(j):
            cols = rows_of(j, deep)
            lhs = jnp.concatenate([act[i], act[4 + i]], axis=0)
            got = dot(lhs, vd[j])
            part8[i, :, cols] = got[:R]
            sc[i, :, cols] = got[R:].astype(BF)

        tiles(n, down_body)
        core8(i).start()

    def reduce(i):
        core8(i).wait_recv()
        if i == 0:
            return

        def body(j):
            sl = rows_of(j, tile)
            s8[i, sl, :] = (part8[i, sl, :] + rc[i, sl, :].astype(F32)).astype(BF)

        tiles(R // tile, body)
        rs8(i).start()

    for number, i in enumerate(order):
        group(i)
        if number:
            reduce(order[number - 1])
    reduce(order[-1])
    keep(sec, sec_out)
    keep(up, up_out)
    keep(act, act_out)
    for i in order[1:]:
        rs8(i).wait_recv()

    def out_body(j):
        sl = rows_of(j, tile)
        v = mid[sl, :] + part8[0, sl, :] + rc[0, sl, :].astype(F32)
        for i in (1, 2, 3):
            v = v + r8[i, sl, :].astype(F32)
        v = v + vec[5:6, :]
        outv[sl, :] = v
        carry_send[sl, :] = v.astype(BF)

    tiles(R // tile, out_body)
    over = remote(carry_send, carry, carry_s, carry_r, across)

    @pl.when(sect == 0)
    def _():
        over.start()

    keep(outv, out)

    for step in range(1, n):
        for a in range(2):
            for side in range(2):
                ok, make = line_send(a, side, step)

                @pl.when(ok)
                def _():
                    make().wait_send()

    for a in range(2):
        for k in range(n - 1, 0, -1):
            pair(a, k).wait_send()
    for i in range(3):
        ag(i).wait_send()
    to_core.wait_send()
    to_chip.wait_send()
    for i in range(4):
        if i:
            ag8(i).wait_send()
            rs8(i).wait_send()
        forward8(i).wait_send()
        core8(i).wait_send()

    @pl.when(sect == 0)
    def _():
        over.wait_send()

    for copy in keeps:
        copy.wait()


def run_forward(dims, x, vec, qvb, upb, prefix, slopes, wq, wo, wu, wd):
    n, seqs, heads, size, rows, deep, half = dims
    R, wide, D = seqs * rows, heads * size, n * deep
    V = lambda shape, dtype: pltpu.VMEM(shape, dtype)
    S = lambda *shape: jax.ShapeDtypeStruct(shape[:-1], shape[-1])
    any_ = pl.BlockSpec(memory_space=pl.ANY)
    vm = pl.BlockSpec(memory_space=pltpu.VMEM)
    sm = pl.BlockSpec(memory_space=pltpu.SMEM)
    dma = lambda k: pltpu.SemaphoreType.DMA((k,))
    outs = (
        S(R, D, F32), S(3, D, wide, BF), S(n, wide, deep, BF), S(D, half, BF), S(n, half, deep, BF),
        S(R, D, BF), S(R, D, F32), S(4, R, D, BF), S(4, R, 3 * wide, BF), S(4, R, wide, BF),
        S(8, R, D, BF), S(8, R, half, F32), S(8, R, half, BF),
    )
    scratch = [
        V((R, D), BF), V((R, D), BF), V((R, D), BF), V((R, D), F32), V((4, R, D), BF), V((4, R, 3 * wide), BF),
        V((4, R, wide), BF), V((8, R, D), BF), V((8, R, half), F32), V((8, R, half), BF), V((R, D), F32),
        V((3, D, wide), BF), V((n, wide, deep), BF), V((D, half), BF), V((n, half, deep), BF),
        V((2, R, D), BF), V((2, R, D), BF), V((2, R, D), F32), V((R, D), BF), V((R, D), BF),
        V((4, R, D), F32), V((4, R, D), BF), V((4, R, D), BF), V((4, R, D), BF), V((4, R, D), BF),
        dma(4 * (n - 1)), dma(4 * (n - 1)), dma(2 * (n - 1)), dma(2 * (n - 1)), dma(4), dma(4), dma(9),
        pltpu.SemaphoreType.DMA(()), pltpu.SemaphoreType.DMA(()),
        dma(3), dma(3), dma(2), dma(2), dma(4), dma(4), dma(4), dma(4), dma(4), dma(4), dma(4), dma(4),
    ]
    return pl.pallas_call(
        functools.partial(forward_kernel, dims),
        out_shape=outs,
        in_specs=[vm, vm, vm, vm, sm, sm, any_, any_, any_, any_],
        out_specs=(any_,) * len(outs),
        scratch_shapes=scratch,
        compiler_params=pltpu.CompilerParams(
            collective_id=0, has_side_effects=True, vmem_limit_bytes=60 * 1024 * 1024
        ),
    )(x, vec, qvb, upb, prefix, slopes, wq, wo, wu, wd)


def score_block(queries, keys, length, slopes, positions):
    raw = jnp.einsum("qhe,khe->hqk", queries, keys, preferred_element_type=F32)
    offsets = (positions[:, None] - positions[None, :]).astype(F32)
    allowed = (positions[None, :] <= positions[:, None]) | (positions[None, :] < length)
    scores = raw * queries.shape[2] ** (-0.5) - slopes[:, None, None] * offsets
    return jnp.where(allowed, scores, -1e30)


def attend_back(grad_mixed, kept, length, slopes, positions):
    queries, keys, values, log_total = kept
    seq_len, heads, size = queries.shape
    grad_heads = grad_mixed.reshape(seq_len, heads, size)
    scores = score_block(queries, keys, length, slopes, positions)
    probs = jnp.exp(scores - log_total[..., None])
    grad_probs = jnp.einsum("qhe,khe->hqk", grad_heads, values, preferred_element_type=F32)
    inner = jnp.sum(probs * grad_probs, axis=-1, keepdims=True)
    grad_raw = (probs * (grad_probs - inner) * size ** (-0.5)).astype(BF)
    grad_q = jnp.einsum("hqk,khe->qhe", grad_raw, keys, preferred_element_type=F32).astype(BF)
    grad_k = jnp.einsum("hqk,qhe->khe", grad_raw, queries, preferred_element_type=F32).astype(BF)
    grad_v = jnp.einsum(
        "hqk,qhe->khe", probs.astype(BF), grad_heads, preferred_element_type=F32
    ).astype(BF)
    return jnp.concatenate([g.reshape(seq_len, heads * size) for g in (grad_q, grad_k, grad_v)], axis=1)


def backward(grad_out, grad_pair, kept, lengths, weights, gains, slopes, positions, planes):
    hidden, normed, heads, mixed_all, middle, second, up, act = kept
    w_qkv, w_out, w_up, w_down = weights
    width = grad_out.shape[1]
    part = width // planes
    rows = hidden[0].shape[0]
    grad_down_bias = jnp.sum(grad_out, axis=0)
    blocks = grad_pair.reshape(-1, planes, part)
    grad_act = jnp.einsum("tzd,zfd->tf", blocks, w_down, preferred_element_type=F32)
    unused, pull = jax.vjp(lambda v: jax.nn.gelu(v, approximate=True), up)
    grad_up = pull(grad_act)[0].astype(BF)
    grad_second = jnp.einsum("tf,df->td", grad_up, w_up, preferred_element_type=F32)
    grad_w_down = jnp.einsum("tf,tzd->zfd", act, blocks, preferred_element_type=F32).astype(BF)
    grad_w_up = jnp.einsum("td,tf->df", second, grad_up, preferred_element_type=F32).astype(BF)
    grad_up_bias = jnp.sum(grad_up.astype(F32), axis=0)
    grad_second = collect_pair(grad_second)
    back, gain_two, shift_two = layer_norm_back(jnp.concatenate(middle, axis=0), gains[1], grad_second)
    grad_middle = grad_out + back
    grad_out_bias = jnp.sum(grad_middle, axis=0)
    grad_proj_all, grad_mid_all, grad_normed = [], [], []
    for seq in range(len(hidden)):
        full = spread_rows(grad_middle[seq * rows : (seq + 1) * rows].astype(BF))
        mid = full.reshape(-1, planes, part)
        grad_mixed = jnp.einsum("tzd,zfd->tf", mid, w_out, preferred_element_type=F32).astype(BF)
        grad_proj = attend_back(grad_mixed, heads[seq], lengths[seq], slopes, positions)
        term = jnp.einsum("tf,df->td", grad_proj, w_qkv, preferred_element_type=F32)
        grad_normed.append(collect_rows(term))
        grad_proj_all.append(grad_proj)
        grad_mid_all.append(mid)
    grad_proj = jnp.concatenate(grad_proj_all, axis=0)
    grad_w_out = jnp.einsum(
        "tf,tzd->zfd",
        jnp.concatenate(mixed_all, axis=0),
        jnp.concatenate(grad_mid_all, axis=0),
        preferred_element_type=F32,
    ).astype(BF)
    grad_w_qkv = jnp.einsum(
        "td,tf->df", jnp.concatenate(normed, axis=0), grad_proj, preferred_element_type=F32
    ).astype(BF)
    proj_sums = jnp.sum(grad_proj.astype(F32), axis=0)
    back, gain_one, shift_one = layer_norm_back(
        jnp.concatenate(hidden, axis=0), gains[0], jnp.concatenate(grad_normed, axis=0)
    )
    vectors = jnp.stack([gain_one, gain_two, shift_one, shift_two, grad_out_bias, grad_down_bias])
    return (
        grad_middle + back,
        (grad_w_qkv, grad_w_out, grad_w_up, grad_w_down),
        (vectors, proj_sums, grad_up_bias),
    )


def on_device(activations, ln_gains, biases, w_qkv, qv_bias, w_out, w_up, up_bias, w_down, prefix):
    is_first = lax.axis_index("section") == 0
    plane = lax.axis_index("dp")
    place = lax.axis_index("tensor")
    planes = lax.axis_size("dp")
    tensors = lax.axis_size("tensor")
    odd = plane % 2 == 1
    seqs, rows, width = activations.shape[1:]
    heads, size_part = qv_bias.shape[2:]
    size = size_part * planes
    wide = heads * size
    deep = w_qkv.shape[1]
    units = w_up.shape[2]
    half = units // 2
    own = activations[0]

    flat = jnp.concatenate([v.reshape(-1) for v in (ln_gains, biases, qv_bias, up_bias)])
    everyone = lax.all_gather(flat, ("dp", "tensor"), axis=0)
    lane = width // (planes * tensors)
    cut = 6 * lane
    features = everyone[:, :cut].reshape(-1, 6, lane).swapaxes(0, 1).reshape(6, width).astype(F32)
    gains, shifts = features[:2], features[2:]
    mine = everyone.reshape(planes, tensors, -1)
    mine = lax.dynamic_index_in_dim(mine, place, 1, keepdims=False)[:, cut:]
    qv_full = mine[:, : 2 * heads * size_part].reshape(planes, 2, heads, size_part)
    qv_full = qv_full.transpose(1, 2, 0, 3).reshape(2, heads, size)
    up_full = mine[:, 2 * heads * size_part :].reshape(planes, up_bias.shape[1], up_bias.shape[2])
    up_full = up_full.transpose(1, 0, 2).reshape(units).astype(F32)
    up_own = jnp.where(odd, up_full[half:], up_full[:half])

    head_ids = place * heads + jnp.arange(heads)
    slopes = jnp.exp2(-8.0 * (head_ids.astype(F32) + 1.0) / (heads * tensors))
    positions = jnp.concatenate([(place ^ j) * rows + jnp.arange(rows) for j in range(tensors)])

    dims = (planes, seqs, heads, size, rows, deep, half)
    vec = jnp.concatenate([features, jnp.zeros((2, width), F32)], axis=0)
    flat_qv = qv_full.astype(F32).reshape(2, wide)
    qvb = jnp.stack([flat_qv[0], jnp.zeros_like(flat_qv[0]), flat_qv[1]])
    got = run_forward(
        dims, own.reshape(seqs * rows, width), vec, qvb, up_own[None], prefix, slopes,
        w_qkv[0].transpose(1, 0, 2), w_out[0], w_up[0], w_down[0],
    )
    output, wq, wo, wu, wd, hid, mid, nb, qkv, mix, sec, up, act = got
    R = seqs * rows
    def per_seq(a):
        a = a.reshape(4, seqs, rows, -1)
        return [a[:, s].reshape(4 * rows, -1) for s in range(seqs)]
    heads_kept = []
    for s, v in enumerate(per_seq(qkv)):
        q, k, w = (v[:, c * wide : (c + 1) * wide].reshape(4 * rows, heads, size) for c in range(3))
        sc = score_block(q, k, prefix[s], slopes, positions)
        heads_kept.append((q, k, w, jax.nn.logsumexp(sc, axis=-1)))
    hid = hid.astype(F32)
    kept = (
        [hid[s * rows : (s + 1) * rows] for s in range(seqs)], per_seq(nb), heads_kept, per_seq(mix),
        [mid[s * rows : (s + 1) * rows] for s in range(seqs)], sec.reshape(8 * R, width),
        up.reshape(8 * R, half), act.reshape(8 * R, half),
    )
    full_q = wq.transpose(1, 0, 2).reshape(planes * deep, 3 * wide)
    weights = (full_q, wo, wu, wd)
    back_common = (gains, slopes, positions, planes)
    grad_top = own.reshape(R, width)
    grad_mid, grads_top, sums_top = backward(
        grad_top.astype(F32), spread_pair(grad_top), kept, prefix, weights, *back_common
    )
    returned = hop(grad_mid.astype(BF), "section", [(1, 0)])
    grad_low, grads_low, sums_low = backward(
        returned.astype(F32), spread_pair(returned), kept, prefix, weights, *back_common
    )

    def scatter(grads):
        g_qkv, g_out, g_up, g_down = grads
        down = scatter_pair(g_down)
        up = scatter_pair(g_up.reshape(planes, deep, half))
        line = jnp.concatenate(
            [g_qkv.reshape(planes, deep, 3 * wide), g_out.reshape(planes, deep, wide)], axis=2
        )
        line = scatter_line(line)
        return line, up, down

    line, up, down = scatter(jax.tree.map(lambda a, b: jnp.where(is_first, a, b), grads_low, grads_top))
    vectors, proj_sums, up_sums = jax.tree.map(lambda a, b: jnp.where(is_first, a, b), sums_low, sums_top)
    up_grad = jnp.where(odd, jnp.concatenate([up[1], up[0]], axis=1), jnp.concatenate(up, axis=1))
    down_grad = jnp.where(odd, jnp.concatenate([down[1], down[0]], axis=0), jnp.concatenate(down, axis=0))

    vec = vectors.reshape(6, planes * tensors, lane).swapaxes(0, 1).reshape(planes * tensors, cut)
    qv_sums = jnp.stack([proj_sums[:wide], proj_sums[2 * wide :]]).reshape(2, heads, planes, size_part)
    qv_sums = qv_sums.transpose(2, 0, 1, 3).reshape(planes, -1)
    zero = jnp.zeros_like(up_sums)
    up_sums = jnp.where(odd, jnp.concatenate([zero, up_sums]), jnp.concatenate([up_sums, zero]))
    up_sums = up_sums.reshape(up_bias.shape[1], planes, up_bias.shape[2]).transpose(1, 0, 2).reshape(planes, -1)
    own_part = jnp.concatenate([qv_sums, up_sums], axis=1)[:, None, :]
    own_part = jnp.where((jnp.arange(tensors) == place)[None, :, None], own_part, 0.0)
    message = jnp.concatenate([vec, own_part.reshape(planes * tensors, -1)], axis=1)
    small = lax.psum_scatter(message, ("dp", "tensor"), scatter_dimension=0, tiled=False)
    mid = cut + 2 * heads * size_part

    ends = jnp.where(is_first, grad_low, output).reshape(seqs, rows, width)
    return (
        ends[None],
        small[: 2 * lane].reshape(1, 2, lane),
        small[2 * lane : cut].reshape(1, 4, lane),
        line[:, : 3 * wide].reshape(1, deep, 3, wide),
        small[cut:mid].reshape(1, 2, heads, size_part),
        line[:, 3 * wide :].reshape(1, wide, deep),
        up_grad[None],
        small[mid:].reshape(1, up_bias.shape[1], up_bias.shape[2]),
        down_grad[None],
    )


def solution(mesh):
    in_specs = (
        P("section", "dp", "tensor", None),
        P("section", None, ("dp", "tensor")),
        P("section", None, ("dp", "tensor")),
        P("section", "dp", None, "tensor"),
        P("section", None, "tensor", "dp"),
        P("section", "tensor", "dp"),
        P("section", "dp", "tensor"),
        P("section", "tensor", "dp"),
        P("section", "tensor", "dp"),
        P("dp"),
    )
    out_specs = (
        P("section", "dp", "tensor", None),
        P("section", None, ("dp", "tensor")),
        P("section", None, ("dp", "tensor")),
        P("section", "dp", None, "tensor"),
        P("section", None, "tensor", "dp"),
        P("section", "tensor", "dp"),
        P("section", "dp", "tensor"),
        P("section", "tensor", "dp"),
        P("section", "tensor", "dp"),
    )
    return jax.shard_map(
        on_device, mesh=mesh, in_specs=in_specs, out_specs=out_specs, check_vma=False
    )
```

```python
import functools

import jax
import jax.numpy as jnp
import numpy as np
from jax import lax
from jax.experimental import pallas as pl
from jax.experimental.pallas import tpu as pltpu
from jax.sharding import PartitionSpec as P

BF = jnp.bfloat16
F32 = jnp.float32


MESH = pl.DeviceIdType.MESH
NT = (((1,), (1,)), ((), ()))
TN = (((0,), (0,)), ((), ()))


def dot(a, b, dims=(((1,), (0,)), ((), ()))):
    return lax.dot_general(a, b, dims, preferred_element_type=F32)


def remote(src, dst, send_sem, recv_sem, device):
    return pltpu.make_async_remote_copy(
        src_ref=src, dst_ref=dst, send_sem=send_sem, recv_sem=recv_sem, device_id=device, device_id_type=MESH
    )


def when(condition):
    return True if condition is True else condition


def greet(devices):
    barrier = pltpu.get_barrier_semaphore()
    for device in devices:
        pl.semaphore_signal(barrier, inc=1, device_id=device, device_id_type=MESH)
    pl.semaphore_wait(barrier, len(devices))


def tiles(count, body):
    def step(i, carry):
        body(i)
        return carry

    lax.fori_loop(0, count, step, 0)


def rows_of(i, size):
    return pl.ds(pl.multiple_of(i * size, size), size)


def norm_rows(value, gain, shift_vec):
    centre = value - jnp.mean(value, axis=-1, keepdims=True)
    spread = jnp.mean(centre * centre, axis=-1, keepdims=True)
    return centre * lax.rsqrt(spread + 1e-05) * gain + shift_vec


def spots(base, shape, dim, rows):
    index = lax.broadcasted_iota(jnp.int32, shape, dim)
    return ((index // rows) ^ base) * rows + lax.rem(index, rows)


def gelu_parts(v):
    cube = v * v * v
    inner = np.float32(np.sqrt(2 / np.pi)) * (v + 0.044715 * cube)
    return jnp.tanh(inner)


def masked_scores(raw, slope, length, place, rows, size):
    gap = spots(place, raw.shape, 0, rows) - spots(place, raw.shape, 1, rows)
    open_ = (gap >= 0) | (spots(place, raw.shape, 1, rows) < length)
    scores = raw * np.float32(size ** (-0.5)) - slope * gap.astype(F32)
    return jnp.where(open_, scores, -1e30)


def forward_kernel(
    dims, x_in, vec, qvb, upb, prefix, slopes, wq_in, wo_in, wu_in, wd_in,
    out, wq, wo, wu, wd, x_out, mid_out, nb_out, qkv_out, mix_out, sec_out, up_out, act_out,
    carry, carry_send, hid, mid, nb, qkv, mix, sec, up, act, outv,
    vq, vo, vu, vd, s1, r1, part, sy, ry, part8, sc, rc, s8, r8,
    line_s, line_r, pair_s, pair_r, own_sem, load_sem, keep_sem, carry_s, carry_r,
    ag_s, ag_r, rs_s, rs_r, ag8_s, ag8_r, f8_s, f8_r, c8_s, c8_r, rs8_s, rs8_r,
):
    n, seqs, heads, size, rows, deep, half = dims
    R = seqs * rows
    wide = heads * size
    D = n * deep
    sect, z, t = lax.axis_index("section"), lax.axis_index("dp"), lax.axis_index("tensor")
    me = (sect, z, t)
    core = (sect, z, t ^ 1)
    chip = (sect, z, t ^ 2)
    plane = (sect, z ^ 1, t)
    diag = (sect, z ^ 1, t ^ 2)
    across = (1 - sect, z, t)
    greet([(sect, z ^ k, t) for k in range(1, n)] + [core, chip, diag, across])

    zl = z & 1
    mine = [
        pltpu.make_async_copy(wq_in, wq.at[:, pl.ds(pl.multiple_of(z * deep, deep), deep)], own_sem.at[0]),
        pltpu.make_async_copy(wo_in, wo.at[z], own_sem.at[1]),
        pltpu.make_async_copy(
            wu_in.at[:, pl.ds(pl.multiple_of(zl * half, half), half)],
            wu.at[pl.ds(pl.multiple_of(z * deep, deep), deep)], own_sem.at[2]),
        pltpu.make_async_copy(
            wd_in.at[pl.ds(pl.multiple_of(zl * half, half), half)], wd.at[z], own_sem.at[3]),
    ]

    def slot(a, b):
        if a == 0:
            return wq.at[:, pl.ds(pl.multiple_of(b * deep, deep), deep)]
        return wo.at[b]

    def line(a, side, step, b):
        to = (sect, z + 1 - 2 * side, t)
        src = (wq_in, wo_in)[a] if step == 1 else slot(a, b)
        i = (a * 2 + side) * (n - 1) + step - 1
        return remote(src, slot(a, b), line_s.at[i], line_r.at[i], to)

    def line_send(a, side, step):
        b = z - (step - 1) if side == 0 else z + (step - 1)
        ok = (b >= 0) & (z < n - 1) if side == 0 else (b <= n - 1) & (z > 0)
        return ok, lambda: line(a, side, step, b)

    def line_recv(a, side, step):
        b = z - step if side == 0 else z + step
        ok = (b >= 0) if side == 0 else (b <= n - 1)
        return ok, lambda: line(a, side, step, b)

    def pair(a, k):
        h = (z ^ k) & 1
        to = (sect, z ^ k, t)
        i = a * (n - 1) + k - 1
        if a == 0:
            src = wu_in.at[:, pl.ds(pl.multiple_of(h * half, half), half)]
            dst = wu.at[pl.ds(pl.multiple_of(z * deep, deep), deep)]
        else:
            src = wd_in.at[pl.ds(pl.multiple_of(h * half, half), half)]
            dst = wd.at[z]
        return remote(src, dst, pair_s.at[i], pair_r.at[i], to)

    def pair_recv(a, k):
        i = a * (n - 1) + k - 1
        if a == 0:
            src = wu_in.at[:, pl.ds(0, half)]
            dst = wu.at[pl.ds(pl.multiple_of((z ^ k) * deep, deep), deep)]
        else:
            src = wd_in.at[pl.ds(0, half)]
            dst = wd.at[z ^ k]
        return remote(src, dst, pair_s.at[i], pair_r.at[i], (sect, z ^ k, t))

    for a in range(2):
        for side in range(2):
            ok, make = line_send(a, side, 1)

            @pl.when(ok)
            def _():
                make().start()

    for copy in mine:
        copy.start()

    tile = 32

    def first_norm():
        def body(i):
            sl = rows_of(i, tile)
            v = hid[sl, :].astype(F32)
            nb[0, sl, :] = norm_rows(v, vec[0:1, :], vec[2:3, :]).astype(BF)

        tiles(R // tile, body)

    def ag(i):
        src, to = ((0, core), (0, chip), (2, core))[i]
        dst = (1, 2, 3)[i]
        return remote(nb.at[src], nb.at[dst], ag_s.at[i], ag_r.at[i], to)

    @pl.when(sect == 0)
    def _():
        hid[...] = x_in[...]
        first_norm()
        ag(1).start()
        ag(0).start()
        ag(1).wait_recv()
        ag(2).start()

    for step in range(1, n):
        for a in range(2):
            for side in range(2):
                ok, make = line_recv(a, side, step)

                @pl.when(ok)
                def _():
                    make().wait_recv()

                if step < n - 1:
                    ok, make = line_send(a, side, step + 1)

                    @pl.when(ok)
                    def _():
                        make().start()

        if step == n - 2 or n == 2:
            for a in range(2):
                for k in range(n - 1, 0, -1):
                    pair(a, k).start()

    for copy in mine:
        copy.wait()
    load_q = pltpu.make_async_copy(wq, vq, load_sem.at[0])
    load_o = pltpu.make_async_copy(wo, vo, load_sem.at[1])
    load_q.start()
    load_o.start()

    @pl.when(sect == 1)
    def _():
        remote(carry_send, carry, carry_s, carry_r, across).wait_recv()
        hid[...] = carry[...]
        first_norm()
        ag(1).start()
        ag(0).start()
        ag(1).wait_recv()
        ag(2).start()

    ag(0).wait_recv()
    ag(2).wait_recv()
    load_q.wait()
    load_o.wait()
    keeps = []

    def keep(src, dst):
        copy = pltpu.make_async_copy(src, dst, keep_sem.at[len(keeps)])
        copy.start()
        keeps.append(copy)

    keep(hid, x_out)
    keep(nb, nb_out)

    tn = min(256, wide)
    for c in range(3):
        def body(i):
            j = lax.rem(i, wide // tn)
            b = i // (wide // tn)
            cols = rows_of(j, tn)
            lhs = jnp.concatenate([nb[2 * b], nb[2 * b + 1]], axis=0)
            got = dot(lhs, vq[c, :, cols]) + qvb[c : c + 1, cols]
            got = got.astype(BF)
            qkv[2 * b, :, pl.ds(pl.multiple_of(c * wide + j * tn, tn), tn)] = got[:R]
            qkv[2 * b + 1, :, pl.ds(pl.multiple_of(c * wide + j * tn, tn), tn)] = got[R:]

        tiles(2 * (wide // tn), body)
    keep(qkv, qkv_out)

    def head(i):
        s, h = i // heads, lax.rem(i, heads)
        pos = rows_of(s, rows)

        def part_of(c):
            cols = pl.ds(pl.multiple_of(c * wide + h * size, size), size)
            return jnp.concatenate([qkv[j, pos, cols] for j in range(4)], axis=0)

        raw = dot(part_of(0), part_of(1), NT)
        scores = masked_scores(raw, slopes[h], prefix[s], t, rows, size)
        expon = jnp.exp(scores - jnp.max(scores, axis=-1, keepdims=True))
        probs = (expon / jnp.sum(expon, axis=-1, keepdims=True)).astype(BF)
        got = dot(probs, part_of(2)).astype(BF)
        for j in range(4):
            mix[j, pos, rows_of(h, size)] = got[j * rows : (j + 1) * rows]

    tiles(seqs * heads, head)
    keep(mix, mix_out)

    def project(pair_of, put):
        lhs_blocks = pair_of

        def body(i):
            lhs = jnp.concatenate([mix[lhs_blocks[0]], mix[lhs_blocks[1]]], axis=0)
            got = dot(lhs, vo[i])
            put(rows_of(i, deep), got)

        tiles(n, body)

    def put_send(cols, got):
        s1[0, :, cols] = got[:R].astype(BF)
        s1[1, :, cols] = got[R:].astype(BF)

    def put_part(cols, got):
        part[0, :, cols] = got[:R]
        part[1, :, cols] = got[R:]

    to_core = remote(s1, r1, rs_s.at[0], rs_r.at[0], core)
    to_chip = remote(sy, ry, rs_s.at[1], rs_r.at[1], chip)
    project((3, 1), put_send)
    to_core.start()
    project((2, 0), put_part)
    to_core.wait_recv()

    def add_chip(i):
        sl = rows_of(i, tile)
        sy[sl, :] = (part[0, sl, :] + r1[0, sl, :].astype(F32)).astype(BF)

    tiles(R // tile, add_chip)
    to_chip.start()
    to_chip.wait_recv()

    def middle_body(i):
        sl = rows_of(i, tile)
        v = hid[sl, :].astype(F32) + part[1, sl, :] + r1[1, sl, :].astype(F32)
        v = v + ry[sl, :].astype(F32) + vec[4:5, :]
        mid[sl, :] = v
        sec[0, sl, :] = norm_rows(v, vec[1:2, :], vec[3:4, :]).astype(BF)

    tiles(R // tile, middle_body)
    keep(mid, mid_out)

    targets = (None, chip, plane, diag)

    def ag8(i):
        return remote(sec.at[0], sec.at[i], ag8_s.at[i], ag8_r.at[i], targets[i])

    def forward8(i):
        return remote(sec.at[i], sec.at[4 + i], f8_s.at[i], f8_r.at[i], core)

    def core8(i):
        return remote(sc.at[i], rc.at[i], c8_s.at[i], c8_r.at[i], core)

    def rs8(i):
        return remote(s8.at[i], r8.at[i], rs8_s.at[i], rs8_r.at[i], targets[i])

    order = (0, 2, 1, 3)
    for i in order[1:]:
        ag8(i).start()
    forward8(0).start()

    for a in range(2):
        for k in range(n - 1, 0, -1):
            pair_recv(a, k).wait_recv()
    load_u = pltpu.make_async_copy(wu, vu, load_sem.at[2])
    load_d = pltpu.make_async_copy(wd, vd, load_sem.at[3])
    load_u.start()
    load_d.start()
    load_u.wait()
    load_d.wait()

    tu = min(256, half)

    def group(i):
        if i:
            ag8(i).wait_recv()
            forward8(i).start()
        forward8(i).wait_recv()

        def up_body(j):
            cols = rows_of(j, tu)
            lhs = jnp.concatenate([sec[i], sec[4 + i]], axis=0)
            v = dot(lhs, vu[:, cols]) + upb[:, cols]
            g = (0.5 * v * (1.0 + gelu_parts(v))).astype(BF)
            up[i, :, cols] = v[:R]
            up[4 + i, :, cols] = v[R:]
            act[i, :, cols] = g[:R]
            act[4 + i, :, cols] = g[R:]

        tiles(half // tu, up_body)

        def down_body(j):
            cols = rows_of(j, deep)
            lhs = jnp.concatenate([act[i], act[4 + i]], axis=0)
            got = dot(lhs, vd[j])
            part8[i, :, cols] = got[:R]
            sc[i, :, cols] = got[R:].astype(BF)

        tiles(n, down_body)
        core8(i).start()

    def reduce(i):
        core8(i).wait_recv()
        if i == 0:
            return

        def body(j):
            sl = rows_of(j, tile)
            s8[i, sl, :] = (part8[i, sl, :] + rc[i, sl, :].astype(F32)).astype(BF)

        tiles(R // tile, body)
        rs8(i).start()

    for number, i in enumerate(order):
        group(i)
        if number:
            reduce(order[number - 1])
    reduce(order[-1])
    keep(sec, sec_out)
    keep(up, up_out)
    keep(act, act_out)
    for i in order[1:]:
        rs8(i).wait_recv()

    def out_body(j):
        sl = rows_of(j, tile)
        v = mid[sl, :] + part8[0, sl, :] + rc[0, sl, :].astype(F32)
        for i in (1, 2, 3):
            v = v + r8[i, sl, :].astype(F32)
        v = v + vec[5:6, :]
        outv[sl, :] = v
        carry_send[sl, :] = v.astype(BF)

    tiles(R // tile, out_body)
    over = remote(carry_send, carry, carry_s, carry_r, across)

    @pl.when(sect == 0)
    def _():
        over.start()

    keep(outv, out)

    for step in range(1, n):
        for a in range(2):
            for side in range(2):
                ok, make = line_send(a, side, step)

                @pl.when(ok)
                def _():
                    make().wait_send()

    for a in range(2):
        for k in range(n - 1, 0, -1):
            pair(a, k).wait_send()
    for i in range(3):
        ag(i).wait_send()
    to_core.wait_send()
    to_chip.wait_send()
    for i in range(4):
        if i:
            ag8(i).wait_send()
            rs8(i).wait_send()
        forward8(i).wait_send()
        core8(i).wait_send()

    @pl.when(sect == 0)
    def _():
        over.wait_send()

    for copy in keeps:
        copy.wait()


def run_forward(dims, x, vec, qvb, upb, prefix, slopes, wq, wo, wu, wd):
    n, seqs, heads, size, rows, deep, half = dims
    R, wide, D = seqs * rows, heads * size, n * deep
    V = lambda shape, dtype: pltpu.VMEM(shape, dtype)
    S = lambda *shape: jax.ShapeDtypeStruct(shape[:-1], shape[-1])
    any_ = pl.BlockSpec(memory_space=pl.ANY)
    vm = pl.BlockSpec(memory_space=pltpu.VMEM)
    sm = pl.BlockSpec(memory_space=pltpu.SMEM)
    dma = lambda k: pltpu.SemaphoreType.DMA((k,))
    outs = (
        S(R, D, F32), S(3, D, wide, BF), S(n, wide, deep, BF), S(D, half, BF), S(n, half, deep, BF),
        S(R, D, BF), S(R, D, F32), S(4, R, D, BF), S(4, R, 3 * wide, BF), S(4, R, wide, BF),
        S(8, R, D, BF), S(8, R, half, F32), S(8, R, half, BF),
    )
    scratch = [
        V((R, D), BF), V((R, D), BF), V((R, D), BF), V((R, D), F32), V((4, R, D), BF), V((4, R, 3 * wide), BF),
        V((4, R, wide), BF), V((8, R, D), BF), V((8, R, half), F32), V((8, R, half), BF), V((R, D), F32),
        V((3, D, wide), BF), V((n, wide, deep), BF), V((D, half), BF), V((n, half, deep), BF),
        V((2, R, D), BF), V((2, R, D), BF), V((2, R, D), F32), V((R, D), BF), V((R, D), BF),
        V((4, R, D), F32), V((4, R, D), BF), V((4, R, D), BF), V((4, R, D), BF), V((4, R, D), BF),
        dma(4 * (n - 1)), dma(4 * (n - 1)), dma(2 * (n - 1)), dma(2 * (n - 1)), dma(4), dma(4), dma(9),
        pltpu.SemaphoreType.DMA(()), pltpu.SemaphoreType.DMA(()),
        dma(3), dma(3), dma(2), dma(2), dma(4), dma(4), dma(4), dma(4), dma(4), dma(4), dma(4), dma(4),
    ]
    return pl.pallas_call(
        functools.partial(forward_kernel, dims),
        out_shape=outs,
        in_specs=[vm, vm, vm, vm, sm, sm, any_, any_, any_, any_],
        out_specs=(any_,) * len(outs),
        scratch_shapes=scratch,
        compiler_params=pltpu.CompilerParams(
            collective_id=0, has_side_effects=True, vmem_limit_bytes=60 * 1024 * 1024
        ),
    )(x, vec, qvb, upb, prefix, slopes, wq, wo, wu, wd)


def backward_kernel(
    dims, top, vec, prefix, slopes, wq, wo, wu, wd, hid_in, mid_in, nb_in, qkv_in, mix_in, sec_in, up_in, act_in,
    dh_out, gq_out, go_out, gu_out, gd_out, sums_out, proj_out, ups_out, ru, rd, rq, ro,
    carry, grad, mid, hid, dmid, gp, gm, gu, gd, gq, go, part, own8, sc, rc, s8, r8,
    s1, r1, sy, ry, sums, proj, ups, tmpq, tmpo,
    load_sem, up_sem, out_sem, carry_s, carry_r, ag8_s, ag8_r, f8_s, f8_r, c8_s, c8_r, rs8_s, rs8_r,
    ag_s, ag_r, rs_s, rs_r, ffn_s, ffn_r, att_s, att_r,
):
    n, seqs, heads, size, rows, deep, half = dims
    R = seqs * rows
    wide = heads * size
    D = n * deep
    sect, z, t = lax.axis_index("section"), lax.axis_index("dp"), lax.axis_index("tensor")
    core = (sect, z, t ^ 1)
    chip = (sect, z, t ^ 2)
    plane = (sect, z ^ 1, t)
    diag = (sect, z ^ 1, t ^ 2)
    across = (1 - sect, z, t)
    greet([(sect, z ^ k, t) for k in range(1, n)] + [core, chip, diag, across])
    zl = z & 1
    tile = 32
    order = (0, 2, 1, 3)
    targets = (None, chip, plane, diag)

    def ag8(i):
        return remote(gp.at[0], gp.at[i], ag8_s.at[i], ag8_r.at[i], targets[i])

    def forward8(i):
        return remote(gp.at[i], gp.at[4 + i], f8_s.at[i], f8_r.at[i], core)

    def core8(i):
        return remote(sc.at[i], rc.at[i], c8_s.at[i], c8_r.at[i], core)

    def rs8(i):
        return remote(s8.at[i - 1], r8.at[i - 1], rs8_s.at[i], rs8_r.at[i], targets[i])

    def load(src, dst, i):
        copy = pltpu.make_async_copy(src, dst, load_sem.at[i])
        copy.start()
        return copy

    load_mid, load_hid = load(mid_in, mid, 0), load(hid_in, hid, 1)
    sums[...] = jnp.zeros_like(sums)
    proj[...] = jnp.zeros_like(proj)
    ups[...] = jnp.zeros_like(ups)
    over = remote(s1.at[0], carry, carry_s, carry_r, across)

    def col_sum(row, value):
        sums[row : row + 1, :] += jnp.sum(value, axis=0, keepdims=True)

    def ffn(a, k):
        i = a * (n - 1) + k - 1
        return remote((gu, gd)[a].at[k], (ru, rd)[a].at[k - 1], ffn_s.at[i], ffn_r.at[i], (sect, z ^ k, t))

    def feed(vu, vd, sec, act, dup, upb):
        loads = [load(wu, vu, 2), load(wd, vd, 3), load(sec_in, sec, 4), load(act_in, act, 5)]

        def up_load(number):
            i, slot = order[number], number % 2
            return [
                pltpu.make_async_copy(up_in.at[i + 4 * b], upb.at[slot, b], up_sem.at[2 * slot + b])
                for b in range(2)
            ]

        for number in range(2):
            for copy in up_load(number):
                copy.start()

        @pl.when(sect == 1)
        def _():
            grad[...] = top[...]

        @pl.when(sect == 0)
        def _():
            over.wait_recv()
            grad[...] = carry[...]

        gp[0] = grad[...]
        for i in order[1:]:
            ag8(i).start()
        forward8(0).start()

        def bias_body(j):
            col_sum(5, grad[rows_of(j, tile), :].astype(F32))

        tiles(R // tile, bias_body)
        for copy in loads:
            copy.wait()
        tu = min(256, half)
        td = min(256, D)

        def group(number):
            i, slot = order[number], number % 2
            if i:
                ag8(i).wait_recv()
                forward8(i).start()
            forward8(i).wait_recv()
            for copy in up_load(number):
                copy.wait()

            def up_body(j):
                cols = rows_of(j, tu)
                got = None
                for b in range(n):
                    at = pl.ds(b * deep, deep)
                    lhs = jnp.concatenate([gp[i, :, at], gp[4 + i, :, at]], axis=0)
                    term = dot(lhs, vd[b, cols, :], NT)
                    got = term if got is None else got + term
                v = jnp.concatenate([upb[slot, 0, :, cols], upb[slot, 1, :, cols]], axis=0)
                th = gelu_parts(v)
                slope = 0.5 * (1.0 + th) + 0.5 * v * (1.0 - th * th) * np.float32(np.sqrt(2 / np.pi)) * (
                    1.0 + np.float32(3 * 0.044715) * v * v
                )
                low = (got * slope).astype(BF)
                dup[i, :, cols] = low[:R]
                dup[4 + i, :, cols] = low[R:]
                ups[0:1, cols] += jnp.sum(low.astype(F32), axis=0, keepdims=True)

            tiles(half // tu, up_body)
            if number + 2 < 4:
                for copy in up_load(number + 2):
                    copy.start()

            def second_body(j):
                cols = rows_of(j, td)
                lhs = jnp.concatenate([dup[i], dup[4 + i]], axis=0)
                got = dot(lhs, vu[cols, :], NT)
                if i == 0:
                    own8[:, cols] = got[:R]
                else:
                    part[slot, :, cols] = got[:R]
                sc[i, :, cols] = got[R:].astype(BF)

            tiles(D // td, second_body)
            core8(i).start()

        def reduce(number):
            i, slot = order[number], number % 2
            core8(i).wait_recv()
            if i == 0:
                return

            def body(j):
                sl = rows_of(j, tile)
                s8[i - 1, sl, :] = (part[slot, sl, :] + rc[i, sl, :].astype(F32)).astype(BF)

            tiles(R // tile, body)
            rs8(i).start()

        for number in range(4):
            group(number)
            if number:
                reduce(number - 1)
        reduce(3)

        th_ = min(256, half)
        for k in list(range(n - 1, 0, -1)) + [0]:
            def down_body(j):
                cols = rows_of(j, th_)
                lhs = act[:, :, cols].reshape(8 * R, th_)
                at = pl.ds(pl.multiple_of((z ^ k) * deep, deep), deep)
                gd[k, cols, :] = dot(lhs, gp[:, :, at].reshape(8 * R, deep), TN).astype(BF)

            tiles(half // th_, down_body)
            dd = min(256, deep)

            def up_body(j):
                at = pl.ds(pl.multiple_of((z ^ k) * deep + j * dd, dd), dd)
                lhs = sec[:, :, at].reshape(8 * R, dd)
                gu[k, rows_of(j, dd), :] = dot(lhs, dup[...].reshape(8 * R, half), TN).astype(BF)

            tiles(deep // dd, up_body)

    pl.run_scoped(
        feed,
        pltpu.VMEM((D, half), BF), pltpu.VMEM((n, half, deep), BF), pltpu.VMEM((8, R, D), BF),
        pltpu.VMEM((8, R, half), BF), pltpu.VMEM((8, R, half), BF), pltpu.VMEM((2, 2, R, half), F32),
    )
    for i in order[1:]:
        rs8(i).wait_recv()
    for a in range(2):
        for k in range(n - 1, 0, -1):
            ffn(a, k).start()
    load_mid.wait()
    load_hid.wait()

    def norm_back(value, gain, dy):
        centre = value - jnp.mean(value, axis=-1, keepdims=True)
        spread = jnp.mean(centre * centre, axis=-1, keepdims=True)
        scale = lax.rsqrt(spread + 1e-05)
        unit = centre * scale
        scaled = dy * gain
        inner = jnp.mean(scaled * unit, axis=-1, keepdims=True)
        return (scaled - jnp.mean(scaled, axis=-1, keepdims=True) - unit * inner) * scale, unit

    def mid_body(j):
        sl = rows_of(j, tile)
        dy = own8[sl, :] + rc[0, sl, :].astype(F32)
        for i in (1, 2, 3):
            dy = dy + r8[i - 1, sl, :].astype(F32)
        back, unit = norm_back(mid[sl, :], vec[1:2, :], dy)
        total = grad[sl, :].astype(F32) + back
        dmid[sl, :] = total
        gm[0, sl, :] = total.astype(BF)
        col_sum(1, dy * unit)
        col_sum(3, dy)
        col_sum(4, total)

    tiles(R // tile, mid_body)

    def ag(i):
        src, to = ((0, core), (0, chip), (2, core))[i]
        dst = (1, 2, 3)[i]
        return remote(gm.at[src], gm.at[dst], ag_s.at[i], ag_r.at[i], to)

    ag(1).start()
    ag(0).start()
    to_core = remote(s1, r1, rs_s.at[0], rs_r.at[0], core)
    to_chip = remote(sy, ry, rs_s.at[1], rs_r.at[1], chip)

    def low_bit(k):
        return k & -k

    def att(k, c):
        i = (k - 1) * 4 + c
        src, dst = (gq.at[k, c], rq.at[k - 1, c]) if c < 3 else (go.at[k], ro.at[k - 1])
        return remote(src, dst, att_s.at[i], att_r.at[i], (sect, z ^ low_bit(k), t))

    send_order = sorted(range(1, n), key=lambda k: (low_bit(k), -k))

    def attention(vq, vo, nb, qkv, mix, dmix, dqkv):
        loads = [load(wo, vo, 2), load(qkv_in, qkv, 3), load(mix_in, mix, 4), load(nb_in, nb, 5), load(wq, vq, 6)]
        ag(1).wait_recv()
        ag(2).start()
        for copy in loads:
            copy.wait()
        ag(0).wait_recv()

        def mixed(b):
            if b == 1:
                ag(2).wait_recv()
            tw = min(256, wide)

            def body(j):
                cols = rows_of(j, tw)
                got = None
                for p in range(n):
                    at = pl.ds(p * deep, deep)
                    lhs = jnp.concatenate([gm[2 * b, :, at], gm[2 * b + 1, :, at]], axis=0)
                    term = dot(lhs, vo[p, cols, :], NT)
                    got = term if got is None else got + term
                low = got.astype(BF)
                dmix[2 * b, :, cols] = low[:R]
                dmix[2 * b + 1, :, cols] = low[R:]

            tiles(wide // tw, body)

        mixed(0)
        mixed(1)

        def head(i):
            s, h = i // heads, lax.rem(i, heads)
            pos = rows_of(s, rows)

            def part_of(ref, c):
                cols = pl.ds(pl.multiple_of(c * wide + h * size, size), size)
                return jnp.concatenate([ref[j, pos, cols] for j in range(4)], axis=0)

            q, k, v, dm = part_of(qkv, 0), part_of(qkv, 1), part_of(qkv, 2), part_of(dmix, 0)
            scores = masked_scores(dot(q, k, NT), slopes[h], prefix[s], t, rows, size)
            expon = jnp.exp(scores - jnp.max(scores, axis=-1, keepdims=True))
            probs = expon / jnp.sum(expon, axis=-1, keepdims=True)
            dp = dot(dm, v, NT)
            inner = jnp.sum(probs * dp, axis=-1, keepdims=True)
            raw = (probs * (dp - inner) * np.float32(size ** (-0.5))).astype(BF)
            for c, got in enumerate((dot(raw, k), dot(raw, q, TN), dot(probs.astype(BF), dm, TN))):
                low = got.astype(BF)
                cols = pl.ds(pl.multiple_of(c * wide + h * size, size), size)
                proj[0:1, cols] += jnp.sum(low.astype(F32), axis=0, keepdims=True)
                for j in range(4):
                    dqkv[j, pos, cols] = low[j * rows : (j + 1) * rows]

        tiles(seqs * heads, head)

        def normed(blocks, put):
            td = min(256, D)

            def body(j):
                cols = rows_of(j, td)
                got = None
                for c in range(3):
                    lhs = jnp.concatenate([dqkv[b, :, c * wide : (c + 1) * wide] for b in blocks], axis=0)
                    term = dot(lhs, vq[c, cols, :], NT)
                    got = term if got is None else got + term
                put(cols, got)

            tiles(D // td, body)

        def put_send(cols, got):
            s1[0, :, cols] = got[:R].astype(BF)
            s1[1, :, cols] = got[R:].astype(BF)

        def put_part(cols, got):
            part[0, :, cols] = got[:R]
            part[1, :, cols] = got[R:]

        normed((3, 1), put_send)
        to_core.start()
        normed((2, 0), put_part)
        to_core.wait_recv()

        def add_chip(i):
            sl = rows_of(i, tile)
            sy[sl, :] = (part[0, sl, :] + r1[0, sl, :].astype(F32)).astype(BF)

        tiles(R // tile, add_chip)
        to_chip.start()
        for k in send_order + [0]:
            tw = min(256, wide)
            at = pl.ds(pl.multiple_of((z ^ k) * deep, deep), deep)

            def out_body(j):
                cols = rows_of(j, tw)
                lhs = mix[:, :, cols].reshape(4 * R, tw)
                go[k, cols, :] = dot(lhs, gm[:, :, at].reshape(4 * R, deep), TN).astype(BF)

            tiles(wide // tw, out_body)
            for c in range(3):
                def body(j):
                    cols = rows_of(j, tw)
                    rhs = dqkv[:, :, pl.ds(pl.multiple_of(c * wide + j * tw, tw), tw)].reshape(4 * R, tw)
                    gq[k, c, :, cols] = dot(nb[:, :, at].reshape(4 * R, deep), rhs, TN).astype(BF)

                tiles(wide // tw, body)
            if k and low_bit(k) == 1:
                for c in range(4):
                    att(k, c).start()

    pl.run_scoped(
        attention,
        pltpu.VMEM((3, D, wide), BF), pltpu.VMEM((n, wide, deep), BF), pltpu.VMEM((4, R, D), BF),
        pltpu.VMEM((4, R, 3 * wide), BF), pltpu.VMEM((4, R, wide), BF), pltpu.VMEM((4, R, wide), BF),
        pltpu.VMEM((4, R, 3 * wide), BF),
    )
    to_chip.wait_recv()
    to_core.wait_send()

    def low_body(j):
        sl = rows_of(j, tile)
        dy = part[1, sl, :] + r1[1, sl, :].astype(F32) + ry[sl, :].astype(F32)
        back, unit = norm_back(hid[sl, :].astype(F32), vec[0:1, :], dy)
        total = dmid[sl, :] + back
        dmid[sl, :] = total
        s1[0, sl, :] = total.astype(BF)
        col_sum(0, dy * unit)
        col_sum(2, dy)

    tiles(R // tile, low_body)

    @pl.when(sect == 1)
    def _():
        over.start()

    outs = []

    def put(src, dst):
        copy = pltpu.make_async_copy(src, dst, out_sem.at[len(outs)])
        copy.start()
        outs.append(copy)

    put(dmid, dh_out)
    put(sums, sums_out)
    put(proj, proj_out)
    put(ups, ups_out)

    for k in send_order:
        if low_bit(k) == 1:
            continue
        for child in send_order:
            if child ^ low_bit(child) != k:
                continue
            for c in range(4):
                att(child, c).wait_recv()
                src = rq.at[child - 1, c] if c < 3 else ro.at[child - 1]
                dst = tmpq if c < 3 else tmpo
                copy = pltpu.make_async_copy(src, dst, load_sem.at[7])
                copy.start()
                copy.wait()
                if c < 3:
                    gq[k, c] = (gq[k, c].astype(F32) + tmpq[...].astype(F32)).astype(BF)
                else:
                    go[k] = (go[k].astype(F32) + tmpo[...].astype(F32)).astype(BF)
                if child == [j for j in send_order if j ^ low_bit(j) == k][-1]:
                    att(k, c).start()

    def final_feed(bu, bd, fu, fd):
        for a in range(2):
            for k in range(n - 1, 0, -1):
                ffn(a, k).wait_recv()
        loads = [load(ru, bu, 2), load(rd, bd, 3)]
        for copy in loads:
            copy.wait()
        step = min(64, deep)

        def up_body(j):
            sl = rows_of(j, step)
            same = gu[0, sl, :].astype(F32)
            other = bu[0, sl, :].astype(F32)
            for k in range(2, n):
                if k % 2 == 0:
                    same = same + bu[k - 1, sl, :].astype(F32)
                else:
                    other = other + bu[k - 1, sl, :].astype(F32)
            fu[0, sl, :] = same
            fu[1, sl, :] = other

        tiles(deep // step, up_body)

        def down_body(j):
            sl = rows_of(j, step)
            same = gd[0, sl, :].astype(F32)
            other = bd[0, sl, :].astype(F32)
            for k in range(2, n):
                if k % 2 == 0:
                    same = same + bd[k - 1, sl, :].astype(F32)
                else:
                    other = other + bd[k - 1, sl, :].astype(F32)
            fd[0, sl, :] = same
            fd[1, sl, :] = other

        tiles(half // step, down_body)
        copies = []
        for b in range(2):
            at = pl.ds(pl.multiple_of((zl ^ b) * half, half), half)
            copies.append(pltpu.make_async_copy(fu.at[b], gu_out.at[:, at], load_sem.at[2 + 2 * b]))
            copies.append(pltpu.make_async_copy(fd.at[b], gd_out.at[at, :], load_sem.at[3 + 2 * b]))
        for copy in copies:
            copy.start()
        for copy in copies:
            copy.wait()

    pl.run_scoped(
        final_feed,
        pltpu.VMEM((n - 1, deep, half), BF), pltpu.VMEM((n - 1, half, deep), BF),
        pltpu.VMEM((2, deep, half), F32), pltpu.VMEM((2, half, deep), F32),
    )

    def final_attention(bq, bo, fq, fo):
        last = [k for k in send_order if k == low_bit(k)]
        for k in last:
            for c in range(4):
                att(k, c).wait_recv()
        loads = [load(rq, bq, 2), load(ro, bo, 3)]
        for copy in loads:
            copy.wait()
        step = min(64, deep)

        def q_body(j):
            sl = rows_of(j, step)
            for c in range(3):
                total = gq[0, c, sl, :].astype(F32)
                for k in last:
                    total = total + bq[k - 1, c, sl, :].astype(F32)
                fq[c, sl, :] = total

        tiles(deep // step, q_body)

        def o_body(j):
            sl = rows_of(j, step)
            total = go[0, sl, :].astype(F32)
            for k in last:
                total = total + bo[k - 1, sl, :].astype(F32)
            fo[sl, :] = total

        tiles(wide // step, o_body)
        copies = [
            pltpu.make_async_copy(fq, gq_out, load_sem.at[2]),
            pltpu.make_async_copy(fo, go_out, load_sem.at[3]),
        ]
        for copy in copies:
            copy.start()
        for copy in copies:
            copy.wait()

    pl.run_scoped(
        final_attention,
        pltpu.VMEM((n - 1, 3, deep, wide), BF), pltpu.VMEM((n - 1, wide, deep), BF),
        pltpu.VMEM((3, deep, wide), F32), pltpu.VMEM((wide, deep), F32),
    )

    for i in range(4):
        if i:
            ag8(i).wait_send()
            rs8(i).wait_send()
        forward8(i).wait_send()
        core8(i).wait_send()
    for i in range(3):
        ag(i).wait_send()
    to_chip.wait_send()
    for a in range(2):
        for k in range(1, n):
            ffn(a, k).wait_send()
    for k in range(1, n):
        for c in range(4):
            att(k, c).wait_send()

    @pl.when(sect == 1)
    def _():
        over.wait_send()

    for copy in outs:
        copy.wait()


def run_backward(dims, top, vec, prefix, slopes, weights, kept):
    n, seqs, heads, size, rows, deep, half = dims
    R, wide, D = seqs * rows, heads * size, n * deep
    V = lambda shape, dtype: pltpu.VMEM(shape, dtype)
    S = lambda *shape: jax.ShapeDtypeStruct(shape[:-1], shape[-1])
    any_ = pl.BlockSpec(memory_space=pl.ANY)
    vm = pl.BlockSpec(memory_space=pltpu.VMEM)
    sm = pl.BlockSpec(memory_space=pltpu.SMEM)
    dma = lambda k: pltpu.SemaphoreType.DMA((k,))
    one = pltpu.SemaphoreType.DMA(())
    outs = (
        S(R, D, F32), S(3, deep, wide, F32), S(wide, deep, F32), S(deep, 2 * half, F32), S(2 * half, deep, F32),
        S(8, D, F32), S(1, 3 * wide, F32), S(1, half, F32),
        S(n - 1, deep, half, BF), S(n - 1, half, deep, BF), S(n - 1, 3, deep, wide, BF), S(n - 1, wide, deep, BF),
    )
    scratch = [
        V((R, D), BF), V((R, D), BF), V((R, D), F32), V((R, D), BF), V((R, D), F32),
        V((8, R, D), BF), V((4, R, D), BF),
        V((n, deep, half), BF), V((n, half, deep), BF), V((n, 3, deep, wide), BF), V((n, wide, deep), BF),
        V((2, R, D), F32), V((R, D), F32), V((4, R, D), BF), V((4, R, D), BF), V((3, R, D), BF), V((3, R, D), BF),
        V((2, R, D), BF), V((2, R, D), BF), V((R, D), BF), V((R, D), BF),
        V((8, D), F32), V((1, 3 * wide), F32), V((1, half), F32), V((deep, wide), BF), V((wide, deep), BF),
        dma(8), dma(4), dma(4), one, one,
        dma(4), dma(4), dma(4), dma(4), dma(4), dma(4), dma(4), dma(4),
        dma(3), dma(3), dma(2), dma(2), dma(2 * (n - 1)), dma(2 * (n - 1)), dma(4 * (n - 1)), dma(4 * (n - 1)),
    ]
    return pl.pallas_call(
        functools.partial(backward_kernel, dims),
        out_shape=outs,
        in_specs=[vm, vm, sm, sm] + [any_] * 12,
        out_specs=(any_,) * len(outs),
        scratch_shapes=scratch,
        compiler_params=pltpu.CompilerParams(
            collective_id=1, has_side_effects=True, vmem_limit_bytes=62 * 1024 * 1024
        ),
    )(top, vec, prefix, slopes, *weights, *kept)


def small_kernel(spread, peers, src, out, got, send_sem, recv_sem):
    sect, z, t = lax.axis_index("section"), lax.axis_index("dp"), lax.axis_index("tensor")
    n, m = peers
    count = n * m
    me = z * m + t

    def peer(k):
        other = me ^ k
        return other, (sect, other // m, lax.rem(other, m))

    greet([peer(k)[1] for k in range(1, count)])
    copies = []
    for k in range(1, count):
        other, device = peer(k)
        block = src if spread else src.at[other]
        copies.append(remote(block, got.at[k], send_sem.at[k], recv_sem.at[k], device))
        copies[-1].start()
    if spread:
        out[me] = src[...]
    else:
        total = src[me]
    for k in range(1, count):
        copies[k - 1].wait_recv()
        if spread:
            out[me ^ k] = got[k]
        else:
            total = total + got[k]
    if not spread:
        out[...] = total
    for copy in copies:
        copy.wait_send()


def small_exchange(value, spread, peers, collective_id):
    count = peers[0] * peers[1]
    block = value.shape if spread else value.shape[1:]
    return pl.pallas_call(
        functools.partial(small_kernel, spread, peers),
        out_shape=jax.ShapeDtypeStruct((count,) + block if spread else block, F32),
        in_specs=[pl.BlockSpec(memory_space=pltpu.VMEM)],
        out_specs=pl.BlockSpec(memory_space=pltpu.VMEM),
        scratch_shapes=[
            pltpu.VMEM((count,) + block, F32),
            pltpu.SemaphoreType.DMA((count,)),
            pltpu.SemaphoreType.DMA((count,)),
        ],
        compiler_params=pltpu.CompilerParams(collective_id=collective_id, has_side_effects=True),
    )(value)


def on_device(activations, ln_gains, biases, w_qkv, qv_bias, w_out, w_up, up_bias, w_down, prefix):
    is_first = lax.axis_index("section") == 0
    plane = lax.axis_index("dp")
    place = lax.axis_index("tensor")
    planes = lax.axis_size("dp")
    tensors = lax.axis_size("tensor")
    odd = plane % 2 == 1
    seqs, rows, width = activations.shape[1:]
    heads, size_part = qv_bias.shape[2:]
    size = size_part * planes
    wide = heads * size
    deep = w_qkv.shape[1]
    units = w_up.shape[2]
    half = units // 2
    own = activations[0]

    flat = jnp.concatenate([v.reshape(-1) for v in (ln_gains, biases, qv_bias, up_bias)])
    peers = (planes, tensors)
    everyone = small_exchange(flat.astype(F32).reshape(-1, 128), True, peers, 2).reshape(planes * tensors, -1)
    lane = width // (planes * tensors)
    cut = 6 * lane
    features = everyone[:, :cut].reshape(-1, 6, lane).swapaxes(0, 1).reshape(6, width)
    mine = everyone.reshape(planes, tensors, -1)
    mine = lax.dynamic_index_in_dim(mine, place, 1, keepdims=False)[:, cut:]
    qv_full = mine[:, : 2 * heads * size_part].reshape(planes, 2, heads, size_part)
    qv_full = qv_full.transpose(1, 2, 0, 3).reshape(2, heads, size)
    up_full = mine[:, 2 * heads * size_part :].reshape(planes, up_bias.shape[1], up_bias.shape[2])
    up_full = up_full.transpose(1, 0, 2).reshape(units)
    up_own = jnp.where(odd, up_full[half:], up_full[:half])

    head_ids = place * heads + jnp.arange(heads)
    slopes = jnp.exp2(-8.0 * (head_ids.astype(F32) + 1.0) / (heads * tensors))

    dims = (planes, seqs, heads, size, rows, deep, half)
    vec = jnp.concatenate([features, jnp.zeros((2, width), F32)], axis=0)
    flat_qv = qv_full.reshape(2, wide)
    qvb = jnp.stack([flat_qv[0], jnp.zeros_like(flat_qv[0]), flat_qv[1]])
    got = run_forward(
        dims, own.reshape(seqs * rows, width), vec, qvb, up_own[None], prefix, slopes,
        w_qkv[0].transpose(1, 0, 2), w_out[0], w_up[0], w_down[0],
    )
    output, weights, kept = got[0], got[1:5], got[5:]
    back = run_backward(dims, own.reshape(seqs * rows, width), vec, prefix, slopes, weights, kept)
    grad_low, grad_q, grad_o, grad_u, grad_d, vectors, proj_sums, up_sums = back[:8]
    proj_sums, up_sums = proj_sums[0], up_sums[0]

    vec = vectors[:6].reshape(6, planes * tensors, lane).swapaxes(0, 1).reshape(planes * tensors, cut)
    qv_sums = jnp.stack([proj_sums[:wide], proj_sums[2 * wide :]]).reshape(2, heads, planes, size_part)
    qv_sums = qv_sums.transpose(2, 0, 1, 3).reshape(planes, -1)
    zero = jnp.zeros_like(up_sums)
    up_sums = jnp.where(odd, jnp.concatenate([zero, up_sums]), jnp.concatenate([up_sums, zero]))
    up_sums = up_sums.reshape(up_bias.shape[1], planes, up_bias.shape[2]).transpose(1, 0, 2).reshape(planes, -1)
    own_part = jnp.concatenate([qv_sums, up_sums], axis=1)[:, None, :]
    own_part = jnp.where((jnp.arange(tensors) == place)[None, :, None], own_part, 0.0)
    message = jnp.concatenate([vec, own_part.reshape(planes * tensors, -1)], axis=1)
    message = message.reshape(planes * tensors, -1, 128)
    small = small_exchange(message, False, peers, 3).reshape(-1)
    mid = cut + 2 * heads * size_part

    ends = jnp.where(is_first, grad_low, output).reshape(seqs, rows, width)
    return (
        ends[None],
        small[: 2 * lane].reshape(1, 2, lane),
        small[2 * lane : cut].reshape(1, 4, lane),
        grad_q.transpose(1, 0, 2)[None],
        small[cut:mid].reshape(1, 2, heads, size_part),
        grad_o[None],
        grad_u[None],
        small[mid:].reshape(1, up_bias.shape[1], up_bias.shape[2]),
        grad_d[None],
    )


def solution(mesh):
    in_specs = (
        P("section", "dp", "tensor", None),
        P("section", None, ("dp", "tensor")),
        P("section", None, ("dp", "tensor")),
        P("section", "dp", None, "tensor"),
        P("section", None, "tensor", "dp"),
        P("section", "tensor", "dp"),
        P("section", "dp", "tensor"),
        P("section", "tensor", "dp"),
        P("section", "tensor", "dp"),
        P("dp"),
    )
    out_specs = (
        P("section", "dp", "tensor", None),
        P("section", None, ("dp", "tensor")),
        P("section", None, ("dp", "tensor")),
        P("section", "dp", None, "tensor"),
        P("section", None, "tensor", "dp"),
        P("section", "tensor", "dp"),
        P("section", "dp", "tensor"),
        P("section", "tensor", "dp"),
        P("section", "tensor", "dp"),
    )
    return jax.shard_map(
        on_device, mesh=mesh, in_specs=in_specs, out_specs=out_specs, check_vma=False
    )
```

```python
import functools

import jax
import jax.numpy as jnp
import numpy as np
from jax import lax
from jax.experimental import pallas as pl
from jax.experimental.pallas import tpu as pltpu
from jax.sharding import PartitionSpec as P

BF = jnp.bfloat16
F32 = jnp.float32


MESH = pl.DeviceIdType.MESH
RELAYED = ((3,), ())
GRADS_RELAYED = ((), (3, 2))
ATT_RELAYED = (0, 1, 2)
NT = (((1,), (1,)), ((), ()))
TN = (((0,), (0,)), ((), ()))


def dot(a, b, dims=(((1,), (0,)), ((), ()))):
    return lax.dot_general(a, b, dims, preferred_element_type=F32)


def remote(src, dst, send_sem, recv_sem, device):
    return pltpu.make_async_remote_copy(
        src_ref=src, dst_ref=dst, send_sem=send_sem, recv_sem=recv_sem, device_id=device, device_id_type=MESH
    )


def when(condition):
    return True if condition is True else condition


def greet(devices):
    barrier = pltpu.get_barrier_semaphore()
    for device in devices:
        pl.semaphore_signal(barrier, inc=1, device_id=device, device_id_type=MESH)
    pl.semaphore_wait(barrier, len(devices))


def tiles(count, body):
    def step(i, carry):
        body(i)
        return carry

    lax.fori_loop(0, count, step, 0)


def rows_of(i, size):
    return pl.ds(pl.multiple_of(i * size, size), size)


def norm_rows(value, gain, shift_vec):
    centre = value - jnp.mean(value, axis=-1, keepdims=True)
    spread = jnp.mean(centre * centre, axis=-1, keepdims=True)
    return centre * lax.rsqrt(spread + 1e-05) * gain + shift_vec


def spots(base, shape, dim, rows):
    index = lax.broadcasted_iota(jnp.int32, shape, dim)
    return ((index // rows) ^ base) * rows + lax.rem(index, rows)


def gelu_parts(v):
    cube = v * v * v
    inner = np.float32(np.sqrt(2 / np.pi)) * (v + 0.044715 * cube)
    return jnp.tanh(inner)


def masked_scores(raw, slope, length, place, rows, size):
    gap = spots(place, raw.shape, 0, rows) - spots(place, raw.shape, 1, rows)
    open_ = (gap >= 0) | (spots(place, raw.shape, 1, rows) < length)
    scores = raw * np.float32(size ** (-0.5)) - slope * gap.astype(F32)
    return jnp.where(open_, scores, -1e30)


def relayed(layer):
    return [k for k in RELAYED[layer]]


def forward_kernel(
    dims, x_in, vec, qvb, upb, prefix, slopes, wq_in, wo_in, wu_in, wd_in,
    out, wq, wo, wu, wd, x_out, mid_out, nb_out, qkv_out, mix_out, sec_out, up_out, act_out, top_out, lent,
    carry, carry_send, hid, mid, nb, qkv, mix, sec, up, act, outv,
    vq, vo, vu, vd, s1, r1, part, sy, ry, part8, sc, rc, s8, r8,
    line_s, line_r, pair_s, pair_r, own_sem, load_sem, keep_sem, carry_s, carry_r,
    ag_s, ag_r, rs_s, rs_r, ag8_s, ag8_r, f8_s, f8_r, c8_s, c8_r, rs8_s, rs8_r,
    top_s, top_r, near_s, near_r, lent_s, lent_r, direct_s,
):
    n, seqs, heads, size, rows, deep, half = dims
    R = seqs * rows
    wide = heads * size
    D = n * deep
    sect, z, t = lax.axis_index("section"), lax.axis_index("dp"), lax.axis_index("tensor")
    me = (sect, z, t)
    core = (sect, z, t ^ 1)
    chip = (sect, z, t ^ 2)
    plane = (sect, z ^ 1, t)
    diag = (sect, z ^ 1, t ^ 2)
    across = (1 - sect, z, t)
    greet([(s, z ^ k, t) for k in range(1, n) for s in (sect, 1 - sect)] + [core, chip, diag, across])

    def lend(b):
        at = pl.ds(pl.multiple_of(((z & 1) ^ b) * half, half), half)
        return remote(wd_in.at[at], lent.at[at], lent_s.at[b], lent_r.at[b], across)

    def on_layer(layer, body):
        pl.when(sect == layer)(body)

    def lends(layer):
        return [b for b in range(2) if any(k & 1 == b for k in relayed(layer))]

    for layer in range(2):
        def body():
            for b in lends(layer):
                lend(b).start()

        on_layer(layer, body)

    zl = z & 1
    mine = [
        pltpu.make_async_copy(wq_in, wq.at[:, pl.ds(pl.multiple_of(z * deep, deep), deep)], own_sem.at[0]),
        pltpu.make_async_copy(wo_in, wo.at[z], own_sem.at[1]),
        pltpu.make_async_copy(
            wu_in.at[:, pl.ds(pl.multiple_of(zl * half, half), half)],
            wu.at[pl.ds(pl.multiple_of(z * deep, deep), deep)], own_sem.at[2]),
        pltpu.make_async_copy(
            wd_in.at[pl.ds(pl.multiple_of(zl * half, half), half)], wd.at[z], own_sem.at[3]),
    ]

    def slot(a, b):
        if a == 0:
            return wq.at[:, pl.ds(pl.multiple_of(b * deep, deep), deep)]
        return wo.at[b]

    def line(a, side, step, b):
        to = (sect, z + 1 - 2 * side, t)
        src = (wq_in, wo_in)[a] if step == 1 else slot(a, b)
        i = (a * 2 + side) * (n - 1) + step - 1
        return remote(src, slot(a, b), line_s.at[i], line_r.at[i], to)

    def line_send(a, side, step):
        b = z - (step - 1) if side == 0 else z + (step - 1)
        ok = (b >= 0) & (z < n - 1) if side == 0 else (b <= n - 1) & (z > 0)
        return ok, lambda: line(a, side, step, b)

    def line_recv(a, side, step):
        b = z - step if side == 0 else z + step
        ok = (b >= 0) if side == 0 else (b <= n - 1)
        return ok, lambda: line(a, side, step, b)

    def pair(a, k):
        h = (z ^ k) & 1
        to = (sect if a == 0 else 1 - sect, z ^ k, t)
        i = a * (n - 1) + k - 1
        if a == 0:
            src = wu_in.at[:, pl.ds(pl.multiple_of(h * half, half), half)]
            dst = wu.at[pl.ds(pl.multiple_of(z * deep, deep), deep)]
        else:
            src = lent.at[pl.ds(pl.multiple_of(h * half, half), half)]
            dst = wd.at[z]
        return remote(src, dst, pair_s.at[i], pair_r.at[i], to)

    def pair_recv(a, k):
        i = a * (n - 1) + k - 1
        if a == 0:
            src = wu_in.at[:, pl.ds(0, half)]
            dst = wu.at[pl.ds(pl.multiple_of((z ^ k) * deep, deep), deep)]
        else:
            src = wd_in.at[pl.ds(0, half)]
            dst = wd.at[z ^ k]
        return remote(src, dst, pair_s.at[i], pair_r.at[i], (sect, z ^ k, t))

    for a in range(2):
        for side in range(2):
            ok, make = line_send(a, side, 1)

            @pl.when(ok)
            def _():
                make().start()

    for copy in mine:
        copy.start()

    tile = 32

    def first_norm():
        def body(i):
            sl = rows_of(i, tile)
            v = hid[sl, :].astype(F32)
            nb[0, sl, :] = norm_rows(v, vec[0:1, :], vec[2:3, :]).astype(BF)

        tiles(R // tile, body)

    def ag(i):
        src, to = ((0, core), (0, chip), (2, core))[i]
        dst = (1, 2, 3)[i]
        return remote(nb.at[src], nb.at[dst], ag_s.at[i], ag_r.at[i], to)

    @pl.when(sect == 0)
    def _():
        hid[...] = x_in[...]
        first_norm()
        ag(1).start()
        ag(0).start()
        ag(1).wait_recv()
        ag(2).start()

    def direct(k):
        i = n - 1 + k - 1
        src = wd_in.at[pl.ds(pl.multiple_of(((z ^ k) & 1) * half, half), half)]
        return remote(src, wd.at[z], direct_s.at[k - 1], pair_r.at[i], (sect, z ^ k, t))

    def relay(layer):
        for b in lends(layer):
            lend(b).wait_recv()
        for k in relayed(layer):
            pair(1, k).start()

    def top(i):
        return remote(x_in, top_out.at[i], top_s.at[i], top_r.at[i], (core, chip, plane, diag)[i])

    def top_near(i):
        return remote(top_out.at[i], top_out.at[4 + i], near_s.at[i], near_r.at[i], core)

    top_own = pltpu.make_async_copy(x_in, top_out.at[0], own_sem.at[4])
    top_land = [remote(x_in, top_out.at[4], top_s.at[0], top_r.at[0], core)]

    @pl.when(sect == 1)
    def _():
        relay(0)

    for step in range(1, n):
        for a in range(2):
            for side in range(2):
                ok, make = line_recv(a, side, step)

                @pl.when(ok)
                def _():
                    make().wait_recv()

                if step < n - 1:
                    ok, make = line_send(a, side, step + 1)

                    @pl.when(ok)
                    def _():
                        make().start()

        if step == n - 2 or n == 2:
            for k in range(n - 1, 0, -1):
                pair(0, k).start()

            for layer in range(2):
                def body():
                    for k in range(n - 1, 0, -1):
                        if k not in relayed(layer):
                            direct(k).start()

                on_layer(layer, body)

    for copy in mine:
        copy.wait()
    load_q = pltpu.make_async_copy(wq, vq, load_sem.at[0])
    load_o = pltpu.make_async_copy(wo, vo, load_sem.at[1])
    load_q.start()
    load_o.start()

    @pl.when(sect == 1)
    def _():
        top_own.start()
        for i in (1, 2, 3):
            top(i).start()
        top_land[0].start()
        remote(carry_send, carry, carry_s, carry_r, across).wait_recv()
        hid[...] = carry[...]
        first_norm()
        ag(1).start()
        ag(0).start()
        ag(1).wait_recv()
        ag(2).start()

    ag(0).wait_recv()
    ag(2).wait_recv()
    load_q.wait()
    load_o.wait()
    keeps = []

    def keep(src, dst):
        copy = pltpu.make_async_copy(src, dst, keep_sem.at[len(keeps)])
        copy.start()
        keeps.append(copy)

    keep(hid, x_out)
    keep(nb, nb_out)

    tn = min(256, wide)
    for c in range(3):
        def body(i):
            j = lax.rem(i, wide // tn)
            b = i // (wide // tn)
            cols = rows_of(j, tn)
            lhs = jnp.concatenate([nb[2 * b], nb[2 * b + 1]], axis=0)
            got = dot(lhs, vq[c, :, cols]) + qvb[c : c + 1, cols]
            got = got.astype(BF)
            qkv[2 * b, :, pl.ds(pl.multiple_of(c * wide + j * tn, tn), tn)] = got[:R]
            qkv[2 * b + 1, :, pl.ds(pl.multiple_of(c * wide + j * tn, tn), tn)] = got[R:]

        tiles(2 * (wide // tn), body)
    keep(qkv, qkv_out)

    def head(i):
        s, h = i // heads, lax.rem(i, heads)
        pos = rows_of(s, rows)

        def part_of(c):
            cols = pl.ds(pl.multiple_of(c * wide + h * size, size), size)
            return jnp.concatenate([qkv[j, pos, cols] for j in range(4)], axis=0)

        raw = dot(part_of(0), part_of(1), NT)
        scores = masked_scores(raw, slopes[h], prefix[s], t, rows, size)
        expon = jnp.exp(scores - jnp.max(scores, axis=-1, keepdims=True))
        probs = (expon / jnp.sum(expon, axis=-1, keepdims=True)).astype(BF)
        got = dot(probs, part_of(2)).astype(BF)
        for j in range(4):
            mix[j, pos, rows_of(h, size)] = got[j * rows : (j + 1) * rows]

    tiles(seqs * heads, head)
    keep(mix, mix_out)

    def project(pair_of, put):
        lhs_blocks = pair_of

        def body(i):
            lhs = jnp.concatenate([mix[lhs_blocks[0]], mix[lhs_blocks[1]]], axis=0)
            got = dot(lhs, vo[i])
            put(rows_of(i, deep), got)

        tiles(n, body)

    def put_send(cols, got):
        s1[0, :, cols] = got[:R].astype(BF)
        s1[1, :, cols] = got[R:].astype(BF)

    def put_part(cols, got):
        part[0, :, cols] = got[:R]
        part[1, :, cols] = got[R:]

    to_core = remote(s1, r1, rs_s.at[0], rs_r.at[0], core)
    to_chip = remote(sy, ry, rs_s.at[1], rs_r.at[1], chip)
    project((3, 1), put_send)
    to_core.start()
    project((2, 0), put_part)
    to_core.wait_recv()

    def add_chip(i):
        sl = rows_of(i, tile)
        sy[sl, :] = (part[0, sl, :] + r1[0, sl, :].astype(F32)).astype(BF)

    tiles(R // tile, add_chip)
    to_chip.start()
    to_chip.wait_recv()

    def middle_body(i):
        sl = rows_of(i, tile)
        v = hid[sl, :].astype(F32) + part[1, sl, :] + r1[1, sl, :].astype(F32)
        v = v + ry[sl, :].astype(F32) + vec[4:5, :]
        mid[sl, :] = v
        sec[0, sl, :] = norm_rows(v, vec[1:2, :], vec[3:4, :]).astype(BF)

    tiles(R // tile, middle_body)
    keep(mid, mid_out)

    targets = (None, chip, plane, diag)

    def ag8(i):
        return remote(sec.at[0], sec.at[i], ag8_s.at[i], ag8_r.at[i], targets[i])

    def forward8(i):
        return remote(sec.at[i], sec.at[4 + i], f8_s.at[i], f8_r.at[i], core)

    def core8(i):
        return remote(sc.at[i], rc.at[i], c8_s.at[i], c8_r.at[i], core)

    def rs8(i):
        return remote(s8.at[i], r8.at[i], rs8_s.at[i], rs8_r.at[i], targets[i])

    order = (0, 2, 1, 3)
    for i in order[1:]:
        ag8(i).start()
    forward8(0).start()

    for a in range(2):
        for k in range(n - 1, 0, -1):
            pair_recv(a, k).wait_recv()

    load_u = pltpu.make_async_copy(wu, vu, load_sem.at[2])
    load_d = pltpu.make_async_copy(wd, vd, load_sem.at[3])
    load_u.start()
    load_d.start()
    load_u.wait()
    load_d.wait()

    tu = min(256, half)

    def group(i):
        if i:
            ag8(i).wait_recv()
            forward8(i).start()
        forward8(i).wait_recv()

        def up_body(j):
            cols = rows_of(j, tu)
            lhs = jnp.concatenate([sec[i], sec[4 + i]], axis=0)
            v = dot(lhs, vu[:, cols]) + upb[:, cols]
            g = (0.5 * v * (1.0 + gelu_parts(v))).astype(BF)
            up[i, :, cols] = v[:R]
            up[4 + i, :, cols] = v[R:]
            act[i, :, cols] = g[:R]
            act[4 + i, :, cols] = g[R:]

        tiles(half // tu, up_body)

        def down_body(j):
            cols = rows_of(j, deep)
            lhs = jnp.concatenate([act[i], act[4 + i]], axis=0)
            got = dot(lhs, vd[j])
            part8[i, :, cols] = got[:R]
            sc[i, :, cols] = got[R:].astype(BF)

        tiles(n, down_body)
        core8(i).start()

    def reduce(i):
        core8(i).wait_recv()
        if i == 0:
            return

        def body(j):
            sl = rows_of(j, tile)
            s8[i, sl, :] = (part8[i, sl, :] + rc[i, sl, :].astype(F32)).astype(BF)

        tiles(R // tile, body)
        rs8(i).start()

    for number, i in enumerate(order):
        group(i)
        if number:
            reduce(order[number - 1])
    reduce(order[-1])
    keep(sec, sec_out)
    keep(up, up_out)
    keep(act, act_out)
    for i in order[1:]:
        rs8(i).wait_recv()

    def out_body(j):
        sl = rows_of(j, tile)
        v = mid[sl, :] + part8[0, sl, :] + rc[0, sl, :].astype(F32)
        for i in (1, 2, 3):
            v = v + r8[i, sl, :].astype(F32)
        v = v + vec[5:6, :]
        outv[sl, :] = v
        carry_send[sl, :] = v.astype(BF)

    tiles(R // tile, out_body)
    over = remote(carry_send, carry, carry_s, carry_r, across)

    @pl.when(sect == 0)
    def _():
        over.start()
        relay(1)

    keep(outv, out)

    for step in range(1, n):
        for a in range(2):
            for side in range(2):
                ok, make = line_send(a, side, step)

                @pl.when(ok)
                def _():
                    make().wait_send()

    for k in range(n - 1, 0, -1):
        pair(0, k).wait_send()
    for i in range(3):
        ag(i).wait_send()
    to_core.wait_send()
    to_chip.wait_send()
    for i in range(4):
        if i:
            ag8(i).wait_send()
            rs8(i).wait_send()
        forward8(i).wait_send()
        core8(i).wait_send()

    for layer in range(2):
        def body():
            for b in lends(layer):
                lend(b).wait_send()
            for k in range(1, n):
                if k not in relayed(layer):
                    direct(k).wait_send()
            for k in relayed(1 - layer):
                pair(1, k).wait_send()

        on_layer(layer, body)

    @pl.when(sect == 0)
    def _():
        over.wait_send()

    @pl.when(sect == 1)
    def _():
        for i in (1, 2, 3):
            top(i).wait_recv()
            top_near(i).start()
        top_land[0].wait_recv()
        for i in (1, 2, 3):
            top_near(i).wait_recv()
        top_own.wait()
        top_land[0].wait_send()
        for i in (1, 2, 3):
            top(i).wait_send()
            top_near(i).wait_send()

    for copy in keeps:
        copy.wait()


def run_forward(dims, x, vec, qvb, upb, prefix, slopes, wq, wo, wu, wd):
    n, seqs, heads, size, rows, deep, half = dims
    R, wide, D = seqs * rows, heads * size, n * deep
    V = lambda shape, dtype: pltpu.VMEM(shape, dtype)
    S = lambda *shape: jax.ShapeDtypeStruct(shape[:-1], shape[-1])
    any_ = pl.BlockSpec(memory_space=pl.ANY)
    vm = pl.BlockSpec(memory_space=pltpu.VMEM)
    sm = pl.BlockSpec(memory_space=pltpu.SMEM)
    dma = lambda k: pltpu.SemaphoreType.DMA((k,))
    outs = (
        S(R, D, F32), S(3, D, wide, BF), S(n, wide, deep, BF), S(D, half, BF), S(n, half, deep, BF),
        S(R, D, BF), S(R, D, F32), S(4, R, D, BF), S(4, R, 3 * wide, BF), S(4, R, wide, BF),
        S(8, R, D, BF), S(8, R, half, F32), S(8, R, half, BF), S(8, R, D, BF), S(2 * half, deep, BF),
    )
    scratch = [
        V((R, D), BF), V((R, D), BF), V((R, D), BF), V((R, D), F32), V((4, R, D), BF), V((4, R, 3 * wide), BF),
        V((4, R, wide), BF), V((8, R, D), BF), V((8, R, half), F32), V((8, R, half), BF), V((R, D), F32),
        V((3, D, wide), BF), V((n, wide, deep), BF), V((D, half), BF), V((n, half, deep), BF),
        V((2, R, D), BF), V((2, R, D), BF), V((2, R, D), F32), V((R, D), BF), V((R, D), BF),
        V((4, R, D), F32), V((4, R, D), BF), V((4, R, D), BF), V((4, R, D), BF), V((4, R, D), BF),
        dma(4 * (n - 1)), dma(4 * (n - 1)), dma(2 * (n - 1)), dma(2 * (n - 1)), dma(5), dma(4), dma(9),
        pltpu.SemaphoreType.DMA(()), pltpu.SemaphoreType.DMA(()),
        dma(3), dma(3), dma(2), dma(2), dma(4), dma(4), dma(4), dma(4), dma(4), dma(4), dma(4), dma(4),
        dma(4), dma(4), dma(4), dma(4), dma(2), dma(2), dma(n - 1),
    ]
    return pl.pallas_call(
        functools.partial(forward_kernel, dims),
        out_shape=outs,
        in_specs=[vm, vm, vm, vm, sm, sm, any_, any_, any_, any_],
        out_specs=(any_,) * len(outs),
        scratch_shapes=scratch,
        compiler_params=pltpu.CompilerParams(
            collective_id=0, has_side_effects=True, vmem_limit_bytes=60 * 1024 * 1024
        ),
    )(x, vec, qvb, upb, prefix, slopes, wq, wo, wu, wd)


def backward_kernel(
    dims, top, vec, prefix, slopes, wq, wo, wu, wd, hid_in, mid_in, nb_in, qkv_in, mix_in, sec_in, up_in, act_in, top_in,
    dh_out, gq_out, go_out, gu_out, gd_out, sums_out, proj_out, ups_out, ru, rd, rq, ro, lent, lentq,
    carry, grad, mid, hid, dmid, gp, gm, gu, gd, gq, go, part, own8, sc, rc, s8, r8,
    s1, r1, sy, ry, sums, proj, ups, tmpq, tmpo,
    load_sem, up_sem, out_sem, carry_s, carry_r, ag8_s, ag8_r, f8_s, f8_r, c8_s, c8_r, rs8_s, rs8_r,
    ag_s, ag_r, rs_s, rs_r, ffn_s, ffn_r, att_s, att_r, lent_s, lent_r, lentq_s, lentq_r, over_s,
):
    n, seqs, heads, size, rows, deep, half = dims
    R = seqs * rows
    wide = heads * size
    D = n * deep
    sect, z, t = lax.axis_index("section"), lax.axis_index("dp"), lax.axis_index("tensor")
    core = (sect, z, t ^ 1)
    chip = (sect, z, t ^ 2)
    plane = (sect, z ^ 1, t)
    diag = (sect, z ^ 1, t ^ 2)
    across = (1 - sect, z, t)
    greet([(s, z ^ k, t) for k in range(1, n) for s in (sect, 1 - sect)] + [core, chip, diag, across])
    zl = z & 1
    tile = 32
    order = (0, 2, 1, 3)
    targets = (None, chip, plane, diag)

    def ag8(i):
        return remote(gp.at[0], gp.at[i], ag8_s.at[i], ag8_r.at[i], targets[i])

    def forward8(i):
        return remote(gp.at[i], gp.at[4 + i], f8_s.at[i], f8_r.at[i], core)

    def core8(i):
        return remote(sc.at[i], rc.at[i], c8_s.at[i], c8_r.at[i], core)

    def rs8(i):
        return remote(s8.at[i - 1], r8.at[i - 1], rs8_s.at[i], rs8_r.at[i], targets[i])

    def load(src, dst, i):
        copy = pltpu.make_async_copy(src, dst, load_sem.at[i])
        copy.start()
        return copy

    load_mid, load_hid = load(mid_in, mid, 0), load(hid_in, hid, 1)
    sums[...] = jnp.zeros_like(sums)
    proj[...] = jnp.zeros_like(proj)
    ups[...] = jnp.zeros_like(ups)
    over = remote(s1.at[0], carry, carry_s, carry_r, across)

    def col_sum(row, value):
        sums[row : row + 1, :] += jnp.sum(value, axis=0, keepdims=True)

    def ffn(a, k):
        i = a * (n - 1) + k - 1
        to = (sect if a == 0 else 1 - sect, z ^ k, t)
        src = gu.at[k] if a == 0 else lent.at[k - 1]
        return remote(src, (ru, rd)[a].at[k - 1], ffn_s.at[i], ffn_r.at[i], to)

    def direct(k):
        return remote(gd.at[k], rd.at[k - 1], lent_s.at[k - 1], ffn_r.at[n - 1 + k - 1], (sect, z ^ k, t))

    def lend(k):
        return remote(gd.at[k], lent.at[k - 1], lent_s.at[k - 1], lent_r.at[k - 1], across)

    def relay(layer):
        for k in GRADS_RELAYED[layer]:
            lend(k).wait_recv()
            ffn(1, k).start()

    def feed(vu, vd, sec, act, dup, upb):
        loads = [load(wu, vu, 2), load(wd, vd, 3), load(sec_in, sec, 4), load(act_in, act, 5)]

        def up_load(number):
            i, slot = order[number], number % 2
            return [
                pltpu.make_async_copy(up_in.at[i + 4 * b], upb.at[slot, b], up_sem.at[2 * slot + b])
                for b in range(2)
            ]

        for number in range(2):
            for copy in up_load(number):
                copy.start()

        load_top = pltpu.make_async_copy(top_in, gp, load_sem.at[6])

        @pl.when(sect == 1)
        def _():
            load_top.start()
            grad[...] = top[...]
            load_top.wait()

        @pl.when(sect == 0)
        def _():
            relay(1)
            over.wait_recv()
            grad[...] = carry[...]
            gp[0] = grad[...]
            for i in order[1:]:
                ag8(i).start()
            forward8(0).start()

        def bias_body(j):
            col_sum(5, grad[rows_of(j, tile), :].astype(F32))

        tiles(R // tile, bias_body)
        for copy in loads:
            copy.wait()
        tu = min(256, half)
        td = min(256, D)

        def group(number):
            i, slot = order[number], number % 2

            @pl.when(sect == 0)
            def _():
                if i:
                    ag8(i).wait_recv()
                    forward8(i).start()
                forward8(i).wait_recv()

            for copy in up_load(number):
                copy.wait()

            def up_body(j):
                cols = rows_of(j, tu)
                got = None
                for b in range(n):
                    at = pl.ds(b * deep, deep)
                    lhs = jnp.concatenate([gp[i, :, at], gp[4 + i, :, at]], axis=0)
                    term = dot(lhs, vd[b, cols, :], NT)
                    got = term if got is None else got + term
                v = jnp.concatenate([upb[slot, 0, :, cols], upb[slot, 1, :, cols]], axis=0)
                th = gelu_parts(v)
                slope = 0.5 * (1.0 + th) + 0.5 * v * (1.0 - th * th) * np.float32(np.sqrt(2 / np.pi)) * (
                    1.0 + np.float32(3 * 0.044715) * v * v
                )
                low = (got * slope).astype(BF)
                dup[i, :, cols] = low[:R]
                dup[4 + i, :, cols] = low[R:]
                ups[0:1, cols] += jnp.sum(low.astype(F32), axis=0, keepdims=True)

            tiles(half // tu, up_body)
            if number + 2 < 4:
                for copy in up_load(number + 2):
                    copy.start()

            def second_body(j):
                cols = rows_of(j, td)
                lhs = jnp.concatenate([dup[i], dup[4 + i]], axis=0)
                got = dot(lhs, vu[cols, :], NT)
                if i == 0:
                    own8[:, cols] = got[:R]
                else:
                    part[slot, :, cols] = got[:R]
                sc[i, :, cols] = got[R:].astype(BF)

            tiles(D // td, second_body)
            core8(i).start()

        def reduce(number):
            i, slot = order[number], number % 2
            core8(i).wait_recv()
            if i == 0:
                return

            def body(j):
                sl = rows_of(j, tile)
                s8[i - 1, sl, :] = (part[slot, sl, :] + rc[i, sl, :].astype(F32)).astype(BF)

            tiles(R // tile, body)
            rs8(i).start()

        for number in range(4):
            group(number)
            if number:
                reduce(number - 1)
        reduce(3)

        th_ = min(256, half)
        for k in list(range(n - 1, 0, -1)) + [0]:
            def down_body(j):
                cols = rows_of(j, th_)
                lhs = act[:, :, cols].reshape(8 * R, th_)
                at = pl.ds(pl.multiple_of((z ^ k) * deep, deep), deep)
                gd[k, cols, :] = dot(lhs, gp[:, :, at].reshape(8 * R, deep), TN).astype(BF)

            tiles(half // th_, down_body)
            dd = min(256, deep)

            def up_body(j):
                at = pl.ds(pl.multiple_of((z ^ k) * deep + j * dd, dd), dd)
                lhs = sec[:, :, at].reshape(8 * R, dd)
                gu[k, rows_of(j, dd), :] = dot(lhs, dup[...].reshape(8 * R, half), TN).astype(BF)

            tiles(deep // dd, up_body)

    pl.run_scoped(
        feed,
        pltpu.VMEM((D, half), BF), pltpu.VMEM((n, half, deep), BF), pltpu.VMEM((8, R, D), BF),
        pltpu.VMEM((8, R, half), BF), pltpu.VMEM((8, R, half), BF), pltpu.VMEM((2, 2, R, half), F32),
    )
    for i in order[1:]:
        rs8(i).wait_recv()
    for layer in range(2):
        @pl.when(sect == layer)
        def _():
            for k in range(n - 1, 0, -1):
                (lend if k in GRADS_RELAYED[layer] else direct)(k).start()
                ffn(0, k).start()

    load_mid.wait()
    load_hid.wait()

    def norm_back(value, gain, dy):
        centre = value - jnp.mean(value, axis=-1, keepdims=True)
        spread = jnp.mean(centre * centre, axis=-1, keepdims=True)
        scale = lax.rsqrt(spread + 1e-05)
        unit = centre * scale
        scaled = dy * gain
        inner = jnp.mean(scaled * unit, axis=-1, keepdims=True)
        return (scaled - jnp.mean(scaled, axis=-1, keepdims=True) - unit * inner) * scale, unit

    def mid_body(j):
        sl = rows_of(j, tile)
        dy = own8[sl, :] + rc[0, sl, :].astype(F32)
        for i in (1, 2, 3):
            dy = dy + r8[i - 1, sl, :].astype(F32)
        back, unit = norm_back(mid[sl, :], vec[1:2, :], dy)
        total = grad[sl, :].astype(F32) + back
        dmid[sl, :] = total
        gm[0, sl, :] = total.astype(BF)
        col_sum(1, dy * unit)
        col_sum(3, dy)
        col_sum(4, total)

    tiles(R // tile, mid_body)

    def ag(i):
        src, to = ((0, core), (0, chip), (2, core))[i]
        dst = (1, 2, 3)[i]
        return remote(gm.at[src], gm.at[dst], ag_s.at[i], ag_r.at[i], to)

    ag(1).start()
    ag(0).start()
    to_core = remote(s1, r1, rs_s.at[0], rs_r.at[0], core)
    to_chip = remote(sy, ry, rs_s.at[1], rs_r.at[1], chip)

    def low_bit(k):
        return k & -k

    def att(k, c):
        i = (k - 1) * 4 + c
        src, dst = (gq.at[k, c], rq.at[k - 1, c]) if c < 3 else (go.at[k], ro.at[k - 1])
        return remote(src, dst, att_s.at[i], att_r.at[i], (sect, z ^ low_bit(k), t))

    def att_lend(k, c):
        i = (k - 1) * 4 + c
        return remote(gq.at[k, c], lentq.at[k - 1, c], lentq_s.at[i], lentq_r.at[i], across)

    def att_relay(k, c):
        i = (k - 1) * 4 + c
        to = (1 - sect, z ^ low_bit(k), t)
        return remote(lentq.at[k - 1, c], rq.at[k - 1, c], over_s.at[i], att_r.at[i], to)

    def att_start(k, c):
        if c not in ATT_RELAYED:
            att(k, c).start()
            return

        @pl.when(sect == 0)
        def _():
            att_lend(k, c).start()

        @pl.when(sect == 1)
        def _():
            att(k, c).start()

    def at_once(k):
        return k > 1 and low_bit(k) == 1

    att_order = [k for k in range(n - 1, 1, -1) if k & 1]
    att_order += sorted((k for k in range(2, n, 2)), key=lambda k: (low_bit(k), -k)) + [1]
    send_order = sorted(range(1, n), key=lambda k: (low_bit(k), -k))

    def attention(vq, vo, nb, qkv, mix, dmix, dqkv):
        loads = [load(wo, vo, 2), load(qkv_in, qkv, 3), load(mix_in, mix, 4), load(nb_in, nb, 5), load(wq, vq, 6)]
        ag(1).wait_recv()
        ag(2).start()
        for copy in loads:
            copy.wait()
        ag(0).wait_recv()

        def mixed(b):
            if b == 1:
                ag(2).wait_recv()
            tw = min(256, wide)

            def body(j):
                cols = rows_of(j, tw)
                got = None
                for p in range(n):
                    at = pl.ds(p * deep, deep)
                    lhs = jnp.concatenate([gm[2 * b, :, at], gm[2 * b + 1, :, at]], axis=0)
                    term = dot(lhs, vo[p, cols, :], NT)
                    got = term if got is None else got + term
                low = got.astype(BF)
                dmix[2 * b, :, cols] = low[:R]
                dmix[2 * b + 1, :, cols] = low[R:]

            tiles(wide // tw, body)

        mixed(0)
        mixed(1)
        tw = min(256, wide)
        for k in send_order + [0]:
            at = pl.ds(pl.multiple_of((z ^ k) * deep, deep), deep)

            def out_body(j):
                cols = rows_of(j, tw)
                lhs = mix[:, :, cols].reshape(4 * R, tw)
                go[k, cols, :] = dot(lhs, gm[:, :, at].reshape(4 * R, deep), TN).astype(BF)

            tiles(wide // tw, out_body)
            if at_once(k):
                att_start(k, 3)

        def head(i):
            s, h = i // heads, lax.rem(i, heads)
            pos = rows_of(s, rows)

            def part_of(ref, c):
                cols = pl.ds(pl.multiple_of(c * wide + h * size, size), size)
                return jnp.concatenate([ref[j, pos, cols] for j in range(4)], axis=0)

            q, k, v, dm = part_of(qkv, 0), part_of(qkv, 1), part_of(qkv, 2), part_of(dmix, 0)
            scores = masked_scores(dot(q, k, NT), slopes[h], prefix[s], t, rows, size)
            expon = jnp.exp(scores - jnp.max(scores, axis=-1, keepdims=True))
            probs = expon / jnp.sum(expon, axis=-1, keepdims=True)
            dp = dot(dm, v, NT)
            inner = jnp.sum(probs * dp, axis=-1, keepdims=True)
            raw = (probs * (dp - inner) * np.float32(size ** (-0.5))).astype(BF)
            for c, got in enumerate((dot(raw, k), dot(raw, q, TN), dot(probs.astype(BF), dm, TN))):
                low = got.astype(BF)
                cols = pl.ds(pl.multiple_of(c * wide + h * size, size), size)
                proj[0:1, cols] += jnp.sum(low.astype(F32), axis=0, keepdims=True)
                for j in range(4):
                    dqkv[j, pos, cols] = low[j * rows : (j + 1) * rows]

        tiles(seqs * heads, head)

        def normed(blocks, put):
            td = min(256, D)

            def body(j):
                cols = rows_of(j, td)
                got = None
                for c in range(3):
                    lhs = jnp.concatenate([dqkv[b, :, c * wide : (c + 1) * wide] for b in blocks], axis=0)
                    term = dot(lhs, vq[c, cols, :], NT)
                    got = term if got is None else got + term
                put(cols, got)

            tiles(D // td, body)

        def put_send(cols, got):
            s1[0, :, cols] = got[:R].astype(BF)
            s1[1, :, cols] = got[R:].astype(BF)

        def put_part(cols, got):
            part[0, :, cols] = got[:R]
            part[1, :, cols] = got[R:]

        def normed_all():
            normed((3, 1), put_send)
            to_core.start()
            normed((2, 0), put_part)
            to_core.wait_recv()

            def add_chip(i):
                sl = rows_of(i, tile)
                sy[sl, :] = (part[0, sl, :] + r1[0, sl, :].astype(F32)).astype(BF)

            tiles(R // tile, add_chip)
            to_chip.start()

        def grads_q():
            for k in send_order + [0]:
                at = pl.ds(pl.multiple_of((z ^ k) * deep, deep), deep)
                for c in range(3):
                    def body(j):
                        cols = rows_of(j, tw)
                        rhs = dqkv[:, :, pl.ds(pl.multiple_of(c * wide + j * tw, tw), tw)].reshape(4 * R, tw)
                        gq[k, c, :, cols] = dot(nb[:, :, at].reshape(4 * R, deep), rhs, TN).astype(BF)

                    tiles(wide // tw, body)
                    if at_once(k):
                        att_start(k, c)

        @pl.when(sect == 0)
        def _():
            grads_q()
            normed_all()

        @pl.when(sect == 1)
        def _():
            normed_all()
            grads_q()

    pl.run_scoped(
        attention,
        pltpu.VMEM((3, D, wide), BF), pltpu.VMEM((n, wide, deep), BF), pltpu.VMEM((4, R, D), BF),
        pltpu.VMEM((4, R, 3 * wide), BF), pltpu.VMEM((4, R, wide), BF), pltpu.VMEM((4, R, wide), BF),
        pltpu.VMEM((4, R, 3 * wide), BF),
    )
    to_chip.wait_recv()
    to_core.wait_send()

    def low_body(j):
        sl = rows_of(j, tile)
        dy = part[1, sl, :] + r1[1, sl, :].astype(F32) + ry[sl, :].astype(F32)
        back, unit = norm_back(hid[sl, :].astype(F32), vec[0:1, :], dy)
        total = dmid[sl, :] + back
        dmid[sl, :] = total
        s1[0, sl, :] = total.astype(BF)
        col_sum(0, dy * unit)
        col_sum(2, dy)

    tiles(R // tile, low_body)

    @pl.when(sect == 1)
    def _():
        over.start()

    outs = []

    def put(src, dst):
        copy = pltpu.make_async_copy(src, dst, out_sem.at[len(outs)])
        copy.start()
        outs.append(copy)

    put(dmid, dh_out)
    put(sums, sums_out)
    put(proj, proj_out)
    put(ups, ups_out)

    for k in send_order:
        if low_bit(k) == 1:
            continue
        for child in send_order:
            if child ^ low_bit(child) != k:
                continue
            for c in range(4):
                att(child, c).wait_recv()
                src = rq.at[child - 1, c] if c < 3 else ro.at[child - 1]
                dst = tmpq if c < 3 else tmpo
                copy = pltpu.make_async_copy(src, dst, load_sem.at[7])
                copy.start()
                copy.wait()
                if c < 3:
                    gq[k, c] = (gq[k, c].astype(F32) + tmpq[...].astype(F32)).astype(BF)
                else:
                    go[k] = (go[k].astype(F32) + tmpo[...].astype(F32)).astype(BF)
                if child == [j for j in send_order if j ^ low_bit(j) == k][-1]:
                    att_start(k, c)

    for c in range(4):
        att_start(1, c)

    @pl.when(sect == 1)
    def _():
        relay(0)
        for k in att_order:
            for c in ATT_RELAYED:
                att_lend(k, c).wait_recv()
                att_relay(k, c).start()

    def final_feed(bu, bd, fu, fd):
        for a in range(2):
            for k in range(n - 1, 0, -1):
                ffn(a, k).wait_recv()
        loads = [load(ru, bu, 2), load(rd, bd, 3)]
        for copy in loads:
            copy.wait()
        step = min(64, deep)

        def up_body(j):
            sl = rows_of(j, step)
            same = gu[0, sl, :].astype(F32)
            other = bu[0, sl, :].astype(F32)
            for k in range(2, n):
                if k % 2 == 0:
                    same = same + bu[k - 1, sl, :].astype(F32)
                else:
                    other = other + bu[k - 1, sl, :].astype(F32)
            fu[0, sl, :] = same
            fu[1, sl, :] = other

        tiles(deep // step, up_body)

        def down_body(j):
            sl = rows_of(j, step)
            same = gd[0, sl, :].astype(F32)
            other = bd[0, sl, :].astype(F32)
            for k in range(2, n):
                if k % 2 == 0:
                    same = same + bd[k - 1, sl, :].astype(F32)
                else:
                    other = other + bd[k - 1, sl, :].astype(F32)
            fd[0, sl, :] = same
            fd[1, sl, :] = other

        tiles(half // step, down_body)
        copies = []
        for b in range(2):
            at = pl.ds(pl.multiple_of((zl ^ b) * half, half), half)
            copies.append(pltpu.make_async_copy(fu.at[b], gu_out.at[:, at], load_sem.at[2 + 2 * b]))
            copies.append(pltpu.make_async_copy(fd.at[b], gd_out.at[at, :], load_sem.at[3 + 2 * b]))
        for copy in copies:
            copy.start()
        for copy in copies:
            copy.wait()

    pl.run_scoped(
        final_feed,
        pltpu.VMEM((n - 1, deep, half), BF), pltpu.VMEM((n - 1, half, deep), BF),
        pltpu.VMEM((2, deep, half), F32), pltpu.VMEM((2, half, deep), F32),
    )

    def final_attention(bq, bo, fq, fo):
        last = [k for k in send_order if k == low_bit(k)]
        for k in last:
            for c in range(4):
                att(k, c).wait_recv()
        loads = [load(rq, bq, 2), load(ro, bo, 3)]
        for copy in loads:
            copy.wait()
        step = min(64, deep)

        def q_body(j):
            sl = rows_of(j, step)
            for c in range(3):
                total = gq[0, c, sl, :].astype(F32)
                for k in last:
                    total = total + bq[k - 1, c, sl, :].astype(F32)
                fq[c, sl, :] = total

        tiles(deep // step, q_body)

        def o_body(j):
            sl = rows_of(j, step)
            total = go[0, sl, :].astype(F32)
            for k in last:
                total = total + bo[k - 1, sl, :].astype(F32)
            fo[sl, :] = total

        tiles(wide // step, o_body)
        copies = [
            pltpu.make_async_copy(fq, gq_out, load_sem.at[2]),
            pltpu.make_async_copy(fo, go_out, load_sem.at[3]),
        ]
        for copy in copies:
            copy.start()
        for copy in copies:
            copy.wait()

    pl.run_scoped(
        final_attention,
        pltpu.VMEM((n - 1, 3, deep, wide), BF), pltpu.VMEM((n - 1, wide, deep), BF),
        pltpu.VMEM((3, deep, wide), F32), pltpu.VMEM((wide, deep), F32),
    )

    for i in range(4):
        @pl.when(sect == 0)
        def _():
            if i:
                ag8(i).wait_send()
            forward8(i).wait_send()

        if i:
            rs8(i).wait_send()
        core8(i).wait_send()
    for i in range(3):
        ag(i).wait_send()
    to_chip.wait_send()
    for layer in range(2):
        @pl.when(sect == layer)
        def _():
            for k in range(1, n):
                ffn(0, k).wait_send()
                (lend if k in GRADS_RELAYED[layer] else direct)(k).wait_send()
            for k in GRADS_RELAYED[1 - layer]:
                ffn(1, k).wait_send()

    for k in range(1, n):
        for c in range(4):
            if c not in ATT_RELAYED:
                att(k, c).wait_send()
                continue

            @pl.when(sect == 0)
            def _():
                att_lend(k, c).wait_send()

            @pl.when(sect == 1)
            def _():
                att(k, c).wait_send()
                att_relay(k, c).wait_send()


    @pl.when(sect == 1)
    def _():
        over.wait_send()

    for copy in outs:
        copy.wait()


def run_backward(dims, top, vec, prefix, slopes, weights, kept):
    n, seqs, heads, size, rows, deep, half = dims
    R, wide, D = seqs * rows, heads * size, n * deep
    V = lambda shape, dtype: pltpu.VMEM(shape, dtype)
    S = lambda *shape: jax.ShapeDtypeStruct(shape[:-1], shape[-1])
    any_ = pl.BlockSpec(memory_space=pl.ANY)
    vm = pl.BlockSpec(memory_space=pltpu.VMEM)
    sm = pl.BlockSpec(memory_space=pltpu.SMEM)
    dma = lambda k: pltpu.SemaphoreType.DMA((k,))
    one = pltpu.SemaphoreType.DMA(())
    outs = (
        S(R, D, F32), S(3, deep, wide, F32), S(wide, deep, F32), S(deep, 2 * half, F32), S(2 * half, deep, F32),
        S(8, D, F32), S(1, 3 * wide, F32), S(1, half, F32),
        S(n - 1, deep, half, BF), S(n - 1, half, deep, BF), S(n - 1, 3, deep, wide, BF), S(n - 1, wide, deep, BF),
        S(n - 1, half, deep, BF), S(n - 1, 3, deep, wide, BF),
    )
    scratch = [
        V((R, D), BF), V((R, D), BF), V((R, D), F32), V((R, D), BF), V((R, D), F32),
        V((8, R, D), BF), V((4, R, D), BF),
        V((n, deep, half), BF), V((n, half, deep), BF), V((n, 3, deep, wide), BF), V((n, wide, deep), BF),
        V((2, R, D), F32), V((R, D), F32), V((4, R, D), BF), V((4, R, D), BF), V((3, R, D), BF), V((3, R, D), BF),
        V((2, R, D), BF), V((2, R, D), BF), V((R, D), BF), V((R, D), BF),
        V((8, D), F32), V((1, 3 * wide), F32), V((1, half), F32), V((deep, wide), BF), V((wide, deep), BF),
        dma(8), dma(4), dma(4), one, one,
        dma(4), dma(4), dma(4), dma(4), dma(4), dma(4), dma(4), dma(4),
        dma(3), dma(3), dma(2), dma(2), dma(2 * (n - 1)), dma(2 * (n - 1)), dma(4 * (n - 1)), dma(4 * (n - 1)), dma(n - 1), dma(n - 1),
        dma(4 * (n - 1)), dma(4 * (n - 1)), dma(4 * (n - 1)),
    ]
    return pl.pallas_call(
        functools.partial(backward_kernel, dims),
        out_shape=outs,
        in_specs=[vm, vm, sm, sm] + [any_] * 13,
        out_specs=(any_,) * len(outs),
        scratch_shapes=scratch,
        compiler_params=pltpu.CompilerParams(
            collective_id=1, has_side_effects=True, vmem_limit_bytes=62 * 1024 * 1024
        ),
    )(top, vec, prefix, slopes, *weights, *kept)


def small_kernel(spread, peers, src, out, got, send_sem, recv_sem):
    sect, z, t = lax.axis_index("section"), lax.axis_index("dp"), lax.axis_index("tensor")
    n, m = peers
    count = n * m
    me = z * m + t

    def peer(k):
        other = me ^ k
        return other, (sect, other // m, lax.rem(other, m))

    greet([peer(k)[1] for k in range(1, count)])
    copies = []
    for k in range(1, count):
        other, device = peer(k)
        block = src if spread else src.at[other]
        copies.append(remote(block, got.at[k], send_sem.at[k], recv_sem.at[k], device))
        copies[-1].start()
    if spread:
        out[me] = src[...]
    else:
        total = src[me]
    for k in range(1, count):
        copies[k - 1].wait_recv()
        if spread:
            out[me ^ k] = got[k]
        else:
            total = total + got[k]
    if not spread:
        out[...] = total
    for copy in copies:
        copy.wait_send()


def small_exchange(value, spread, peers, collective_id):
    count = peers[0] * peers[1]
    block = value.shape if spread else value.shape[1:]
    return pl.pallas_call(
        functools.partial(small_kernel, spread, peers),
        out_shape=jax.ShapeDtypeStruct((count,) + block if spread else block, F32),
        in_specs=[pl.BlockSpec(memory_space=pltpu.VMEM)],
        out_specs=pl.BlockSpec(memory_space=pltpu.VMEM),
        scratch_shapes=[
            pltpu.VMEM((count,) + block, F32),
            pltpu.SemaphoreType.DMA((count,)),
            pltpu.SemaphoreType.DMA((count,)),
        ],
        compiler_params=pltpu.CompilerParams(collective_id=collective_id, has_side_effects=True),
    )(value)


def on_device(activations, ln_gains, biases, w_qkv, qv_bias, w_out, w_up, up_bias, w_down, prefix):
    is_first = lax.axis_index("section") == 0
    plane = lax.axis_index("dp")
    place = lax.axis_index("tensor")
    planes = lax.axis_size("dp")
    tensors = lax.axis_size("tensor")
    odd = plane % 2 == 1
    seqs, rows, width = activations.shape[1:]
    heads, size_part = qv_bias.shape[2:]
    size = size_part * planes
    wide = heads * size
    deep = w_qkv.shape[1]
    units = w_up.shape[2]
    half = units // 2
    own = activations[0]

    flat = jnp.concatenate([v.reshape(-1) for v in (ln_gains, biases, qv_bias, up_bias)])
    peers = (planes, tensors)
    everyone = small_exchange(flat.astype(F32).reshape(-1, 128), True, peers, 2).reshape(planes * tensors, -1)
    lane = width // (planes * tensors)
    cut = 6 * lane
    features = everyone[:, :cut].reshape(-1, 6, lane).swapaxes(0, 1).reshape(6, width)
    mine = everyone.reshape(planes, tensors, -1)
    mine = lax.dynamic_index_in_dim(mine, place, 1, keepdims=False)[:, cut:]
    qv_full = mine[:, : 2 * heads * size_part].reshape(planes, 2, heads, size_part)
    qv_full = qv_full.transpose(1, 2, 0, 3).reshape(2, heads, size)
    up_full = mine[:, 2 * heads * size_part :].reshape(planes, up_bias.shape[1], up_bias.shape[2])
    up_full = up_full.transpose(1, 0, 2).reshape(units)
    up_own = jnp.where(odd, up_full[half:], up_full[:half])

    head_ids = place * heads + jnp.arange(heads)
    slopes = jnp.exp2(-8.0 * (head_ids.astype(F32) + 1.0) / (heads * tensors))

    dims = (planes, seqs, heads, size, rows, deep, half)
    vec = jnp.concatenate([features, jnp.zeros((2, width), F32)], axis=0)
    flat_qv = qv_full.reshape(2, wide)
    qvb = jnp.stack([flat_qv[0], jnp.zeros_like(flat_qv[0]), flat_qv[1]])
    got = run_forward(
        dims, own.reshape(seqs * rows, width), vec, qvb, up_own[None], prefix, slopes,
        w_qkv[0].transpose(1, 0, 2), w_out[0], w_up[0], w_down[0],
    )
    output, weights, kept = got[0], got[1:5], got[5:14]
    back = run_backward(dims, own.reshape(seqs * rows, width), vec, prefix, slopes, weights, kept)
    grad_low, grad_q, grad_o, grad_u, grad_d, vectors, proj_sums, up_sums = back[:8]
    proj_sums, up_sums = proj_sums[0], up_sums[0]

    vec = vectors[:6].reshape(6, planes * tensors, lane).swapaxes(0, 1).reshape(planes * tensors, cut)
    qv_sums = jnp.stack([proj_sums[:wide], proj_sums[2 * wide :]]).reshape(2, heads, planes, size_part)
    qv_sums = qv_sums.transpose(2, 0, 1, 3).reshape(planes, -1)
    zero = jnp.zeros_like(up_sums)
    up_sums = jnp.where(odd, jnp.concatenate([zero, up_sums]), jnp.concatenate([up_sums, zero]))
    up_sums = up_sums.reshape(up_bias.shape[1], planes, up_bias.shape[2]).transpose(1, 0, 2).reshape(planes, -1)
    own_part = jnp.concatenate([qv_sums, up_sums], axis=1)[:, None, :]
    own_part = jnp.where((jnp.arange(tensors) == place)[None, :, None], own_part, 0.0)
    message = jnp.concatenate([vec, own_part.reshape(planes * tensors, -1)], axis=1)
    message = message.reshape(planes * tensors, -1, 128)
    small = small_exchange(message, False, peers, 3).reshape(-1)
    mid = cut + 2 * heads * size_part

    ends = jnp.where(is_first, grad_low, output).reshape(seqs, rows, width)
    return (
        ends[None],
        small[: 2 * lane].reshape(1, 2, lane),
        small[2 * lane : cut].reshape(1, 4, lane),
        grad_q.transpose(1, 0, 2)[None],
        small[cut:mid].reshape(1, 2, heads, size_part),
        grad_o[None],
        grad_u[None],
        small[mid:].reshape(1, up_bias.shape[1], up_bias.shape[2]),
        grad_d[None],
    )


def solution(mesh):
    in_specs = (
        P("section", "dp", "tensor", None),
        P("section", None, ("dp", "tensor")),
        P("section", None, ("dp", "tensor")),
        P("section", "dp", None, "tensor"),
        P("section", None, "tensor", "dp"),
        P("section", "tensor", "dp"),
        P("section", "dp", "tensor"),
        P("section", "tensor", "dp"),
        P("section", "tensor", "dp"),
        P("dp"),
    )
    out_specs = (
        P("section", "dp", "tensor", None),
        P("section", None, ("dp", "tensor")),
        P("section", None, ("dp", "tensor")),
        P("section", "dp", None, "tensor"),
        P("section", None, "tensor", "dp"),
        P("section", "tensor", "dp"),
        P("section", "dp", "tensor"),
        P("section", "tensor", "dp"),
        P("section", "tensor", "dp"),
    )
    return jax.shard_map(
        on_device, mesh=mesh, in_specs=in_specs, out_specs=out_specs, check_vma=False
    )
```

```python
import functools

import jax
import jax.numpy as jnp
import numpy as np
from jax import lax
from jax.experimental import pallas as pl
from jax.experimental.pallas import tpu as pltpu
from jax.sharding import PartitionSpec as P

BF = jnp.bfloat16
F32 = jnp.float32


MESH = pl.DeviceIdType.MESH
RELAYED = ((3,), ())
GRADS_RELAYED = ((), (3, 2))
ATT_RELAYED = (0, 1, 2)
NT = (((1,), (1,)), ((), ()))
TN = (((0,), (0,)), ((), ()))


def dot(a, b, dims=(((1,), (0,)), ((), ()))):
    return lax.dot_general(a, b, dims, preferred_element_type=F32)


def remote(src, dst, send_sem, recv_sem, device):
    return pltpu.make_async_remote_copy(
        src_ref=src, dst_ref=dst, send_sem=send_sem, recv_sem=recv_sem, device_id=device, device_id_type=MESH
    )


def when(condition):
    return True if condition is True else condition


def greet(devices):
    barrier = pltpu.get_barrier_semaphore()
    for device in devices:
        pl.semaphore_signal(barrier, inc=1, device_id=device, device_id_type=MESH)
    pl.semaphore_wait(barrier, len(devices))


def tiles(count, body):
    def step(i, carry):
        body(i)
        return carry

    lax.fori_loop(0, count, step, 0)


def rows_of(i, size):
    return pl.ds(pl.multiple_of(i * size, size), size)


def norm_rows(value, gain, shift_vec):
    centre = value - jnp.mean(value, axis=-1, keepdims=True)
    spread = jnp.mean(centre * centre, axis=-1, keepdims=True)
    return centre * lax.rsqrt(spread + 1e-05) * gain + shift_vec


def spots(base, shape, dim, rows):
    index = lax.broadcasted_iota(jnp.int32, shape, dim)
    return ((index // rows) ^ base) * rows + lax.rem(index, rows)


def gelu_parts(v):
    cube = v * v * v
    inner = np.float32(np.sqrt(2 / np.pi)) * (v + 0.044715 * cube)
    return jnp.tanh(inner)


def masked_scores(raw, slope, length, place, rows, size):
    gap = spots(place, raw.shape, 0, rows) - spots(place, raw.shape, 1, rows)
    open_ = (gap >= 0) | (spots(place, raw.shape, 1, rows) < length)
    scores = raw * np.float32(size ** (-0.5)) - slope * gap.astype(F32)
    return jnp.where(open_, scores, -1e30)


def relayed(layer):
    return [k for k in RELAYED[layer]]


def peers_of(n):
    sect, z, t = lax.axis_index("section"), lax.axis_index("dp"), lax.axis_index("tensor")
    return [(sect, z ^ (k // 4), t ^ (k % 4)) for k in range(1, 4 * n)]


def note_copy(n, k, src, dst, send_sem, recv_sem):
    return remote(src, dst.at[k], send_sem.at[k], recv_sem.at[k], peers_of(n)[k - 1])


def forward_kernel(
    dims, x_in, note, prefix, slopes, wq_in, wo_in, wu_in, wd_in,
    out, wq, wo, wu, wd, x_out, mid_out, nb_out, qkv_out, mix_out, sec_out, up_out, act_out, top_out, lent, vec_out,
    notes, panel, vec, qvb, upb, note_s, note_r,
    carry, carry_send, hid, mid, nb, qkv, mix, sec, up, act, outv,
    vq, vo, vu, vd, s1, r1, part, sy, ry, part8, sc, rc, s8, r8,
    line_s, line_r, pair_s, pair_r, own_sem, load_sem, keep_sem, carry_s, carry_r,
    ag_s, ag_r, rs_s, rs_r, ag8_s, ag8_r, f8_s, f8_r, c8_s, c8_r, rs8_s, rs8_r,
    top_s, top_r, near_s, near_r, lent_s, lent_r, direct_s, cor_s, cor_r,
):
    n, seqs, heads, size, rows, deep, half = dims
    R = seqs * rows
    wide = heads * size
    D = n * deep
    sect, z, t = lax.axis_index("section"), lax.axis_index("dp"), lax.axis_index("tensor")
    me = (sect, z, t)
    core = (sect, z, t ^ 1)
    chip = (sect, z, t ^ 2)
    plane = (sect, z ^ 1, t)
    diag = (sect, z ^ 1, t ^ 2)
    across = (1 - sect, z, t)
    greet(peers_of(n) + [(1 - sect, z ^ k, t) for k in range(n)])
    share = [note_copy(n, k, note, notes, note_s, note_r) for k in range(1, 4 * n)]
    for copy in share:
        copy.start()

    def lend(b):
        at = pl.ds(pl.multiple_of(((z & 1) ^ b) * half, half), half)
        return remote(wd_in.at[at], lent.at[at], lent_s.at[b], lent_r.at[b], across)

    def on_layer(layer, body):
        pl.when(sect == layer)(body)

    def lends(layer):
        return [b for b in range(2) if any(k & 1 == b for k in relayed(layer))]

    for layer in range(2):
        def body():
            for b in lends(layer):
                lend(b).start()

        on_layer(layer, body)

    zl = z & 1
    mine = [
        pltpu.make_async_copy(wq_in, wq.at[:, pl.ds(pl.multiple_of(z * deep, deep), deep)], own_sem.at[0]),
        pltpu.make_async_copy(wo_in, wo.at[z], own_sem.at[1]),
        pltpu.make_async_copy(
            wu_in.at[:, pl.ds(pl.multiple_of(zl * half, half), half)],
            wu.at[pl.ds(pl.multiple_of(z * deep, deep), deep)], own_sem.at[2]),
        pltpu.make_async_copy(
            wd_in.at[pl.ds(pl.multiple_of(zl * half, half), half)], wd.at[z], own_sem.at[3]),
    ]

    def slot(a, b):
        if a == 0:
            return wq.at[:, pl.ds(pl.multiple_of(b * deep, deep), deep)]
        return wo.at[b]

    def line(a, side, step, b):
        to = (sect, z + 1 - 2 * side, t)
        src = (wq_in, wo_in)[a] if step == 1 else slot(a, b)
        i = (a * 2 + side) * (n - 1) + step - 1
        return remote(src, slot(a, b), line_s.at[i], line_r.at[i], to)

    def line_send(a, side, step):
        b = z - (step - 1) if side == 0 else z + (step - 1)
        ok = (b >= 0) & (z < n - 1) if side == 0 else (b <= n - 1) & (z > 0)
        return ok, lambda: line(a, side, step, b)

    def line_recv(a, side, step):
        b = z - step if side == 0 else z + step
        ok = (b >= 0) if side == 0 else (b <= n - 1)
        return ok, lambda: line(a, side, step, b)

    def pair(a, k):
        h = (z ^ k) & 1
        to = (sect if a == 0 else 1 - sect, z ^ k, t)
        i = a * (n - 1) + k - 1
        if a == 0:
            src = wu_in.at[:, pl.ds(pl.multiple_of(h * half, half), half)]
            dst = wu.at[pl.ds(pl.multiple_of(z * deep, deep), deep)]
        else:
            src = lent.at[pl.ds(pl.multiple_of(h * half, half), half)]
            dst = wd.at[z]
        return remote(src, dst, pair_s.at[i], pair_r.at[i], to)

    def pair_recv(a, k):
        i = a * (n - 1) + k - 1
        if a == 0:
            src = wu_in.at[:, pl.ds(0, half)]
            dst = wu.at[pl.ds(pl.multiple_of((z ^ k) * deep, deep), deep)]
        else:
            src = wd_in.at[pl.ds(0, half)]
            dst = wd.at[z ^ k]
        return remote(src, dst, pair_s.at[i], pair_r.at[i], (sect, z ^ k, t))

    for a in range(2):
        for side in range(2):
            ok, make = line_send(a, side, 1)

            @pl.when(ok)
            def _():
                make().start()

    for copy in mine:
        copy.start()

    def vectors():
        for copy in share:
            copy.wait_recv()
        notes[0] = note[...]
        panel[...] = jnp.zeros_like(panel)
        me = z * 4 + t
        lane = D // (4 * n)
        for k in range(4 * n):
            panel[((me ^ k) * lane) // 128] += notes[k, 0:8, :]
        for j in range(D // 128):
            vec[:, j * 128 : (j + 1) * 128] = panel[j]
        low = notes[0, 8:32, :]
        for k in range(4, 4 * n, 4):
            low = low + notes[k, 8:32, :]
        qvb[...] = jnp.zeros_like(qvb)
        for h in range(heads):
            for c in range(2):
                qvb[2 * c : 2 * c + 1, h * size : (h + 1) * size] = low[c * heads + h : c * heads + h + 1, :]
        count = half // 128
        first = low[2 * heads : 2 * heads + count]
        later = low[2 * heads + count : 2 * heads + 2 * count]
        units = jnp.where(zl == 1, later, first)
        for j in range(count):
            upb[0:1, j * 128 : (j + 1) * 128] = units[j : j + 1, :]

    tile = 32

    def first_norm():
        def body(i):
            sl = rows_of(i, tile)
            v = hid[sl, :].astype(F32)
            nb[0, sl, :] = norm_rows(v, vec[0:1, :], vec[2:3, :]).astype(BF)

        tiles(R // tile, body)

    def ag(i):
        src, to = ((0, core), (0, chip), (2, core))[i]
        dst = (1, 2, 3)[i]
        return remote(nb.at[src], nb.at[dst], ag_s.at[i], ag_r.at[i], to)

    vectors()

    @pl.when(sect == 0)
    def _():
        hid[...] = x_in[...]
        first_norm()
        ag(1).start()
        ag(0).start()
        ag(1).wait_recv()
        ag(2).start()

    def direct(k):
        i = n - 1 + k - 1
        src = wd_in.at[pl.ds(pl.multiple_of(((z ^ k) & 1) * half, half), half)]
        return remote(src, wd.at[z], direct_s.at[k - 1], pair_r.at[i], (sect, z ^ k, t))

    def relay(layer):
        for b in lends(layer):
            lend(b).wait_recv()
        for k in relayed(layer):
            pair(1, k).start()

    def top(i):
        return remote(x_in, top_out.at[i], top_s.at[i], top_r.at[i], (core, chip, plane, diag)[i])

    def top_near(i):
        return remote(top_out.at[i], top_out.at[4 + i], near_s.at[i], near_r.at[i], core)

    top_own = pltpu.make_async_copy(x_in, top_out.at[0], own_sem.at[4])
    top_land = [remote(x_in, top_out.at[4], top_s.at[0], top_r.at[0], core)]

    @pl.when(sect == 1)
    def _():
        relay(0)

    for step in range(1, n):
        for a in range(2):
            for side in range(2):
                ok, make = line_recv(a, side, step)

                @pl.when(ok)
                def _():
                    make().wait_recv()

                if step < n - 1:
                    ok, make = line_send(a, side, step + 1)

                    @pl.when(ok)
                    def _():
                        make().start()

        if step == n - 2 or n == 2:
            for k in range(n - 1, 0, -1):
                pair(0, k).start()

            for layer in range(2):
                def body():
                    for k in range(n - 1, 0, -1):
                        if k not in relayed(layer):
                            direct(k).start()

                on_layer(layer, body)

    for copy in mine:
        copy.wait()
    load_q = pltpu.make_async_copy(wq, vq, load_sem.at[0])
    load_o = pltpu.make_async_copy(wo, vo, load_sem.at[1])
    load_q.start()
    load_o.start()

    @pl.when(sect == 1)
    def _():
        top_own.start()
        for i in (1, 2, 3):
            top(i).start()
        top_land[0].start()
        remote(carry_send, carry, carry_s, carry_r, across).wait_recv()
        hid[...] = carry[...]
        first_norm()
        ag(1).start()
        ag(0).start()
        ag(1).wait_recv()
        ag(2).start()

    ag(0).wait_recv()
    ag(2).wait_recv()
    load_q.wait()
    load_o.wait()
    keeps = []

    def keep(src, dst):
        copy = pltpu.make_async_copy(src, dst, keep_sem.at[len(keeps)])
        copy.start()
        keeps.append(copy)

    keep(hid, x_out)
    keep(nb, nb_out)
    keep(vec, vec_out)

    tn = min(256, wide)
    for c in range(3):
        def body(i):
            j = lax.rem(i, wide // tn)
            b = i // (wide // tn)
            cols = rows_of(j, tn)
            lhs = jnp.concatenate([nb[2 * b], nb[2 * b + 1]], axis=0)
            got = dot(lhs, vq[c, :, cols]) + qvb[c : c + 1, cols]
            got = got.astype(BF)
            qkv[2 * b, :, pl.ds(pl.multiple_of(c * wide + j * tn, tn), tn)] = got[:R]
            qkv[2 * b + 1, :, pl.ds(pl.multiple_of(c * wide + j * tn, tn), tn)] = got[R:]

        tiles(2 * (wide // tn), body)
    keep(qkv, qkv_out)

    def head(i):
        s, h = i // heads, lax.rem(i, heads)
        pos = rows_of(s, rows)

        def part_of(c):
            cols = pl.ds(pl.multiple_of(c * wide + h * size, size), size)
            return jnp.concatenate([qkv[j, pos, cols] for j in range(4)], axis=0)

        raw = dot(part_of(0), part_of(1), NT)
        scores = masked_scores(raw, slopes[h], prefix[s], t, rows, size)
        expon = jnp.exp(scores - jnp.max(scores, axis=-1, keepdims=True))
        probs = (expon / jnp.sum(expon, axis=-1, keepdims=True)).astype(BF)
        got = dot(probs, part_of(2)).astype(BF)
        for j in range(4):
            mix[j, pos, rows_of(h, size)] = got[j * rows : (j + 1) * rows]

    tiles(seqs * heads, head)
    keep(mix, mix_out)

    def project(pair_of, put):
        lhs_blocks = pair_of

        def body(i):
            lhs = jnp.concatenate([mix[lhs_blocks[0]], mix[lhs_blocks[1]]], axis=0)
            got = dot(lhs, vo[i])
            put(rows_of(i, deep), got)

        tiles(n, body)

    def put_send(cols, got):
        s1[0, :, cols] = got[:R].astype(BF)
        s1[1, :, cols] = got[R:].astype(BF)

    def put_part(cols, got):
        part[0, :, cols] = got[:R]
        part[1, :, cols] = got[R:]

    to_core = remote(s1, r1, rs_s.at[0], rs_r.at[0], core)
    to_chip = remote(sy, ry, rs_s.at[1], rs_r.at[1], chip)
    project((3, 1), put_send)
    to_core.start()
    project((2, 0), put_part)
    to_core.wait_recv()

    def add_chip(i):
        sl = rows_of(i, tile)
        sy[sl, :] = (part[0, sl, :] + r1[0, sl, :].astype(F32)).astype(BF)

    tiles(R // tile, add_chip)
    to_chip.start()
    to_chip.wait_recv()

    def middle_body(i):
        sl = rows_of(i, tile)
        v = hid[sl, :].astype(F32) + part[1, sl, :] + r1[1, sl, :].astype(F32)
        v = v + ry[sl, :].astype(F32) + vec[4:5, :]
        mid[sl, :] = v
        sec[0, sl, :] = norm_rows(v, vec[1:2, :], vec[3:4, :]).astype(BF)

    tiles(R // tile, middle_body)
    keep(mid, mid_out)

    targets = (None, chip, plane, diag)

    def ag8(i):
        return remote(sec.at[0], sec.at[i], ag8_s.at[i], ag8_r.at[i], targets[i])

    def corner8(i):
        at = pl.ds(i * (R // 2), R // 2)
        return remote(sec.at[2 - i, at], sec.at[3, at], cor_s.at[i], cor_r.at[i], (chip, plane)[i])

    def forward8(i):
        return remote(sec.at[i], sec.at[4 + i], f8_s.at[i], f8_r.at[i], core)

    def core8(i):
        return remote(sc.at[i], rc.at[i], c8_s.at[i], c8_r.at[i], core)

    def rs8(i):
        return remote(s8.at[i], r8.at[i], rs8_s.at[i], rs8_r.at[i], targets[i])

    order = (0, 2, 1, 3)
    for i in order[1:3]:
        ag8(i).start()
    forward8(0).start()

    for a in range(2):
        for k in range(n - 1, 0, -1):
            pair_recv(a, k).wait_recv()

    load_u = pltpu.make_async_copy(wu, vu, load_sem.at[2])
    load_d = pltpu.make_async_copy(wd, vd, load_sem.at[3])
    load_u.start()
    load_d.start()
    load_u.wait()
    load_d.wait()

    tu = min(256, half)

    def group(i):
        if i == order[1]:
            for k, side in ((2, 0), (1, 1)):
                ag8(k).wait_recv()
                corner8(side).start()
                forward8(k).start()
        if i == 3:
            corner8(0).wait_recv()
            corner8(1).wait_recv()
            forward8(3).start()
        forward8(i).wait_recv()

        def up_body(j):
            cols = rows_of(j, tu)
            lhs = jnp.concatenate([sec[i], sec[4 + i]], axis=0)
            v = dot(lhs, vu[:, cols]) + upb[:, cols]
            g = (0.5 * v * (1.0 + gelu_parts(v))).astype(BF)
            up[i, :, cols] = v[:R]
            up[4 + i, :, cols] = v[R:]
            act[i, :, cols] = g[:R]
            act[4 + i, :, cols] = g[R:]

        tiles(half // tu, up_body)

        def down_body(j):
            cols = rows_of(j, deep)
            lhs = jnp.concatenate([act[i], act[4 + i]], axis=0)
            got = dot(lhs, vd[j])
            part8[i, :, cols] = got[:R]
            sc[i, :, cols] = got[R:].astype(BF)

        tiles(n, down_body)
        core8(i).start()

    def reduce(i):
        core8(i).wait_recv()
        if i == 0:
            return

        def body(j):
            sl = rows_of(j, tile)
            s8[i, sl, :] = (part8[i, sl, :] + rc[i, sl, :].astype(F32)).astype(BF)

        tiles(R // tile, body)
        rs8(i).start()

    for number, i in enumerate(order):
        group(i)
        if number:
            reduce(order[number - 1])
    reduce(order[-1])
    keep(sec, sec_out)
    keep(up, up_out)
    keep(act, act_out)
    for i in order[1:]:
        rs8(i).wait_recv()

    def out_body(j):
        sl = rows_of(j, tile)
        v = mid[sl, :] + part8[0, sl, :] + rc[0, sl, :].astype(F32)
        for i in (1, 2, 3):
            v = v + r8[i, sl, :].astype(F32)
        v = v + vec[5:6, :]
        outv[sl, :] = v
        carry_send[sl, :] = v.astype(BF)

    tiles(R // tile, out_body)
    over = remote(carry_send, carry, carry_s, carry_r, across)

    @pl.when(sect == 0)
    def _():
        over.start()
        relay(1)

    keep(outv, out)

    for copy in share:
        copy.wait_send()
    for step in range(1, n):
        for a in range(2):
            for side in range(2):
                ok, make = line_send(a, side, step)

                @pl.when(ok)
                def _():
                    make().wait_send()

    for k in range(n - 1, 0, -1):
        pair(0, k).wait_send()
    for i in range(3):
        ag(i).wait_send()
    to_core.wait_send()
    to_chip.wait_send()
    for i in range(4):
        if i in (1, 2):
            ag8(i).wait_send()
            corner8(i - 1).wait_send()
        if i:
            rs8(i).wait_send()
        forward8(i).wait_send()
        core8(i).wait_send()

    for layer in range(2):
        def body():
            for b in lends(layer):
                lend(b).wait_send()
            for k in range(1, n):
                if k not in relayed(layer):
                    direct(k).wait_send()
            for k in relayed(1 - layer):
                pair(1, k).wait_send()

        on_layer(layer, body)

    @pl.when(sect == 0)
    def _():
        over.wait_send()

    @pl.when(sect == 1)
    def _():
        for i in (1, 2, 3):
            top(i).wait_recv()
            top_near(i).start()
        top_land[0].wait_recv()
        for i in (1, 2, 3):
            top_near(i).wait_recv()
        top_own.wait()
        top_land[0].wait_send()
        for i in (1, 2, 3):
            top(i).wait_send()
            top_near(i).wait_send()

    for copy in keeps:
        copy.wait()


def run_forward(dims, x, note, prefix, slopes, wq, wo, wu, wd):
    n, seqs, heads, size, rows, deep, half = dims
    R, wide, D = seqs * rows, heads * size, n * deep
    V = lambda shape, dtype: pltpu.VMEM(shape, dtype)
    S = lambda *shape: jax.ShapeDtypeStruct(shape[:-1], shape[-1])
    any_ = pl.BlockSpec(memory_space=pl.ANY)
    vm = pl.BlockSpec(memory_space=pltpu.VMEM)
    sm = pl.BlockSpec(memory_space=pltpu.SMEM)
    dma = lambda k: pltpu.SemaphoreType.DMA((k,))
    outs = (
        S(R, D, F32), S(3, D, wide, BF), S(n, wide, deep, BF), S(D, half, BF), S(n, half, deep, BF),
        S(R, D, BF), S(R, D, F32), S(4, R, D, BF), S(4, R, 3 * wide, BF), S(4, R, wide, BF),
        S(8, R, D, BF), S(8, R, half, F32), S(8, R, half, BF), S(8, R, D, BF), S(2 * half, deep, BF), S(8, D, F32),
    )
    scratch = [
        V((4 * n, 32, 128), F32), V((D // 128, 8, 128), F32), V((8, D), F32), V((4, wide), F32), V((1, half), F32),
        dma(4 * n), dma(4 * n),
        V((R, D), BF), V((R, D), BF), V((R, D), BF), V((R, D), F32), V((4, R, D), BF), V((4, R, 3 * wide), BF),
        V((4, R, wide), BF), V((8, R, D), BF), V((8, R, half), F32), V((8, R, half), BF), V((R, D), F32),
        V((3, D, wide), BF), V((n, wide, deep), BF), V((D, half), BF), V((n, half, deep), BF),
        V((2, R, D), BF), V((2, R, D), BF), V((2, R, D), F32), V((R, D), BF), V((R, D), BF),
        V((4, R, D), F32), V((4, R, D), BF), V((4, R, D), BF), V((4, R, D), BF), V((4, R, D), BF),
        dma(4 * (n - 1)), dma(4 * (n - 1)), dma(2 * (n - 1)), dma(2 * (n - 1)), dma(5), dma(4), dma(10),
        pltpu.SemaphoreType.DMA(()), pltpu.SemaphoreType.DMA(()),
        dma(3), dma(3), dma(2), dma(2), dma(4), dma(4), dma(4), dma(4), dma(4), dma(4), dma(4), dma(4),
        dma(4), dma(4), dma(4), dma(4), dma(2), dma(2), dma(n - 1), dma(2), dma(2),
    ]
    return pl.pallas_call(
        functools.partial(forward_kernel, dims),
        out_shape=outs,
        in_specs=[vm, vm, sm, sm, any_, any_, any_, any_],
        out_specs=(any_,) * len(outs),
        scratch_shapes=scratch,
        compiler_params=pltpu.CompilerParams(
            collective_id=0, has_side_effects=True, vmem_limit_bytes=60 * 1024 * 1024
        ),
    )(x, note, prefix, slopes, wq, wo, wu, wd)


def backward_kernel(
    dims, top, vec, prefix, slopes, wq, wo, wu, wd, hid_in, mid_in, nb_in, qkv_in, mix_in, sec_in, up_in, act_in, top_in,
    dh_out, gq_out, go_out, gu_out, gd_out, sums_out, low_out, ru, rd, rq, ro, lent, lentq,
    carry, grad, mid, hid, dmid, gp, gm, gu, gd, gq, go, part, own8, sc, rc, s8, r8,
    s1, r1, sy, ry, sums, proj, ups, tmpq, tmpo, panel, low, notes, lows, sums_v, low_v, note_s, note_r, low_s, low_r,
    load_sem, up_sem, out_sem, carry_s, carry_r, ag8_s, ag8_r, f8_s, f8_r, c8_s, c8_r, rs8_s, rs8_r,
    ag_s, ag_r, rs_s, rs_r, ffn_s, ffn_r, att_s, att_r, lent_s, lent_r, lentq_s, lentq_r, over_s, cor_s, cor_r,
):
    n, seqs, heads, size, rows, deep, half = dims
    R = seqs * rows
    wide = heads * size
    D = n * deep
    sect, z, t = lax.axis_index("section"), lax.axis_index("dp"), lax.axis_index("tensor")
    core = (sect, z, t ^ 1)
    chip = (sect, z, t ^ 2)
    plane = (sect, z ^ 1, t)
    diag = (sect, z ^ 1, t ^ 2)
    across = (1 - sect, z, t)
    greet(peers_of(n) + [(1 - sect, z ^ k, t) for k in range(n)])
    zl = z & 1
    tile = 32
    order = (0, 2, 1, 3)
    targets = (None, chip, plane, diag)

    def ag8(i):
        return remote(gp.at[0], gp.at[i], ag8_s.at[i], ag8_r.at[i], targets[i])

    def corner8(i):
        at = pl.ds(i * (R // 2), R // 2)
        return remote(gp.at[2 - i, at], gp.at[3, at], cor_s.at[i], cor_r.at[i], (chip, plane)[i])

    def forward8(i):
        return remote(gp.at[i], gp.at[4 + i], f8_s.at[i], f8_r.at[i], core)

    def core8(i):
        return remote(sc.at[i], rc.at[i], c8_s.at[i], c8_r.at[i], core)

    def rs8(i):
        return remote(s8.at[i - 1], r8.at[i - 1], rs8_s.at[i], rs8_r.at[i], targets[i])

    def load(src, dst, i):
        copy = pltpu.make_async_copy(src, dst, load_sem.at[i])
        copy.start()
        return copy

    load_mid, load_hid = load(mid_in, mid, 0), load(hid_in, hid, 1)
    sums[...] = jnp.zeros_like(sums)
    proj[...] = jnp.zeros_like(proj)
    ups[...] = jnp.zeros_like(ups)
    over = remote(s1.at[0], carry, carry_s, carry_r, across)

    def col_sum(row, value):
        sums[row : row + 1, :] += jnp.sum(value, axis=0, keepdims=True)

    def ffn(a, k):
        i = a * (n - 1) + k - 1
        to = (sect if a == 0 else 1 - sect, z ^ k, t)
        src = gu.at[k] if a == 0 else lent.at[k - 1]
        return remote(src, (ru, rd)[a].at[k - 1], ffn_s.at[i], ffn_r.at[i], to)

    def direct(k):
        return remote(gd.at[k], rd.at[k - 1], lent_s.at[k - 1], ffn_r.at[n - 1 + k - 1], (sect, z ^ k, t))

    def lend(k):
        return remote(gd.at[k], lent.at[k - 1], lent_s.at[k - 1], lent_r.at[k - 1], across)

    def relay(layer):
        for k in GRADS_RELAYED[layer]:
            lend(k).wait_recv()
            ffn(1, k).start()

    def feed(vu, vd, sec, act, dup, upb):
        loads = [load(wd, vd, 3), load(wu, vu, 2), load(sec_in, sec, 4), load(act_in, act, 5)]

        def up_load(number, turn):
            i, slot = turn[number], number % 2
            return [
                pltpu.make_async_copy(up_in.at[i + 4 * b], upb.at[slot, b], up_sem.at[2 * slot + b])
                for b in range(2)
            ]

        load_top = pltpu.make_async_copy(top_in, gp, load_sem.at[6])
        for layer in range(2):
            @pl.when(sect == layer)
            def _():
                for number in range(2):
                    for copy in up_load(number, order[:: 1 - 2 * layer]):
                        copy.start()


        @pl.when(sect == 1)
        def _():
            load_top.start()
            grad[...] = top[...]
            load_top.wait()

        @pl.when(sect == 0)
        def _():
            relay(1)
            over.wait_recv()
            grad[...] = carry[...]
            gp[0] = grad[...]
            for i in order[1:3]:
                ag8(i).start()
            forward8(0).start()

        def bias_body(j):
            col_sum(5, grad[rows_of(j, tile), :].astype(F32))

        tiles(R // tile, bias_body)
        for copy in loads:
            copy.wait()
        tu = min(256, half)
        td = min(256, D)

        def group(number, turn, arriving):
            i, slot = turn[number], number % 2
            if arriving:
                if number == 1:
                    for k, side in ((2, 0), (1, 1)):
                        ag8(k).wait_recv()
                        corner8(side).start()
                        forward8(k).start()
                if i == 3:
                    corner8(0).wait_recv()
                    corner8(1).wait_recv()
                    forward8(3).start()
                forward8(i).wait_recv()
            for copy in up_load(number, turn):
                copy.wait()

            def up_body(j):
                cols = rows_of(j, tu)
                got = None
                for b in range(n):
                    at = pl.ds(b * deep, deep)
                    lhs = jnp.concatenate([gp[i, :, at], gp[4 + i, :, at]], axis=0)
                    term = dot(lhs, vd[b, cols, :], NT)
                    got = term if got is None else got + term
                v = jnp.concatenate([upb[slot, 0, :, cols], upb[slot, 1, :, cols]], axis=0)
                th = gelu_parts(v)
                slope = 0.5 * (1.0 + th) + 0.5 * v * (1.0 - th * th) * np.float32(np.sqrt(2 / np.pi)) * (
                    1.0 + np.float32(3 * 0.044715) * v * v
                )
                low = (got * slope).astype(BF)
                dup[i, :, cols] = low[:R]
                dup[4 + i, :, cols] = low[R:]
                ups[0:1, cols] += jnp.sum(low.astype(F32), axis=0, keepdims=True)

            tiles(half // tu, up_body)
            if number + 2 < 4:
                for copy in up_load(number + 2, turn):
                    copy.start()

            def second_body(j):
                cols = rows_of(j, td)
                lhs = jnp.concatenate([dup[i], dup[4 + i]], axis=0)
                got = dot(lhs, vu[cols, :], NT)
                if i == 0:
                    own8[:, cols] = got[:R]
                else:
                    part[slot, :, cols] = got[:R]
                sc[i, :, cols] = got[R:].astype(BF)

            tiles(D // td, second_body)
            core8(i).start()

        def reduce(number, turn):
            i, slot = turn[number], number % 2
            core8(i).wait_recv()
            if i == 0:
                return

            def body(j):
                sl = rows_of(j, tile)
                s8[i - 1, sl, :] = (part[slot, sl, :] + rc[i, sl, :].astype(F32)).astype(BF)

            tiles(R // tile, body)
            rs8(i).start()

        def every(turn, arriving):
            for number in range(4):
                group(number, turn, arriving)
                if number:
                    reduce(number - 1, turn)
            reduce(3, turn)

        @pl.when(sect == 0)
        def _():
            every(order, True)

        @pl.when(sect == 1)
        def _():
            every(order[::-1], False)

        th_ = min(256, half)
        for k in list(range(n - 1, 0, -1)) + [0]:
            def down_body(j):
                cols = rows_of(j, th_)
                lhs = act[:, :, cols].reshape(8 * R, th_)
                at = pl.ds(pl.multiple_of((z ^ k) * deep, deep), deep)
                gd[k, cols, :] = dot(lhs, gp[:, :, at].reshape(8 * R, deep), TN).astype(BF)

            tiles(half // th_, down_body)
            dd = min(256, deep)

            def up_body(j):
                at = pl.ds(pl.multiple_of((z ^ k) * deep + j * dd, dd), dd)
                lhs = sec[:, :, at].reshape(8 * R, dd)
                gu[k, rows_of(j, dd), :] = dot(lhs, dup[...].reshape(8 * R, half), TN).astype(BF)

            tiles(deep // dd, up_body)

    pl.run_scoped(
        feed,
        pltpu.VMEM((D, half), BF), pltpu.VMEM((n, half, deep), BF), pltpu.VMEM((8, R, D), BF),
        pltpu.VMEM((8, R, half), BF), pltpu.VMEM((8, R, half), BF), pltpu.VMEM((2, 2, R, half), F32),
    )
    for i in order[1:]:
        rs8(i).wait_recv()
    for layer in range(2):
        @pl.when(sect == layer)
        def _():
            for k in range(n - 1, 0, -1):
                (lend if k in GRADS_RELAYED[layer] else direct)(k).start()
                ffn(0, k).start()

    load_mid.wait()
    load_hid.wait()

    def norm_back(value, gain, dy):
        centre = value - jnp.mean(value, axis=-1, keepdims=True)
        spread = jnp.mean(centre * centre, axis=-1, keepdims=True)
        scale = lax.rsqrt(spread + 1e-05)
        unit = centre * scale
        scaled = dy * gain
        inner = jnp.mean(scaled * unit, axis=-1, keepdims=True)
        return (scaled - jnp.mean(scaled, axis=-1, keepdims=True) - unit * inner) * scale, unit

    def mid_body(j):
        sl = rows_of(j, tile)
        dy = own8[sl, :] + rc[0, sl, :].astype(F32)
        for i in (1, 2, 3):
            dy = dy + r8[i - 1, sl, :].astype(F32)
        back, unit = norm_back(mid[sl, :], vec[1:2, :], dy)
        total = grad[sl, :].astype(F32) + back
        dmid[sl, :] = total
        gm[0, sl, :] = total.astype(BF)
        col_sum(1, dy * unit)
        col_sum(3, dy)
        col_sum(4, total)

    tiles(R // tile, mid_body)

    def ag(i):
        src, to = ((0, core), (0, chip), (2, core))[i]
        dst = (1, 2, 3)[i]
        return remote(gm.at[src], gm.at[dst], ag_s.at[i], ag_r.at[i], to)

    ag(1).start()
    ag(0).start()
    to_core = remote(s1, r1, rs_s.at[0], rs_r.at[0], core)
    to_chip = remote(sy, ry, rs_s.at[1], rs_r.at[1], chip)

    def low_bit(k):
        return k & -k

    def att(k, c):
        i = (k - 1) * 4 + c
        src, dst = (gq.at[k, c], rq.at[k - 1, c]) if c < 3 else (go.at[k], ro.at[k - 1])
        return remote(src, dst, att_s.at[i], att_r.at[i], (sect, z ^ low_bit(k), t))

    def att_lend(k, c):
        i = (k - 1) * 4 + c
        return remote(gq.at[k, c], lentq.at[k - 1, c], lentq_s.at[i], lentq_r.at[i], across)

    def att_relay(k, c):
        i = (k - 1) * 4 + c
        to = (1 - sect, z ^ low_bit(k), t)
        return remote(lentq.at[k - 1, c], rq.at[k - 1, c], over_s.at[i], att_r.at[i], to)

    def att_start(k, c):
        if c not in ATT_RELAYED:
            att(k, c).start()
            return

        @pl.when(sect == 0)
        def _():
            att_lend(k, c).start()

        @pl.when(sect == 1)
        def _():
            att(k, c).start()

    def at_once(k):
        return k > 1 and low_bit(k) == 1

    att_order = [k for k in range(n - 1, 1, -1) if k & 1]
    att_order += sorted((k for k in range(2, n, 2)), key=lambda k: (low_bit(k), -k)) + [1]
    send_order = sorted(range(1, n), key=lambda k: (low_bit(k), -k))

    def attention(vq, vo, nb, qkv, mix, dmix, dqkv):
        loads = [load(wo, vo, 2), load(qkv_in, qkv, 3), load(mix_in, mix, 4), load(nb_in, nb, 5), load(wq, vq, 6)]
        ag(1).wait_recv()
        ag(2).start()
        for copy in loads:
            copy.wait()
        ag(0).wait_recv()

        def mixed(b):
            if b == 1:
                ag(2).wait_recv()
            tw = min(256, wide)

            def body(j):
                cols = rows_of(j, tw)
                got = None
                for p in range(n):
                    at = pl.ds(p * deep, deep)
                    lhs = jnp.concatenate([gm[2 * b, :, at], gm[2 * b + 1, :, at]], axis=0)
                    term = dot(lhs, vo[p, cols, :], NT)
                    got = term if got is None else got + term
                low = got.astype(BF)
                dmix[2 * b, :, cols] = low[:R]
                dmix[2 * b + 1, :, cols] = low[R:]

            tiles(wide // tw, body)

        mixed(0)
        mixed(1)
        tw = min(256, wide)
        for k in send_order + [0]:
            at = pl.ds(pl.multiple_of((z ^ k) * deep, deep), deep)

            def out_body(j):
                cols = rows_of(j, tw)
                lhs = mix[:, :, cols].reshape(4 * R, tw)
                go[k, cols, :] = dot(lhs, gm[:, :, at].reshape(4 * R, deep), TN).astype(BF)

            tiles(wide // tw, out_body)
            if at_once(k):
                att_start(k, 3)

        def head(i):
            s, h = i // heads, lax.rem(i, heads)
            pos = rows_of(s, rows)

            def part_of(ref, c):
                cols = pl.ds(pl.multiple_of(c * wide + h * size, size), size)
                return jnp.concatenate([ref[j, pos, cols] for j in range(4)], axis=0)

            q, k, v, dm = part_of(qkv, 0), part_of(qkv, 1), part_of(qkv, 2), part_of(dmix, 0)
            scores = masked_scores(dot(q, k, NT), slopes[h], prefix[s], t, rows, size)
            expon = jnp.exp(scores - jnp.max(scores, axis=-1, keepdims=True))
            probs = expon / jnp.sum(expon, axis=-1, keepdims=True)
            dp = dot(dm, v, NT)
            inner = jnp.sum(probs * dp, axis=-1, keepdims=True)
            raw = (probs * (dp - inner) * np.float32(size ** (-0.5))).astype(BF)
            for c, got in enumerate((dot(raw, k), dot(raw, q, TN), dot(probs.astype(BF), dm, TN))):
                low = got.astype(BF)
                cols = pl.ds(pl.multiple_of(c * wide + h * size, size), size)
                proj[0:1, cols] += jnp.sum(low.astype(F32), axis=0, keepdims=True)
                for j in range(4):
                    dqkv[j, pos, cols] = low[j * rows : (j + 1) * rows]

        tiles(seqs * heads, head)

        def normed(blocks, put):
            td = min(256, D)

            def body(j):
                cols = rows_of(j, td)
                got = None
                for c in range(3):
                    lhs = jnp.concatenate([dqkv[b, :, c * wide : (c + 1) * wide] for b in blocks], axis=0)
                    term = dot(lhs, vq[c, cols, :], NT)
                    got = term if got is None else got + term
                put(cols, got)

            tiles(D // td, body)

        def put_send(cols, got):
            s1[0, :, cols] = got[:R].astype(BF)
            s1[1, :, cols] = got[R:].astype(BF)

        def put_part(cols, got):
            part[0, :, cols] = got[:R]
            part[1, :, cols] = got[R:]

        def normed_all():
            normed((3, 1), put_send)
            to_core.start()
            normed((2, 0), put_part)
            to_core.wait_recv()

            def add_chip(i):
                sl = rows_of(i, tile)
                sy[sl, :] = (part[0, sl, :] + r1[0, sl, :].astype(F32)).astype(BF)

            tiles(R // tile, add_chip)
            to_chip.start()

        def grads_q():
            for k in send_order + [0]:
                at = pl.ds(pl.multiple_of((z ^ k) * deep, deep), deep)
                for c in range(3):
                    def body(j):
                        cols = rows_of(j, tw)
                        rhs = dqkv[:, :, pl.ds(pl.multiple_of(c * wide + j * tw, tw), tw)].reshape(4 * R, tw)
                        gq[k, c, :, cols] = dot(nb[:, :, at].reshape(4 * R, deep), rhs, TN).astype(BF)

                    tiles(wide // tw, body)
                    if at_once(k):
                        att_start(k, c)

        @pl.when(sect == 0)
        def _():
            grads_q()
            normed_all()

        @pl.when(sect == 1)
        def _():
            normed_all()
            grads_q()

    pl.run_scoped(
        attention,
        pltpu.VMEM((3, D, wide), BF), pltpu.VMEM((n, wide, deep), BF), pltpu.VMEM((4, R, D), BF),
        pltpu.VMEM((4, R, 3 * wide), BF), pltpu.VMEM((4, R, wide), BF), pltpu.VMEM((4, R, wide), BF),
        pltpu.VMEM((4, R, 3 * wide), BF),
    )
    to_chip.wait_recv()
    to_core.wait_send()

    def low_body(j):
        sl = rows_of(j, tile)
        dy = part[1, sl, :] + r1[1, sl, :].astype(F32) + ry[sl, :].astype(F32)
        back, unit = norm_back(hid[sl, :].astype(F32), vec[0:1, :], dy)
        total = dmid[sl, :] + back
        dmid[sl, :] = total
        s1[0, sl, :] = total.astype(BF)
        col_sum(0, dy * unit)
        col_sum(2, dy)

    tiles(R // tile, low_body)

    @pl.when(sect == 1)
    def _():
        over.start()

    outs = []

    def put(src, dst):
        copy = pltpu.make_async_copy(src, dst, out_sem.at[len(outs)])
        copy.start()
        outs.append(copy)

    put(dmid, dh_out)

    lane = D // (4 * n)
    for j in range(D // 128):
        panel[j] = sums[:, j * 128 : (j + 1) * 128]
    for h in range(heads):
        for c in range(2):
            at = 2 * c * wide + h * size
            low[c * heads + h : c * heads + h + 1, :] = proj[0:1, at : at + size]
    count = half // 128
    for j in range(count):
        row = ups[0:1, j * 128 : (j + 1) * 128]
        at = 2 * heads + j
        low[at : at + 1, :] = jnp.where(zl == 0, row, 0.0)
        low[at + count : at + count + 1, :] = jnp.where(zl == 1, row, 0.0)
    me = z * 4 + t
    share = []
    for k in range(1, 4 * n):
        to = peers_of(n)[k - 1]
        share.append(
            remote(panel.at[((me ^ k) * lane) // 128], notes.at[k], note_s.at[k], note_r.at[k], to))
        if k % 4 == 0:
            share.append(remote(low, lows.at[k // 4], low_s.at[k // 4], low_r.at[k // 4], to))
    for copy in share:
        copy.start()

    for k in send_order:
        if low_bit(k) == 1:
            continue
        for child in send_order:
            if child ^ low_bit(child) != k:
                continue
            for c in range(4):
                att(child, c).wait_recv()
                src = rq.at[child - 1, c] if c < 3 else ro.at[child - 1]
                dst = tmpq if c < 3 else tmpo
                copy = pltpu.make_async_copy(src, dst, load_sem.at[7])
                copy.start()
                copy.wait()
                if c < 3:
                    gq[k, c] = (gq[k, c].astype(F32) + tmpq[...].astype(F32)).astype(BF)
                else:
                    go[k] = (go[k].astype(F32) + tmpo[...].astype(F32)).astype(BF)
                if child == [j for j in send_order if j ^ low_bit(j) == k][-1]:
                    att_start(k, c)

    for c in range(4):
        att_start(1, c)

    @pl.when(sect == 1)
    def _():
        relay(0)
        for k in att_order:
            for c in ATT_RELAYED:
                att_lend(k, c).wait_recv()
                att_relay(k, c).start()

    for copy in share:
        copy.wait_recv()
    total = panel[(me * lane) // 128]
    for k in range(1, 4 * n):
        total = total + notes[k]
    sums_v[...] = total
    total = low[...]
    for k in range(1, n):
        total = total + lows[k]
    low_v[...] = total
    put(sums_v, sums_out)
    put(low_v, low_out)

    def final_feed(bu, bd, fu, fd):
        for a in range(2):
            for k in range(n - 1, 0, -1):
                ffn(a, k).wait_recv()
        loads = [load(ru, bu, 2), load(rd, bd, 3)]
        for copy in loads:
            copy.wait()
        step = min(64, deep)

        def up_body(j):
            sl = rows_of(j, step)
            same = gu[0, sl, :].astype(F32)
            other = bu[0, sl, :].astype(F32)
            for k in range(2, n):
                if k % 2 == 0:
                    same = same + bu[k - 1, sl, :].astype(F32)
                else:
                    other = other + bu[k - 1, sl, :].astype(F32)
            fu[0, sl, :] = same
            fu[1, sl, :] = other

        tiles(deep // step, up_body)

        def down_body(j):
            sl = rows_of(j, step)
            same = gd[0, sl, :].astype(F32)
            other = bd[0, sl, :].astype(F32)
            for k in range(2, n):
                if k % 2 == 0:
                    same = same + bd[k - 1, sl, :].astype(F32)
                else:
                    other = other + bd[k - 1, sl, :].astype(F32)
            fd[0, sl, :] = same
            fd[1, sl, :] = other

        tiles(half // step, down_body)
        copies = []
        for b in range(2):
            at = pl.ds(pl.multiple_of((zl ^ b) * half, half), half)
            copies.append(pltpu.make_async_copy(fu.at[b], gu_out.at[:, at], load_sem.at[2 + 2 * b]))
            copies.append(pltpu.make_async_copy(fd.at[b], gd_out.at[at, :], load_sem.at[3 + 2 * b]))
        for copy in copies:
            copy.start()
        for copy in copies:
            copy.wait()

    pl.run_scoped(
        final_feed,
        pltpu.VMEM((n - 1, deep, half), BF), pltpu.VMEM((n - 1, half, deep), BF),
        pltpu.VMEM((2, deep, half), F32), pltpu.VMEM((2, half, deep), F32),
    )

    def final_attention(bq, bo, fq, fo):
        last = [k for k in send_order if k == low_bit(k)]
        for k in last:
            for c in range(4):
                att(k, c).wait_recv()
        loads = [load(rq, bq, 2), load(ro, bo, 3)]
        for copy in loads:
            copy.wait()
        step = min(64, deep)

        def q_body(j):
            sl = rows_of(j, step)
            for c in range(3):
                total = gq[0, c, sl, :].astype(F32)
                for k in last:
                    total = total + bq[k - 1, c, sl, :].astype(F32)
                fq[c, sl, :] = total

        tiles(deep // step, q_body)

        def o_body(j):
            sl = rows_of(j, step)
            total = go[0, sl, :].astype(F32)
            for k in last:
                total = total + bo[k - 1, sl, :].astype(F32)
            fo[sl, :] = total

        tiles(wide // step, o_body)
        copies = [
            pltpu.make_async_copy(fq, gq_out, load_sem.at[2]),
            pltpu.make_async_copy(fo, go_out, load_sem.at[3]),
        ]
        for copy in copies:
            copy.start()
        for copy in copies:
            copy.wait()

    pl.run_scoped(
        final_attention,
        pltpu.VMEM((n - 1, 3, deep, wide), BF), pltpu.VMEM((n - 1, wide, deep), BF),
        pltpu.VMEM((3, deep, wide), F32), pltpu.VMEM((wide, deep), F32),
    )

    for i in range(4):
        @pl.when(sect == 0)
        def _():
            if i in (1, 2):
                ag8(i).wait_send()
                corner8(i - 1).wait_send()
            forward8(i).wait_send()

        if i:
            rs8(i).wait_send()
        core8(i).wait_send()
    for i in range(3):
        ag(i).wait_send()
    to_chip.wait_send()
    for layer in range(2):
        @pl.when(sect == layer)
        def _():
            for k in range(1, n):
                ffn(0, k).wait_send()
                (lend if k in GRADS_RELAYED[layer] else direct)(k).wait_send()
            for k in GRADS_RELAYED[1 - layer]:
                ffn(1, k).wait_send()

    for k in range(1, n):
        for c in range(4):
            if c not in ATT_RELAYED:
                att(k, c).wait_send()
                continue

            @pl.when(sect == 0)
            def _():
                att_lend(k, c).wait_send()

            @pl.when(sect == 1)
            def _():
                att(k, c).wait_send()
                att_relay(k, c).wait_send()


    @pl.when(sect == 1)
    def _():
        over.wait_send()

    for copy in share:
        copy.wait_send()
    for copy in outs:
        copy.wait()


def run_backward(dims, top, vec, prefix, slopes, weights, kept):
    n, seqs, heads, size, rows, deep, half = dims
    R, wide, D = seqs * rows, heads * size, n * deep
    V = lambda shape, dtype: pltpu.VMEM(shape, dtype)
    S = lambda *shape: jax.ShapeDtypeStruct(shape[:-1], shape[-1])
    any_ = pl.BlockSpec(memory_space=pl.ANY)
    vm = pl.BlockSpec(memory_space=pltpu.VMEM)
    sm = pl.BlockSpec(memory_space=pltpu.SMEM)
    dma = lambda k: pltpu.SemaphoreType.DMA((k,))
    one = pltpu.SemaphoreType.DMA(())
    outs = (
        S(R, D, F32), S(3, deep, wide, F32), S(wide, deep, F32), S(deep, 2 * half, F32), S(2 * half, deep, F32),
        S(8, 128, F32), S(24, 128, F32),
        S(n - 1, deep, half, BF), S(n - 1, half, deep, BF), S(n - 1, 3, deep, wide, BF), S(n - 1, wide, deep, BF),
        S(n - 1, half, deep, BF), S(n - 1, 3, deep, wide, BF),
    )
    scratch = [
        V((R, D), BF), V((R, D), BF), V((R, D), F32), V((R, D), BF), V((R, D), F32),
        V((8, R, D), BF), V((4, R, D), BF),
        V((n, deep, half), BF), V((n, half, deep), BF), V((n, 3, deep, wide), BF), V((n, wide, deep), BF),
        V((2, R, D), F32), V((R, D), F32), V((4, R, D), BF), V((4, R, D), BF), V((3, R, D), BF), V((3, R, D), BF),
        V((2, R, D), BF), V((2, R, D), BF), V((R, D), BF), V((R, D), BF),
        V((8, D), F32), V((1, 3 * wide), F32), V((1, half), F32), V((deep, wide), BF), V((wide, deep), BF),
        V((D // 128, 8, 128), F32), V((24, 128), F32), V((4 * n, 8, 128), F32), V((n, 24, 128), F32),
        V((8, 128), F32), V((24, 128), F32), dma(4 * n), dma(4 * n), dma(n), dma(n),
        dma(8), dma(4), dma(4), one, one,
        dma(4), dma(4), dma(4), dma(4), dma(4), dma(4), dma(4), dma(4),
        dma(3), dma(3), dma(2), dma(2), dma(2 * (n - 1)), dma(2 * (n - 1)), dma(4 * (n - 1)), dma(4 * (n - 1)), dma(n - 1), dma(n - 1),
        dma(4 * (n - 1)), dma(4 * (n - 1)), dma(4 * (n - 1)), dma(2), dma(2),
    ]
    return pl.pallas_call(
        functools.partial(backward_kernel, dims),
        out_shape=outs,
        in_specs=[vm, vm, sm, sm] + [any_] * 13,
        out_specs=(any_,) * len(outs),
        scratch_shapes=scratch,
        compiler_params=pltpu.CompilerParams(
            collective_id=1, has_side_effects=True, vmem_limit_bytes=62 * 1024 * 1024
        ),
    )(top, vec, prefix, slopes, *weights, *kept)


def on_device(activations, ln_gains, biases, w_qkv, qv_bias, w_out, w_up, up_bias, w_down, prefix):
    is_first = lax.axis_index("section") == 0
    plane = lax.axis_index("dp")
    place = lax.axis_index("tensor")
    planes = lax.axis_size("dp")
    tensors = lax.axis_size("tensor")
    seqs, rows, width = activations.shape[1:]
    heads, part = qv_bias.shape[2:]
    size = part * planes
    deep = w_qkv.shape[1]
    units = w_up.shape[2]
    lane = width // (planes * tensors)
    own = activations[0].reshape(seqs * rows, width)
    spot = (plane * tensors + place) * lane % 128

    def placed(block, start):
        length = block.shape[1]
        wide_block = jnp.tile(block.astype(F32), (1, 128 // length))
        lanes = jnp.arange(128)
        return jnp.where((lanes >= start) & (lanes < start + length), wide_block, 0.0)

    features = placed(jnp.concatenate([ln_gains[0], biases[0]]), spot)
    note = jnp.concatenate([
        features, jnp.zeros((2, 128), F32), placed(qv_bias[0].reshape(2 * heads, part), plane * part),
        placed(up_bias[0], plane * part),
    ])
    head_ids = place * heads + jnp.arange(heads)
    slopes = jnp.exp2(-8.0 * (head_ids.astype(F32) + 1.0) / (heads * tensors))
    dims = (planes, seqs, heads, size, rows, deep, units // 2)
    got = run_forward(
        dims, own, note, prefix, slopes, w_qkv[0].transpose(1, 0, 2), w_out[0], w_up[0], w_down[0]
    )
    output, weights, kept, vec = got[0], got[1:5], got[5:14], got[15]
    back = run_backward(dims, own, vec, prefix, slopes, weights, kept)
    grad_low, grad_q, grad_o, grad_u, grad_d, sums, low = back[:7]
    sums = lax.dynamic_slice_in_dim(sums, spot, lane, 1)
    low = lax.dynamic_slice_in_dim(low, plane * part, part, 1)
    ends = jnp.where(is_first, grad_low, output).reshape(seqs, rows, width)
    return (
        ends[None],
        sums[None, 0:2],
        sums[None, 2:6],
        grad_q.transpose(1, 0, 2)[None],
        low[: 2 * heads].reshape(1, 2, heads, part),
        grad_o[None],
        grad_u[None],
        low[2 * heads :][None],
        grad_d[None],
    )


def solution(mesh):
    in_specs = (
        P("section", "dp", "tensor", None),
        P("section", None, ("dp", "tensor")),
        P("section", None, ("dp", "tensor")),
        P("section", "dp", None, "tensor"),
        P("section", None, "tensor", "dp"),
        P("section", "tensor", "dp"),
        P("section", "dp", "tensor"),
        P("section", "tensor", "dp"),
        P("section", "tensor", "dp"),
        P("dp"),
    )
    out_specs = (
        P("section", "dp", "tensor", None),
        P("section", None, ("dp", "tensor")),
        P("section", None, ("dp", "tensor")),
        P("section", "dp", None, "tensor"),
        P("section", None, "tensor", "dp"),
        P("section", "tensor", "dp"),
        P("section", "dp", "tensor"),
        P("section", "tensor", "dp"),
        P("section", "tensor", "dp"),
    )
    return jax.shard_map(
        on_device, mesh=mesh, in_specs=in_specs, out_specs=out_specs, check_vma=False
    )
```

```python
import functools

import jax
import jax.numpy as jnp
import numpy as np
from jax import lax
from jax.experimental import pallas as pl
from jax.experimental.pallas import tpu as pltpu
from jax.sharding import PartitionSpec as P

BF = jnp.bfloat16
F32 = jnp.float32


MESH = pl.DeviceIdType.MESH
EARLY = True
RELAYED = ((3,), ())
GRADS_RELAYED = ((), (3, 2))
ATT_RELAYED = (0, 1)
NT = (((1,), (1,)), ((), ()))
TN = (((0,), (0,)), ((), ()))


def dot(a, b, dims=(((1,), (0,)), ((), ()))):
    return lax.dot_general(a, b, dims, preferred_element_type=F32)


def remote(src, dst, send_sem, recv_sem, device):
    return pltpu.make_async_remote_copy(
        src_ref=src, dst_ref=dst, send_sem=send_sem, recv_sem=recv_sem, device_id=device, device_id_type=MESH
    )


def when(condition):
    return True if condition is True else condition


def greet(devices):
    barrier = pltpu.get_barrier_semaphore()
    for device in devices:
        pl.semaphore_signal(barrier, inc=1, device_id=device, device_id_type=MESH)
    pl.semaphore_wait(barrier, len(devices))


def tiles(count, body):
    def step(i, carry):
        body(i)
        return carry

    lax.fori_loop(0, count, step, 0)


def half_tiles(count, part, body):
    tiles(count // 2, lambda i: body(i + part * (count // 2)))


def rows_of(i, size):
    return pl.ds(pl.multiple_of(i * size, size), size)


def norm_rows(value, gain, shift_vec):
    centre = value - jnp.mean(value, axis=-1, keepdims=True)
    spread = jnp.mean(centre * centre, axis=-1, keepdims=True)
    return centre * lax.rsqrt(spread + 1e-05) * gain + shift_vec


def spots(base, shape, dim, rows):
    index = lax.broadcasted_iota(jnp.int32, shape, dim)
    return ((index // rows) ^ base) * rows + lax.rem(index, rows)


def gelu_parts(v):
    cube = v * v * v
    inner = np.float32(np.sqrt(2 / np.pi)) * (v + 0.044715 * cube)
    return jnp.tanh(inner)


def masked_scores(raw, slope, length, place, rows, size):
    gap = spots(place, raw.shape, 0, rows) - spots(place, raw.shape, 1, rows)
    open_ = (gap >= 0) | (spots(place, raw.shape, 1, rows) < length)
    scores = raw * np.float32(size ** (-0.5)) - slope * gap.astype(F32)
    return jnp.where(open_, scores, -1e30)


def relayed(layer):
    return [k for k in RELAYED[layer]]


def peers_of(n):
    sect, z, t = lax.axis_index("section"), lax.axis_index("dp"), lax.axis_index("tensor")
    return [(sect, z ^ (k // 4), t ^ (k % 4)) for k in range(1, 4 * n)]


def note_copy(n, k, src, dst, send_sem, recv_sem):
    return remote(src, dst.at[k], send_sem.at[k], recv_sem.at[k], peers_of(n)[k - 1])


def forward_kernel(
    dims, x_in, note, prefix, slopes, wq_in, wo_in, wu_in, wd_in,
    out, wq, wo, wu, wd, x_out, mid_out, nb_out, qkv_out, mix_out, sec_out, up_out, act_out, top_out, lent, vec_out,
    notes, panel, vec, qvb, upb, note_s, note_r,
    carry, carry_send, hid, mid, nb, qkv, mix, sec, up, act, outv,
    vq, vo, vu, vd, s1, r1, part, sy, ry, part8, sc, rc, s8, r8,
    line_s, line_r, pair_s, pair_r, own_sem, load_sem, keep_sem, carry_s, carry_r,
    ag_s, ag_r, rs_s, rs_r, ag8_s, ag8_r, f8_s, f8_r, c8_s, c8_r, rs8_s, rs8_r,
    top_s, top_r, near_s, near_r, lent_s, lent_r, direct_s, cor_s, cor_r,
):
    n, seqs, heads, size, rows, deep, half = dims
    R = seqs * rows
    wide = heads * size
    D = n * deep
    sect, z, t = lax.axis_index("section"), lax.axis_index("dp"), lax.axis_index("tensor")
    me = (sect, z, t)
    core = (sect, z, t ^ 1)
    chip = (sect, z, t ^ 2)
    plane = (sect, z ^ 1, t)
    diag = (sect, z ^ 1, t ^ 2)
    across = (1 - sect, z, t)
    greet(peers_of(n) + [(1 - sect, z ^ k, t) for k in range(n)])
    share = [note_copy(n, k, note, notes, note_s, note_r) for k in range(1, 4 * n)]
    for copy in share:
        copy.start()

    def lend(b):
        at = pl.ds(pl.multiple_of(((z & 1) ^ b) * half, half), half)
        return remote(wd_in.at[at], lent.at[at], lent_s.at[b], lent_r.at[b], across)

    def on_layer(layer, body):
        pl.when(sect == layer)(body)

    def lends(layer):
        return [b for b in range(2) if any(k & 1 == b for k in relayed(layer))]

    for layer in range(2):
        def body():
            for b in lends(layer):
                lend(b).start()

        on_layer(layer, body)

    zl = z & 1
    mine = [
        pltpu.make_async_copy(wq_in, wq.at[:, pl.ds(pl.multiple_of(z * deep, deep), deep)], own_sem.at[0]),
        pltpu.make_async_copy(wo_in, wo.at[z], own_sem.at[1]),
        pltpu.make_async_copy(
            wu_in.at[:, pl.ds(pl.multiple_of(zl * half, half), half)],
            wu.at[pl.ds(pl.multiple_of(z * deep, deep), deep)], own_sem.at[2]),
        pltpu.make_async_copy(
            wd_in.at[pl.ds(pl.multiple_of(zl * half, half), half)], wd.at[z], own_sem.at[3]),
    ]

    def slot(a, b):
        if a == 0:
            return wq.at[:, pl.ds(pl.multiple_of(b * deep, deep), deep)]
        return wo.at[b]

    def line(a, side, step, b):
        to = (sect, z + 1 - 2 * side, t)
        src = (wq_in, wo_in)[a] if step == 1 else slot(a, b)
        i = (a * 2 + side) * (n - 1) + step - 1
        return remote(src, slot(a, b), line_s.at[i], line_r.at[i], to)

    def line_send(a, side, step):
        b = z - (step - 1) if side == 0 else z + (step - 1)
        ok = (b >= 0) & (z < n - 1) if side == 0 else (b <= n - 1) & (z > 0)
        return ok, lambda: line(a, side, step, b)

    def line_recv(a, side, step):
        b = z - step if side == 0 else z + step
        ok = (b >= 0) if side == 0 else (b <= n - 1)
        return ok, lambda: line(a, side, step, b)

    def pair(a, k):
        h = (z ^ k) & 1
        to = (sect if a == 0 else 1 - sect, z ^ k, t)
        i = a * (n - 1) + k - 1
        if a == 0:
            src = wu_in.at[:, pl.ds(pl.multiple_of(h * half, half), half)]
            dst = wu.at[pl.ds(pl.multiple_of(z * deep, deep), deep)]
        else:
            src = lent.at[pl.ds(pl.multiple_of(h * half, half), half)]
            dst = wd.at[z]
        return remote(src, dst, pair_s.at[i], pair_r.at[i], to)

    def pair_recv(a, k):
        i = a * (n - 1) + k - 1
        if a == 0:
            src = wu_in.at[:, pl.ds(0, half)]
            dst = wu.at[pl.ds(pl.multiple_of((z ^ k) * deep, deep), deep)]
        else:
            src = wd_in.at[pl.ds(0, half)]
            dst = wd.at[z ^ k]
        return remote(src, dst, pair_s.at[i], pair_r.at[i], (sect, z ^ k, t))

    for a in range(2):
        for side in range(2):
            ok, make = line_send(a, side, 1)

            @pl.when(ok)
            def _():
                make().start()

    for copy in mine:
        copy.start()

    def vectors():
        for copy in share:
            copy.wait_recv()
        notes[0] = note[...]
        panel[...] = jnp.zeros_like(panel)
        me = z * 4 + t
        lane = D // (4 * n)
        for k in range(4 * n):
            panel[((me ^ k) * lane) // 128] += notes[k, 0:8, :]
        for j in range(D // 128):
            vec[:, j * 128 : (j + 1) * 128] = panel[j]
        low = notes[0, 8:32, :]
        for k in range(4, 4 * n, 4):
            low = low + notes[k, 8:32, :]
        qvb[...] = jnp.zeros_like(qvb)
        for h in range(heads):
            for c in range(2):
                qvb[2 * c : 2 * c + 1, h * size : (h + 1) * size] = low[c * heads + h : c * heads + h + 1, :]
        count = half // 128
        first = low[2 * heads : 2 * heads + count]
        later = low[2 * heads + count : 2 * heads + 2 * count]
        units = jnp.where(zl == 1, later, first)
        for j in range(count):
            upb[0:1, j * 128 : (j + 1) * 128] = units[j : j + 1, :]

    tile = 32

    def part_of_rows(h, size=R):
        return pl.ds(h * (size // 2), size // 2)

    def first_norm(h):
        def body(i):
            sl = rows_of(i, tile)
            v = hid[sl, :].astype(F32)
            nb[0, sl, :] = norm_rows(v, vec[0:1, :], vec[2:3, :]).astype(BF)

        half_tiles(R // tile, h, body)
        ag(1, h).start()
        ag(0, h).start()

    def ag(i, h):
        src, to = ((0, core), (0, chip), (2, core))[i]
        dst = (1, 2, 3)[i]
        at = part_of_rows(h)
        return remote(nb.at[src, at], nb.at[dst, at], ag_s.at[2 * i + h], ag_r.at[2 * i + h], to)

    def over(h):
        at = part_of_rows(h)
        return remote(carry_send.at[at], carry.at[at], carry_s.at[h], carry_r.at[h], across)

    def pass_on():
        for h in range(2):
            ag(1, h).wait_recv()
            ag(2, h).start()

    vectors()

    @pl.when(sect == 0)
    def _():
        hid[...] = x_in[...]
        first_norm(0)
        first_norm(1)
        pass_on()

    def direct(k):
        i = n - 1 + k - 1
        src = wd_in.at[pl.ds(pl.multiple_of(((z ^ k) & 1) * half, half), half)]
        return remote(src, wd.at[z], direct_s.at[k - 1], pair_r.at[i], (sect, z ^ k, t))

    def relay(layer):
        for b in lends(layer):
            lend(b).wait_recv()
        for k in relayed(layer):
            pair(1, k).start()

    def top(i):
        return remote(x_in, top_out.at[i], top_s.at[i], top_r.at[i], (core, chip, plane, diag)[i])

    def top_near(i):
        return remote(top_out.at[i], top_out.at[4 + i], near_s.at[i], near_r.at[i], core)

    top_own = pltpu.make_async_copy(x_in, top_out.at[0], own_sem.at[4])
    top_land = [remote(x_in, top_out.at[4], top_s.at[0], top_r.at[0], core)]

    @pl.when(sect == 1)
    def _():
        relay(0)

    for step in range(1, n):
        for a in range(2):
            for side in range(2):
                ok, make = line_recv(a, side, step)

                @pl.when(ok)
                def _():
                    make().wait_recv()

                if step < n - 1:
                    ok, make = line_send(a, side, step + 1)

                    @pl.when(ok)
                    def _():
                        make().start()

        if step == n - 2 or n == 2:
            for k in range(n - 1, 0, -1):
                pair(0, k).start()

    for layer in range(2):
        def body():
            for k in range(n - 1, 0, -1):
                if k not in relayed(layer):
                    direct(k).start()

        on_layer(layer, body)

    for copy in mine:
        copy.wait()
    load_q = pltpu.make_async_copy(wq, vq, load_sem.at[0])
    load_o = pltpu.make_async_copy(wo, vo, load_sem.at[1])
    load_q.start()
    load_o.start()

    @pl.when(sect == 1)
    def _():
        top_own.start()
        for i in (1, 2, 3):
            top(i).start()
        top_land[0].start()
        for h in range(2):
            over(h).wait_recv()
            hid[part_of_rows(h), :] = carry[part_of_rows(h), :]
            first_norm(h)

    load_q.wait()
    load_o.wait()
    ag(0, 0).wait_recv()
    ag(0, 1).wait_recv()
    keeps = []

    def keep(src, dst):
        copy = pltpu.make_async_copy(src, dst, keep_sem.at[len(keeps)])
        copy.start()
        keeps.append(copy)

    keep(hid, x_out)
    keep(vec, vec_out)

    tn = min(256, wide)

    def project_in(b):
        for c in range(3):
            def body(j):
                cols = rows_of(j, tn)
                lhs = jnp.concatenate([nb[2 * b], nb[2 * b + 1]], axis=0)
                got = dot(lhs, vq[c, :, cols]) + qvb[c : c + 1, cols]
                got = got.astype(BF)
                qkv[2 * b, :, pl.ds(pl.multiple_of(c * wide + j * tn, tn), tn)] = got[:R]
                qkv[2 * b + 1, :, pl.ds(pl.multiple_of(c * wide + j * tn, tn), tn)] = got[R:]

            tiles(wide // tn, body)

    project_in(0)

    @pl.when(sect == 1)
    def _():
        pass_on()

    ag(2, 0).wait_recv()
    ag(2, 1).wait_recv()
    project_in(1)
    keep(nb, nb_out)
    keep(qkv, qkv_out)

    def head(i):
        s, h = i // heads, lax.rem(i, heads)
        pos = rows_of(s, rows)

        def part_of(c):
            cols = pl.ds(pl.multiple_of(c * wide + h * size, size), size)
            return jnp.concatenate([qkv[j, pos, cols] for j in range(4)], axis=0)

        raw = dot(part_of(0), part_of(1), NT)
        scores = masked_scores(raw, slopes[h], prefix[s], t, rows, size)
        expon = jnp.exp(scores - jnp.max(scores, axis=-1, keepdims=True))
        probs = (expon / jnp.sum(expon, axis=-1, keepdims=True)).astype(BF)
        got = dot(probs, part_of(2)).astype(BF)
        for j in range(4):
            mix[j, pos, rows_of(h, size)] = got[j * rows : (j + 1) * rows]

    tiles(seqs * heads, head)
    keep(mix, mix_out)

    def project(pair_of, put):
        lhs_blocks = pair_of

        def body(i):
            lhs = jnp.concatenate([mix[lhs_blocks[0]], mix[lhs_blocks[1]]], axis=0)
            got = dot(lhs, vo[i])
            put(rows_of(i, deep), got)

        tiles(n, body)

    def put_send(cols, got):
        s1[0, :, cols] = got[:R].astype(BF)
        s1[1, :, cols] = got[R:].astype(BF)

    def put_part(cols, got):
        part[0, :, cols] = got[:R]
        part[1, :, cols] = got[R:]

    to_core = remote(s1, r1, rs_s.at[0], rs_r.at[0], core)
    to_chip = remote(sy, ry, rs_s.at[1], rs_r.at[1], chip)
    project((3, 1), put_send)
    to_core.start()
    project((2, 0), put_part)
    to_core.wait_recv()

    def add_chip(i):
        sl = rows_of(i, tile)
        sy[sl, :] = (part[0, sl, :] + r1[0, sl, :].astype(F32)).astype(BF)

    tiles(R // tile, add_chip)
    to_chip.start()
    to_chip.wait_recv()

    def middle_body(i):
        sl = rows_of(i, tile)
        v = hid[sl, :].astype(F32) + part[1, sl, :] + r1[1, sl, :].astype(F32)
        v = v + ry[sl, :].astype(F32) + vec[4:5, :]
        mid[sl, :] = v
        sec[0, sl, :] = norm_rows(v, vec[1:2, :], vec[3:4, :]).astype(BF)


    targets = (None, chip, plane, diag)

    def ag8(i, h):
        at = part_of_rows(h)
        return remote(sec.at[0, at], sec.at[i, at], ag8_s.at[2 * i + h], ag8_r.at[2 * i + h], targets[i])

    def corner8(i):
        at = pl.ds(i * (R // 2), R // 2)
        return remote(sec.at[2 - i, at], sec.at[3, at], cor_s.at[i], cor_r.at[i], (chip, plane)[i])

    def forward8(i):
        return remote(sec.at[i], sec.at[4 + i], f8_s.at[i], f8_r.at[i], core)

    def core8(i):
        return remote(sc.at[i], rc.at[i], c8_s.at[i], c8_r.at[i], core)

    def rs8(i):
        return remote(s8.at[i], r8.at[i], rs8_s.at[i], rs8_r.at[i], targets[i])

    order = (0, 2, 1, 3)
    for h in range(2):
        half_tiles(R // tile, h, middle_body)
        for i in order[1:3]:
            ag8(i, h).start()
    forward8(0).start()
    keep(mid, mid_out)

    def arrive():
        ag8(2, 0).wait_recv()
        corner8(0).start()
        ag8(2, 1).wait_recv()
        forward8(2).start()
        ag8(1, 0).wait_recv()
        ag8(1, 1).wait_recv()
        corner8(1).start()
        forward8(1).start()

    def arrive_corner():
        corner8(0).wait_recv()
        corner8(1).wait_recv()
        forward8(3).start()

    load_u = pltpu.make_async_copy(wu, vu, load_sem.at[2])
    load_d = pltpu.make_async_copy(wd, vd, load_sem.at[3])

    def weights_in(a):
        for k in range(n - 1, 0, -1):
            pair_recv(a, k).wait_recv()
        (load_u, load_d)[a].start()

    tu = min(256, half)

    def up_part(i):
        def up_body(j):
            cols = rows_of(j, tu)
            lhs = jnp.concatenate([sec[i], sec[4 + i]], axis=0)
            v = dot(lhs, vu[:, cols]) + upb[:, cols]
            g = (0.5 * v * (1.0 + gelu_parts(v))).astype(BF)
            up[i, :, cols] = v[:R]
            up[4 + i, :, cols] = v[R:]
            act[i, :, cols] = g[:R]
            act[4 + i, :, cols] = g[R:]

        tiles(half // tu, up_body)

    def down_part(i):
        def down_body(j):
            cols = rows_of(j, deep)
            lhs = jnp.concatenate([act[i], act[4 + i]], axis=0)
            got = dot(lhs, vd[j])
            part8[i, :, cols] = got[:R]
            sc[i, :, cols] = got[R:].astype(BF)

        tiles(n, down_body)
        core8(i).start()

    def reduce(i):
        core8(i).wait_recv()
        if i == 0:
            return

        def body(j):
            sl = rows_of(j, tile)
            s8[i, sl, :] = (part8[i, sl, :] + rc[i, sl, :].astype(F32)).astype(BF)

        tiles(R // tile, body)
        rs8(i).start()

    @pl.when(sect == 0)
    def _():
        arrive()
        arrive_corner()
        weights_in(0)
        weights_in(1)
        for i in range(4):
            forward8(i).wait_recv()
        load_u.wait()
        load_d.wait()
        for number, i in enumerate(order[::-1]):
            up_part(i)
            down_part(i)
            if number:
                reduce(order[4 - number])
        reduce(order[0])

    @pl.when(sect == 1)
    def _():
        weights_in(0)
        weights_in(1)
        load_u.wait()
        load_d.wait()
        for number, i in enumerate(order):
            if number == 1:
                arrive()
            if number == 3:
                arrive_corner()
            forward8(i).wait_recv()
            up_part(i)
            down_part(i)
            if number:
                reduce(order[number - 1])
        reduce(order[3])

    keep(sec, sec_out)
    keep(up, up_out)
    keep(act, act_out)
    for i in order[1:]:
        rs8(i).wait_recv()

    def out_body(j):
        sl = rows_of(j, tile)
        v = mid[sl, :] + part8[0, sl, :] + rc[0, sl, :].astype(F32)
        for i in (1, 2, 3):
            v = v + r8[i, sl, :].astype(F32)
        v = v + vec[5:6, :]
        outv[sl, :] = v
        carry_send[sl, :] = v.astype(BF)

    for h in range(2):
        half_tiles(R // tile, h, out_body)

        @pl.when(sect == 0)
        def _():
            over(h).start()

    @pl.when(sect == 0)
    def _():
        relay(1)

    keep(outv, out)

    for copy in share:
        copy.wait_send()
    for step in range(1, n):
        for a in range(2):
            for side in range(2):
                ok, make = line_send(a, side, step)

                @pl.when(ok)
                def _():
                    make().wait_send()

    for k in range(n - 1, 0, -1):
        pair(0, k).wait_send()
    for i in range(6):
        ag(i // 2, i % 2).wait_send()
    to_core.wait_send()
    to_chip.wait_send()
    for i in range(4):
        if i in (1, 2):
            ag8(i, 0).wait_send()
            ag8(i, 1).wait_send()
            corner8(i - 1).wait_send()
        if i:
            rs8(i).wait_send()
        forward8(i).wait_send()
        core8(i).wait_send()

    for layer in range(2):
        def body():
            for b in lends(layer):
                lend(b).wait_send()
            for k in range(1, n):
                if k not in relayed(layer):
                    direct(k).wait_send()
            for k in relayed(1 - layer):
                pair(1, k).wait_send()

        on_layer(layer, body)

    @pl.when(sect == 0)
    def _():
        over(0).wait_send()
        over(1).wait_send()

    @pl.when(sect == 1)
    def _():
        for i in (1, 2, 3):
            top(i).wait_recv()
            top_near(i).start()
        top_land[0].wait_recv()
        for i in (1, 2, 3):
            top_near(i).wait_recv()
        top_own.wait()
        top_land[0].wait_send()
        for i in (1, 2, 3):
            top(i).wait_send()
            top_near(i).wait_send()

    for copy in keeps:
        copy.wait()


def run_forward(dims, x, note, prefix, slopes, wq, wo, wu, wd):
    n, seqs, heads, size, rows, deep, half = dims
    R, wide, D = seqs * rows, heads * size, n * deep
    V = lambda shape, dtype: pltpu.VMEM(shape, dtype)
    S = lambda *shape: jax.ShapeDtypeStruct(shape[:-1], shape[-1])
    any_ = pl.BlockSpec(memory_space=pl.ANY)
    vm = pl.BlockSpec(memory_space=pltpu.VMEM)
    sm = pl.BlockSpec(memory_space=pltpu.SMEM)
    dma = lambda k: pltpu.SemaphoreType.DMA((k,))
    outs = (
        S(R, D, F32), S(3, D, wide, BF), S(n, wide, deep, BF), S(D, half, BF), S(n, half, deep, BF),
        S(R, D, BF), S(R, D, F32), S(4, R, D, BF), S(4, R, 3 * wide, BF), S(4, R, wide, BF),
        S(8, R, D, BF), S(8, R, half, F32), S(8, R, half, BF), S(8, R, D, BF), S(2 * half, deep, BF), S(8, D, F32),
    )
    scratch = [
        V((4 * n, 32, 128), F32), V((D // 128, 8, 128), F32), V((8, D), F32), V((4, wide), F32), V((1, half), F32),
        dma(4 * n), dma(4 * n),
        V((R, D), BF), V((R, D), BF), V((R, D), BF), V((R, D), F32), V((4, R, D), BF), V((4, R, 3 * wide), BF),
        V((4, R, wide), BF), V((8, R, D), BF), V((8, R, half), F32), V((8, R, half), BF), V((R, D), F32),
        V((3, D, wide), BF), V((n, wide, deep), BF), V((D, half), BF), V((n, half, deep), BF),
        V((2, R, D), BF), V((2, R, D), BF), V((2, R, D), F32), V((R, D), BF), V((R, D), BF),
        V((4, R, D), F32), V((4, R, D), BF), V((4, R, D), BF), V((4, R, D), BF), V((4, R, D), BF),
        dma(4 * (n - 1)), dma(4 * (n - 1)), dma(2 * (n - 1)), dma(2 * (n - 1)), dma(5), dma(4), dma(10),
        dma(2), dma(2),
        dma(6), dma(6), dma(2), dma(2), dma(8), dma(8), dma(4), dma(4), dma(4), dma(4), dma(4), dma(4),
        dma(4), dma(4), dma(4), dma(4), dma(2), dma(2), dma(n - 1), dma(2), dma(2),
    ]
    return pl.pallas_call(
        functools.partial(forward_kernel, dims),
        out_shape=outs,
        in_specs=[vm, vm, sm, sm, any_, any_, any_, any_],
        out_specs=(any_,) * len(outs),
        scratch_shapes=scratch,
        compiler_params=pltpu.CompilerParams(
            collective_id=0, has_side_effects=True, vmem_limit_bytes=60 * 1024 * 1024
        ),
    )(x, note, prefix, slopes, wq, wo, wu, wd)


def backward_kernel(
    dims, top, vec, prefix, slopes, wq, wo, wu, wd, hid_in, mid_in, nb_in, qkv_in, mix_in, sec_in, up_in, act_in, top_in,
    dh_out, gq_out, go_out, gu_out, gd_out, sums_out, low_out, ru, rd, rq, ro, lent, lentq,
    carry, grad, mid, hid, dmid, gp, gm, gu, gd, gq, go, part, own8, sc, rc, s8, r8,
    s1, r1, sy, ry, sums, proj, ups, tmpq, tmpo, panel, low, notes, lows, sums_v, low_v, note_s, note_r, low_s, low_r,
    load_sem, up_sem, out_sem, carry_s, carry_r, ag8_s, ag8_r, f8_s, f8_r, c8_s, c8_r, rs8_s, rs8_r,
    ag_s, ag_r, rs_s, rs_r, ffn_s, ffn_r, att_s, att_r, lent_s, lent_r, lentq_s, lentq_r, over_s, cor_s, cor_r,
):
    n, seqs, heads, size, rows, deep, half = dims
    R = seqs * rows
    wide = heads * size
    D = n * deep
    sect, z, t = lax.axis_index("section"), lax.axis_index("dp"), lax.axis_index("tensor")
    core = (sect, z, t ^ 1)
    chip = (sect, z, t ^ 2)
    plane = (sect, z ^ 1, t)
    diag = (sect, z ^ 1, t ^ 2)
    across = (1 - sect, z, t)
    greet(peers_of(n) + [(1 - sect, z ^ k, t) for k in range(n)])
    zl = z & 1
    tile = 32
    order = (0, 2, 1, 3)
    targets = (None, chip, plane, diag)

    def part_of_rows(h):
        return pl.ds(h * (R // 2), R // 2)

    def ag8(i, h):
        at = part_of_rows(h)
        return remote(gp.at[0, at], gp.at[i, at], ag8_s.at[2 * i + h], ag8_r.at[2 * i + h], targets[i])

    def corner8(i):
        at = pl.ds(i * (R // 2), R // 2)
        return remote(gp.at[2 - i, at], gp.at[3, at], cor_s.at[i], cor_r.at[i], (chip, plane)[i])

    def forward8(i):
        return remote(gp.at[i], gp.at[4 + i], f8_s.at[i], f8_r.at[i], core)

    def core8(i):
        return remote(sc.at[i], rc.at[i], c8_s.at[i], c8_r.at[i], core)

    def rs8(i):
        return remote(s8.at[i - 1], r8.at[i - 1], rs8_s.at[i], rs8_r.at[i], targets[i])

    def load(src, dst, i):
        copy = pltpu.make_async_copy(src, dst, load_sem.at[i])
        copy.start()
        return copy

    load_mid, load_hid = load(mid_in, mid, 0), load(hid_in, hid, 1)
    sums[...] = jnp.zeros_like(sums)
    proj[...] = jnp.zeros_like(proj)
    ups[...] = jnp.zeros_like(ups)

    def over(h):
        at = part_of_rows(h)
        return remote(s1.at[0, at], carry.at[at], carry_s.at[h], carry_r.at[h], across)

    def col_sum(row, value):
        sums[row : row + 1, :] += jnp.sum(value, axis=0, keepdims=True)

    def ffn(a, k):
        i = a * (n - 1) + k - 1
        to = (sect if a == 0 else 1 - sect, z ^ k, t)
        src = gu.at[k] if a == 0 else lent.at[k - 1]
        return remote(src, (ru, rd)[a].at[k - 1], ffn_s.at[i], ffn_r.at[i], to)

    def direct(k):
        return remote(gd.at[k], rd.at[k - 1], lent_s.at[k - 1], ffn_r.at[n - 1 + k - 1], (sect, z ^ k, t))

    def lend(k):
        return remote(gd.at[k], lent.at[k - 1], lent_s.at[k - 1], lent_r.at[k - 1], across)

    def ffn_start(layer, k):
        (lend if k in GRADS_RELAYED[layer] else direct)(k).start()
        ffn(0, k).start()

    def relay(layer):
        for k in GRADS_RELAYED[layer]:
            lend(k).wait_recv()
            ffn(1, k).start()

    def feed(vu, vd, sec, act, dup, upb):
        loads = [load(wd, vd, 3), load(wu, vu, 2), load(sec_in, sec, 4), load(act_in, act, 5)]

        def up_load(number, turn):
            i, slot = turn[number], number % 2
            return [
                pltpu.make_async_copy(up_in.at[i + 4 * b], upb.at[slot, b], up_sem.at[2 * slot + b])
                for b in range(2)
            ]

        load_top = pltpu.make_async_copy(top_in, gp, load_sem.at[6])
        for layer in range(2):
            @pl.when(sect == layer)
            def _():
                for number in range(2):
                    for copy in up_load(number, order[:: 1 - 2 * layer]):
                        copy.start()


        @pl.when(sect == 1)
        def _():
            load_top.start()
            grad[...] = top[...]
            load_top.wait()

        @pl.when(sect == 0)
        def _():
            relay(1)
            for h in range(2):
                over(h).wait_recv()
                value = carry[part_of_rows(h), :]
                grad[part_of_rows(h), :] = value
                gp[0, part_of_rows(h), :] = value
                for i in order[1:3]:
                    ag8(i, h).start()
            forward8(0).start()

        def bias_body(j):
            col_sum(5, grad[rows_of(j, tile), :].astype(F32))

        tiles(R // tile, bias_body)
        for copy in loads:
            copy.wait()
        tu = min(256, half)
        td = min(256, D)

        def group(number, turn, arriving):
            i, slot = turn[number], number % 2
            if arriving:
                if number == 1:
                    ag8(2, 0).wait_recv()
                    corner8(0).start()
                    ag8(2, 1).wait_recv()
                    forward8(2).start()
                    ag8(1, 0).wait_recv()
                    ag8(1, 1).wait_recv()
                    corner8(1).start()
                    forward8(1).start()
                if i == 3:
                    corner8(0).wait_recv()
                    corner8(1).wait_recv()
                    forward8(3).start()
                forward8(i).wait_recv()
            for copy in up_load(number, turn):
                copy.wait()

            def up_body(j):
                cols = rows_of(j, tu)
                got = None
                for b in range(n):
                    at = pl.ds(b * deep, deep)
                    lhs = jnp.concatenate([gp[i, :, at], gp[4 + i, :, at]], axis=0)
                    term = dot(lhs, vd[b, cols, :], NT)
                    got = term if got is None else got + term
                v = jnp.concatenate([upb[slot, 0, :, cols], upb[slot, 1, :, cols]], axis=0)
                th = gelu_parts(v)
                slope = 0.5 * (1.0 + th) + 0.5 * v * (1.0 - th * th) * np.float32(np.sqrt(2 / np.pi)) * (
                    1.0 + np.float32(3 * 0.044715) * v * v
                )
                low = (got * slope).astype(BF)
                dup[i, :, cols] = low[:R]
                dup[4 + i, :, cols] = low[R:]
                ups[0:1, cols] += jnp.sum(low.astype(F32), axis=0, keepdims=True)

            tiles(half // tu, up_body)
            if number + 2 < 4:
                for copy in up_load(number + 2, turn):
                    copy.start()

            def second_body(j):
                cols = rows_of(j, td)
                lhs = jnp.concatenate([dup[i], dup[4 + i]], axis=0)
                got = dot(lhs, vu[cols, :], NT)
                if i == 0:
                    own8[:, cols] = got[:R]
                else:
                    part[slot, :, cols] = got[:R]
                sc[i, :, cols] = got[R:].astype(BF)

            tiles(D // td, second_body)
            core8(i).start()

        def reduce(number, turn):
            i, slot = turn[number], number % 2
            core8(i).wait_recv()
            if i == 0:
                return

            def body(j):
                sl = rows_of(j, tile)
                s8[i - 1, sl, :] = (part[slot, sl, :] + rc[i, sl, :].astype(F32)).astype(BF)

            tiles(R // tile, body)
            rs8(i).start()

        def every(turn, arriving):
            for number in range(4):
                group(number, turn, arriving)
                if number:
                    reduce(number - 1, turn)
            reduce(3, turn)

        @pl.when(sect == 0)
        def _():
            every(order, True)

        @pl.when(sect == 1)
        def _():
            every(order[::-1], False)

        th_ = min(256, half)
        for k in list(range(n - 1, 0, -1)) + [0]:
            def down_body(j):
                cols = rows_of(j, th_)
                lhs = act[:, :, cols].reshape(8 * R, th_)
                at = pl.ds(pl.multiple_of((z ^ k) * deep, deep), deep)
                gd[k, cols, :] = dot(lhs, gp[:, :, at].reshape(8 * R, deep), TN).astype(BF)

            tiles(half // th_, down_body)
            dd = min(256, deep)

            def up_body(j):
                at = pl.ds(pl.multiple_of((z ^ k) * deep + j * dd, dd), dd)
                lhs = sec[:, :, at].reshape(8 * R, dd)
                gu[k, rows_of(j, dd), :] = dot(lhs, dup[...].reshape(8 * R, half), TN).astype(BF)

            tiles(deep // dd, up_body)
            if EARLY and k:
                @pl.when(sect == 0)
                def _():
                    ffn_start(0, k)

    pl.run_scoped(
        feed,
        pltpu.VMEM((D, half), BF), pltpu.VMEM((n, half, deep), BF), pltpu.VMEM((8, R, D), BF),
        pltpu.VMEM((8, R, half), BF), pltpu.VMEM((8, R, half), BF), pltpu.VMEM((2, 2, R, half), F32),
    )
    for i in order[1:]:
        rs8(i).wait_recv()
    for layer in range(1 if EARLY else 0, 2):
        @pl.when(sect == layer)
        def _():
            for k in range(n - 1, 0, -1):
                ffn_start(layer, k)

    load_mid.wait()
    load_hid.wait()

    def norm_back(value, gain, dy):
        centre = value - jnp.mean(value, axis=-1, keepdims=True)
        spread = jnp.mean(centre * centre, axis=-1, keepdims=True)
        scale = lax.rsqrt(spread + 1e-05)
        unit = centre * scale
        scaled = dy * gain
        inner = jnp.mean(scaled * unit, axis=-1, keepdims=True)
        return (scaled - jnp.mean(scaled, axis=-1, keepdims=True) - unit * inner) * scale, unit

    def mid_body(j):
        sl = rows_of(j, tile)
        dy = own8[sl, :] + rc[0, sl, :].astype(F32)
        for i in (1, 2, 3):
            dy = dy + r8[i - 1, sl, :].astype(F32)
        back, unit = norm_back(mid[sl, :], vec[1:2, :], dy)
        total = grad[sl, :].astype(F32) + back
        dmid[sl, :] = total
        gm[0, sl, :] = total.astype(BF)
        col_sum(1, dy * unit)
        col_sum(3, dy)
        col_sum(4, total)

    def ag(i, h):
        src, to = ((0, core), (0, chip), (2, core))[i]
        dst = (1, 2, 3)[i]
        at = part_of_rows(h)
        return remote(gm.at[src, at], gm.at[dst, at], ag_s.at[2 * i + h], ag_r.at[2 * i + h], to)

    for h in range(2):
        half_tiles(R // tile, h, mid_body)
        ag(1, h).start()
        ag(0, h).start()
    to_core = remote(s1, r1, rs_s.at[0], rs_r.at[0], core)
    to_chip = remote(sy, ry, rs_s.at[1], rs_r.at[1], chip)

    def low_bit(k):
        return k & -k

    def att(k, c):
        i = (k - 1) * 4 + c
        src, dst = (gq.at[k, c], rq.at[k - 1, c]) if c < 3 else (go.at[k], ro.at[k - 1])
        return remote(src, dst, att_s.at[i], att_r.at[i], (sect, z ^ low_bit(k), t))

    def att_lend(k, c):
        i = (k - 1) * 4 + c
        return remote(gq.at[k, c], lentq.at[k - 1, c], lentq_s.at[i], lentq_r.at[i], across)

    def att_relay(k, c):
        i = (k - 1) * 4 + c
        to = (1 - sect, z ^ low_bit(k), t)
        return remote(lentq.at[k - 1, c], rq.at[k - 1, c], over_s.at[i], att_r.at[i], to)

    def att_start(k, c):
        if c not in ATT_RELAYED:
            att(k, c).start()
            return

        @pl.when(sect == 0)
        def _():
            att_lend(k, c).start()

        @pl.when(sect == 1)
        def _():
            att(k, c).start()

    def at_once(k):
        return k > 1 and low_bit(k) == 1

    att_order = [k for k in range(n - 1, 1, -1) if k & 1]
    att_order += sorted((k for k in range(2, n, 2)), key=lambda k: (low_bit(k), -k)) + [1]
    send_order = sorted(range(1, n), key=lambda k: (low_bit(k), -k))

    def attention(vq, vo, nb, qkv, mix, dmix, dqkv):
        loads = [load(wo, vo, 2), load(qkv_in, qkv, 3), load(mix_in, mix, 4), load(nb_in, nb, 5), load(wq, vq, 6)]
        loads[0].wait()
        ag(0, 0).wait_recv()
        ag(0, 1).wait_recv()

        def mixed(b):
            if b == 1:
                for h in range(2):
                    ag(1, h).wait_recv()
                    ag(2, h).start()
                for copy in loads[1:]:
                    copy.wait()
                ag(2, 0).wait_recv()
                ag(2, 1).wait_recv()
            tw = min(256, wide)

            def body(j):
                cols = rows_of(j, tw)
                got = None
                for p in range(n):
                    at = pl.ds(p * deep, deep)
                    lhs = jnp.concatenate([gm[2 * b, :, at], gm[2 * b + 1, :, at]], axis=0)
                    term = dot(lhs, vo[p, cols, :], NT)
                    got = term if got is None else got + term
                low = got.astype(BF)
                dmix[2 * b, :, cols] = low[:R]
                dmix[2 * b + 1, :, cols] = low[R:]

            tiles(wide // tw, body)

        mixed(0)
        mixed(1)
        tw = min(256, wide)
        for k in send_order + [0]:
            at = pl.ds(pl.multiple_of((z ^ k) * deep, deep), deep)

            def out_body(j):
                cols = rows_of(j, tw)
                lhs = mix[:, :, cols].reshape(4 * R, tw)
                go[k, cols, :] = dot(lhs, gm[:, :, at].reshape(4 * R, deep), TN).astype(BF)

            tiles(wide // tw, out_body)
            if at_once(k):
                att_start(k, 3)

        def head(i):
            s, h = i // heads, lax.rem(i, heads)
            pos = rows_of(s, rows)

            def part_of(ref, c):
                cols = pl.ds(pl.multiple_of(c * wide + h * size, size), size)
                return jnp.concatenate([ref[j, pos, cols] for j in range(4)], axis=0)

            q, k, v, dm = part_of(qkv, 0), part_of(qkv, 1), part_of(qkv, 2), part_of(dmix, 0)
            scores = masked_scores(dot(q, k, NT), slopes[h], prefix[s], t, rows, size)
            expon = jnp.exp(scores - jnp.max(scores, axis=-1, keepdims=True))
            probs = expon / jnp.sum(expon, axis=-1, keepdims=True)
            dp = dot(dm, v, NT)
            inner = jnp.sum(probs * dp, axis=-1, keepdims=True)
            raw = (probs * (dp - inner) * np.float32(size ** (-0.5))).astype(BF)
            for c, got in enumerate((dot(raw, k), dot(raw, q, TN), dot(probs.astype(BF), dm, TN))):
                low = got.astype(BF)
                cols = pl.ds(pl.multiple_of(c * wide + h * size, size), size)
                proj[0:1, cols] += jnp.sum(low.astype(F32), axis=0, keepdims=True)
                for j in range(4):
                    dqkv[j, pos, cols] = low[j * rows : (j + 1) * rows]

        tiles(seqs * heads, head)

        def normed(blocks, put):
            td = min(256, D)

            def body(j):
                cols = rows_of(j, td)
                got = None
                for c in range(3):
                    lhs = jnp.concatenate([dqkv[b, :, c * wide : (c + 1) * wide] for b in blocks], axis=0)
                    term = dot(lhs, vq[c, cols, :], NT)
                    got = term if got is None else got + term
                put(cols, got)

            tiles(D // td, body)

        def put_send(cols, got):
            s1[0, :, cols] = got[:R].astype(BF)
            s1[1, :, cols] = got[R:].astype(BF)

        def put_part(cols, got):
            part[0, :, cols] = got[:R]
            part[1, :, cols] = got[R:]

        def normed_all():
            normed((3, 1), put_send)
            to_core.start()
            normed((2, 0), put_part)
            to_core.wait_recv()

            def add_chip(i):
                sl = rows_of(i, tile)
                sy[sl, :] = (part[0, sl, :] + r1[0, sl, :].astype(F32)).astype(BF)

            tiles(R // tile, add_chip)
            to_chip.start()

        def grads_q():
            for k in send_order + [0]:
                at = pl.ds(pl.multiple_of((z ^ k) * deep, deep), deep)
                for c in range(3):
                    def body(j):
                        cols = rows_of(j, tw)
                        rhs = dqkv[:, :, pl.ds(pl.multiple_of(c * wide + j * tw, tw), tw)].reshape(4 * R, tw)
                        gq[k, c, :, cols] = dot(nb[:, :, at].reshape(4 * R, deep), rhs, TN).astype(BF)

                    tiles(wide // tw, body)
                    if at_once(k):
                        att_start(k, c)

        @pl.when(sect == 0)
        def _():
            grads_q()
            normed_all()

        @pl.when(sect == 1)
        def _():
            normed_all()
            grads_q()

    pl.run_scoped(
        attention,
        pltpu.VMEM((3, D, wide), BF), pltpu.VMEM((n, wide, deep), BF), pltpu.VMEM((4, R, D), BF),
        pltpu.VMEM((4, R, 3 * wide), BF), pltpu.VMEM((4, R, wide), BF), pltpu.VMEM((4, R, wide), BF),
        pltpu.VMEM((4, R, 3 * wide), BF),
    )
    to_chip.wait_recv()
    to_core.wait_send()

    def low_body(j):
        sl = rows_of(j, tile)
        dy = part[1, sl, :] + r1[1, sl, :].astype(F32) + ry[sl, :].astype(F32)
        back, unit = norm_back(hid[sl, :].astype(F32), vec[0:1, :], dy)
        total = dmid[sl, :] + back
        dmid[sl, :] = total
        s1[0, sl, :] = total.astype(BF)
        col_sum(0, dy * unit)
        col_sum(2, dy)

    for h in range(2):
        half_tiles(R // tile, h, low_body)

        @pl.when(sect == 1)
        def _():
            over(h).start()

    outs = []

    def put(src, dst):
        copy = pltpu.make_async_copy(src, dst, out_sem.at[len(outs)])
        copy.start()
        outs.append(copy)

    put(dmid, dh_out)

    lane = D // (4 * n)
    for j in range(D // 128):
        panel[j] = sums[:, j * 128 : (j + 1) * 128]
    for h in range(heads):
        for c in range(2):
            at = 2 * c * wide + h * size
            low[c * heads + h : c * heads + h + 1, :] = proj[0:1, at : at + size]
    count = half // 128
    for j in range(count):
        row = ups[0:1, j * 128 : (j + 1) * 128]
        at = 2 * heads + j
        low[at : at + 1, :] = jnp.where(zl == 0, row, 0.0)
        low[at + count : at + count + 1, :] = jnp.where(zl == 1, row, 0.0)
    me = z * 4 + t
    share = []
    for k in range(1, 4 * n):
        to = peers_of(n)[k - 1]
        share.append(
            remote(panel.at[((me ^ k) * lane) // 128], notes.at[k], note_s.at[k], note_r.at[k], to))
        if k % 4 == 0:
            share.append(remote(low, lows.at[k // 4], low_s.at[k // 4], low_r.at[k // 4], to))
    for copy in share:
        copy.start()

    for k in send_order:
        if low_bit(k) == 1:
            continue
        for child in send_order:
            if child ^ low_bit(child) != k:
                continue
            for c in range(4):
                att(child, c).wait_recv()
                src = rq.at[child - 1, c] if c < 3 else ro.at[child - 1]
                dst = tmpq if c < 3 else tmpo
                copy = pltpu.make_async_copy(src, dst, load_sem.at[7])
                copy.start()
                copy.wait()
                if c < 3:
                    gq[k, c] = (gq[k, c].astype(F32) + tmpq[...].astype(F32)).astype(BF)
                else:
                    go[k] = (go[k].astype(F32) + tmpo[...].astype(F32)).astype(BF)
                if child == [j for j in send_order if j ^ low_bit(j) == k][-1]:
                    att_start(k, c)

    for c in range(4):
        att_start(1, c)

    @pl.when(sect == 1)
    def _():
        relay(0)
        for k in att_order:
            for c in ATT_RELAYED:
                att_lend(k, c).wait_recv()
                att_relay(k, c).start()

    for copy in share:
        copy.wait_recv()
    total = panel[(me * lane) // 128]
    for k in range(1, 4 * n):
        total = total + notes[k]
    sums_v[...] = total
    total = low[...]
    for k in range(1, n):
        total = total + lows[k]
    low_v[...] = total
    put(sums_v, sums_out)
    put(low_v, low_out)

    def final_feed(bu, bd, fu, fd):
        for a in range(2):
            for k in range(n - 1, 0, -1):
                ffn(a, k).wait_recv()
        loads = [load(ru, bu, 2), load(rd, bd, 3)]
        for copy in loads:
            copy.wait()
        step = min(64, deep)

        def up_body(j):
            sl = rows_of(j, step)
            same = gu[0, sl, :].astype(F32)
            other = bu[0, sl, :].astype(F32)
            for k in range(2, n):
                if k % 2 == 0:
                    same = same + bu[k - 1, sl, :].astype(F32)
                else:
                    other = other + bu[k - 1, sl, :].astype(F32)
            fu[0, sl, :] = same
            fu[1, sl, :] = other

        tiles(deep // step, up_body)

        def down_body(j):
            sl = rows_of(j, step)
            same = gd[0, sl, :].astype(F32)
            other = bd[0, sl, :].astype(F32)
            for k in range(2, n):
                if k % 2 == 0:
                    same = same + bd[k - 1, sl, :].astype(F32)
                else:
                    other = other + bd[k - 1, sl, :].astype(F32)
            fd[0, sl, :] = same
            fd[1, sl, :] = other

        tiles(half // step, down_body)
        copies = []
        for b in range(2):
            at = pl.ds(pl.multiple_of((zl ^ b) * half, half), half)
            copies.append(pltpu.make_async_copy(fu.at[b], gu_out.at[:, at], load_sem.at[2 + 2 * b]))
            copies.append(pltpu.make_async_copy(fd.at[b], gd_out.at[at, :], load_sem.at[3 + 2 * b]))
        for copy in copies:
            copy.start()
        for copy in copies:
            copy.wait()

    pl.run_scoped(
        final_feed,
        pltpu.VMEM((n - 1, deep, half), BF), pltpu.VMEM((n - 1, half, deep), BF),
        pltpu.VMEM((2, deep, half), F32), pltpu.VMEM((2, half, deep), F32),
    )

    def final_attention(bq, bo, fq, fo):
        last = [k for k in send_order if k == low_bit(k)]
        for k in last:
            for c in range(4):
                att(k, c).wait_recv()
        loads = [load(rq, bq, 2), load(ro, bo, 3)]
        for copy in loads:
            copy.wait()
        step = min(64, deep)

        def q_body(j):
            sl = rows_of(j, step)
            for c in range(3):
                total = gq[0, c, sl, :].astype(F32)
                for k in last:
                    total = total + bq[k - 1, c, sl, :].astype(F32)
                fq[c, sl, :] = total

        tiles(deep // step, q_body)

        def o_body(j):
            sl = rows_of(j, step)
            total = go[0, sl, :].astype(F32)
            for k in last:
                total = total + bo[k - 1, sl, :].astype(F32)
            fo[sl, :] = total

        tiles(wide // step, o_body)
        copies = [
            pltpu.make_async_copy(fq, gq_out, load_sem.at[2]),
            pltpu.make_async_copy(fo, go_out, load_sem.at[3]),
        ]
        for copy in copies:
            copy.start()
        for copy in copies:
            copy.wait()

    pl.run_scoped(
        final_attention,
        pltpu.VMEM((n - 1, 3, deep, wide), BF), pltpu.VMEM((n - 1, wide, deep), BF),
        pltpu.VMEM((3, deep, wide), F32), pltpu.VMEM((wide, deep), F32),
    )

    for i in range(4):
        @pl.when(sect == 0)
        def _():
            if i in (1, 2):
                ag8(i, 0).wait_send()
                ag8(i, 1).wait_send()
                corner8(i - 1).wait_send()
            forward8(i).wait_send()

        if i:
            rs8(i).wait_send()
        core8(i).wait_send()
    for i in range(6):
        ag(i // 2, i % 2).wait_send()
    to_chip.wait_send()
    for layer in range(2):
        @pl.when(sect == layer)
        def _():
            for k in range(1, n):
                ffn(0, k).wait_send()
                (lend if k in GRADS_RELAYED[layer] else direct)(k).wait_send()
            for k in GRADS_RELAYED[1 - layer]:
                ffn(1, k).wait_send()

    for k in range(1, n):
        for c in range(4):
            if c not in ATT_RELAYED:
                att(k, c).wait_send()
                continue

            @pl.when(sect == 0)
            def _():
                att_lend(k, c).wait_send()

            @pl.when(sect == 1)
            def _():
                att(k, c).wait_send()
                att_relay(k, c).wait_send()


    @pl.when(sect == 1)
    def _():
        over(0).wait_send()
        over(1).wait_send()

    for copy in share:
        copy.wait_send()
    for copy in outs:
        copy.wait()


def run_backward(dims, top, vec, prefix, slopes, weights, kept):
    n, seqs, heads, size, rows, deep, half = dims
    R, wide, D = seqs * rows, heads * size, n * deep
    V = lambda shape, dtype: pltpu.VMEM(shape, dtype)
    S = lambda *shape: jax.ShapeDtypeStruct(shape[:-1], shape[-1])
    any_ = pl.BlockSpec(memory_space=pl.ANY)
    vm = pl.BlockSpec(memory_space=pltpu.VMEM)
    sm = pl.BlockSpec(memory_space=pltpu.SMEM)
    dma = lambda k: pltpu.SemaphoreType.DMA((k,))
    outs = (
        S(R, D, F32), S(3, deep, wide, F32), S(wide, deep, F32), S(deep, 2 * half, F32), S(2 * half, deep, F32),
        S(8, 128, F32), S(24, 128, F32),
        S(n - 1, deep, half, BF), S(n - 1, half, deep, BF), S(n - 1, 3, deep, wide, BF), S(n - 1, wide, deep, BF),
        S(n - 1, half, deep, BF), S(n - 1, 3, deep, wide, BF),
    )
    scratch = [
        V((R, D), BF), V((R, D), BF), V((R, D), F32), V((R, D), BF), V((R, D), F32),
        V((8, R, D), BF), V((4, R, D), BF),
        V((n, deep, half), BF), V((n, half, deep), BF), V((n, 3, deep, wide), BF), V((n, wide, deep), BF),
        V((2, R, D), F32), V((R, D), F32), V((4, R, D), BF), V((4, R, D), BF), V((3, R, D), BF), V((3, R, D), BF),
        V((2, R, D), BF), V((2, R, D), BF), V((R, D), BF), V((R, D), BF),
        V((8, D), F32), V((1, 3 * wide), F32), V((1, half), F32), V((deep, wide), BF), V((wide, deep), BF),
        V((D // 128, 8, 128), F32), V((24, 128), F32), V((4 * n, 8, 128), F32), V((n, 24, 128), F32),
        V((8, 128), F32), V((24, 128), F32), dma(4 * n), dma(4 * n), dma(n), dma(n),
        dma(8), dma(4), dma(4), dma(2), dma(2),
        dma(8), dma(8), dma(4), dma(4), dma(4), dma(4), dma(4), dma(4),
        dma(6), dma(6), dma(2), dma(2), dma(2 * (n - 1)), dma(2 * (n - 1)), dma(4 * (n - 1)), dma(4 * (n - 1)), dma(n - 1), dma(n - 1),
        dma(4 * (n - 1)), dma(4 * (n - 1)), dma(4 * (n - 1)), dma(2), dma(2),
    ]
    return pl.pallas_call(
        functools.partial(backward_kernel, dims),
        out_shape=outs,
        in_specs=[vm, vm, sm, sm] + [any_] * 13,
        out_specs=(any_,) * len(outs),
        scratch_shapes=scratch,
        compiler_params=pltpu.CompilerParams(
            collective_id=1, has_side_effects=True, vmem_limit_bytes=62 * 1024 * 1024
        ),
    )(top, vec, prefix, slopes, *weights, *kept)


def on_device(activations, ln_gains, biases, w_qkv, qv_bias, w_out, w_up, up_bias, w_down, prefix):
    is_first = lax.axis_index("section") == 0
    plane = lax.axis_index("dp")
    place = lax.axis_index("tensor")
    planes = lax.axis_size("dp")
    tensors = lax.axis_size("tensor")
    seqs, rows, width = activations.shape[1:]
    heads, part = qv_bias.shape[2:]
    size = part * planes
    deep = w_qkv.shape[1]
    units = w_up.shape[2]
    lane = width // (planes * tensors)
    own = activations[0].reshape(seqs * rows, width)
    spot = (plane * tensors + place) * lane % 128

    def placed(block, start):
        length = block.shape[1]
        wide_block = jnp.tile(block.astype(F32), (1, 128 // length))
        lanes = jnp.arange(128)
        return jnp.where((lanes >= start) & (lanes < start + length), wide_block, 0.0)

    features = placed(jnp.concatenate([ln_gains[0], biases[0]]), spot)
    note = jnp.concatenate([
        features, jnp.zeros((2, 128), F32), placed(qv_bias[0].reshape(2 * heads, part), plane * part),
        placed(up_bias[0], plane * part),
    ])
    head_ids = place * heads + jnp.arange(heads)
    slopes = jnp.exp2(-8.0 * (head_ids.astype(F32) + 1.0) / (heads * tensors))
    dims = (planes, seqs, heads, size, rows, deep, units // 2)
    got = run_forward(
        dims, own, note, prefix, slopes, w_qkv[0].transpose(1, 0, 2), w_out[0], w_up[0], w_down[0]
    )
    output, weights, kept, vec = got[0], got[1:5], got[5:14], got[15]
    back = run_backward(dims, own, vec, prefix, slopes, weights, kept)
    grad_low, grad_q, grad_o, grad_u, grad_d, sums, low = back[:7]
    sums = lax.dynamic_slice_in_dim(sums, spot, lane, 1)
    low = lax.dynamic_slice_in_dim(low, plane * part, part, 1)
    ends = jnp.where(is_first, grad_low, output).reshape(seqs, rows, width)
    return (
        ends[None],
        sums[None, 0:2],
        sums[None, 2:6],
        grad_q.transpose(1, 0, 2)[None],
        low[: 2 * heads].reshape(1, 2, heads, part),
        grad_o[None],
        grad_u[None],
        low[2 * heads :][None],
        grad_d[None],
    )


def solution(mesh):
    in_specs = (
        P("section", "dp", "tensor", None),
        P("section", None, ("dp", "tensor")),
        P("section", None, ("dp", "tensor")),
        P("section", "dp", None, "tensor"),
        P("section", None, "tensor", "dp"),
        P("section", "tensor", "dp"),
        P("section", "dp", "tensor"),
        P("section", "tensor", "dp"),
        P("section", "tensor", "dp"),
        P("dp"),
    )
    out_specs = (
        P("section", "dp", "tensor", None),
        P("section", None, ("dp", "tensor")),
        P("section", None, ("dp", "tensor")),
        P("section", "dp", None, "tensor"),
        P("section", None, "tensor", "dp"),
        P("section", "tensor", "dp"),
        P("section", "dp", "tensor"),
        P("section", "tensor", "dp"),
        P("section", "tensor", "dp"),
    )
    return jax.shard_map(
        on_device, mesh=mesh, in_specs=in_specs, out_specs=out_specs, check_vma=False
    )
```

```python
import functools

import jax
import jax.numpy as jnp
import numpy as np
from jax import lax
from jax.experimental import pallas as pl
from jax.experimental.pallas import tpu as pltpu
from jax.sharding import PartitionSpec as P

BF = jnp.bfloat16
F32 = jnp.float32


MESH = pl.DeviceIdType.MESH
EARLY = True
RELAYED = ((3,), ())
GRADS_RELAYED = ((), (3, 2))
ATT_RELAYED = (0, 1, 2)
NT = (((1,), (1,)), ((), ()))
TN = (((0,), (0,)), ((), ()))


def dot(a, b, dims=(((1,), (0,)), ((), ()))):
    return lax.dot_general(a, b, dims, preferred_element_type=F32)


def remote(src, dst, send_sem, recv_sem, device):
    return pltpu.make_async_remote_copy(
        src_ref=src, dst_ref=dst, send_sem=send_sem, recv_sem=recv_sem, device_id=device, device_id_type=MESH
    )


def when(condition):
    return True if condition is True else condition


def greet(devices):
    barrier = pltpu.get_barrier_semaphore()
    for device in devices:
        pl.semaphore_signal(barrier, inc=1, device_id=device, device_id_type=MESH)
    pl.semaphore_wait(barrier, len(devices))


def tiles(count, body):
    def step(i, carry):
        body(i)
        return carry

    lax.fori_loop(0, count, step, 0)


def half_tiles(count, part, body):
    tiles(count // 2, lambda i: body(i + part * (count // 2)))


def rows_of(i, size):
    return pl.ds(pl.multiple_of(i * size, size), size)


def norm_rows(value, gain, shift_vec):
    centre = value - jnp.mean(value, axis=-1, keepdims=True)
    spread = jnp.mean(centre * centre, axis=-1, keepdims=True)
    return centre * lax.rsqrt(spread + 1e-05) * gain + shift_vec


def spots(base, shape, dim, rows):
    index = lax.broadcasted_iota(jnp.int32, shape, dim)
    return ((index // rows) ^ base) * rows + lax.rem(index, rows)


def gelu_parts(v):
    cube = v * v * v
    inner = np.float32(np.sqrt(2 / np.pi)) * (v + 0.044715 * cube)
    return jnp.tanh(inner)


def masked_scores(raw, slope, length, place, rows, size):
    gap = spots(place, raw.shape, 0, rows) - spots(place, raw.shape, 1, rows)
    open_ = (gap >= 0) | (spots(place, raw.shape, 1, rows) < length)
    scores = raw * np.float32(size ** (-0.5)) - slope * gap.astype(F32)
    return jnp.where(open_, scores, -1e30)


def relayed(layer):
    return [k for k in RELAYED[layer]]


def peers_of(n):
    sect, z, t = lax.axis_index("section"), lax.axis_index("dp"), lax.axis_index("tensor")
    return [(sect, z ^ (k // 4), t ^ (k % 4)) for k in range(1, 4 * n)]


def note_copy(n, k, src, dst, send_sem, recv_sem):
    return remote(src, dst.at[k], send_sem.at[k], recv_sem.at[k], peers_of(n)[k - 1])


def forward_kernel(
    dims, x_in, note, prefix, slopes, wq_in, wo_in, wu_in, wd_in,
    out, wq, wo, wu, wd, x_out, mid_out, nb_out, qkv_out, mix_out, sec_out, up_out, act_out, top_out, lent, vec_out,
    notes, panel, vec, qvb, upb, note_s, note_r,
    carry, carry_send, hid, mid, nb, qkv, mix, sec, up, act, outv,
    vq, vo, vu, vd, s1, r1, part, sy, ry, part8, sc, rc, s8, r8,
    line_s, line_r, pair_s, pair_r, own_sem, load_sem, keep_sem, carry_s, carry_r,
    ag_s, ag_r, rs_s, rs_r, ag8_s, ag8_r, f8_s, f8_r, c8_s, c8_r, rs8_s, rs8_r,
    top_s, top_r, near_s, near_r, lent_s, lent_r, direct_s, cor_s, cor_r,
):
    n, seqs, heads, size, rows, deep, half = dims
    R = seqs * rows
    wide = heads * size
    D = n * deep
    sect, z, t = lax.axis_index("section"), lax.axis_index("dp"), lax.axis_index("tensor")
    me = (sect, z, t)
    core = (sect, z, t ^ 1)
    chip = (sect, z, t ^ 2)
    plane = (sect, z ^ 1, t)
    diag = (sect, z ^ 1, t ^ 2)
    across = (1 - sect, z, t)
    greet(peers_of(n) + [(1 - sect, z ^ k, t) for k in range(n)])
    share = [note_copy(n, k, note, notes, note_s, note_r) for k in range(1, 4 * n)]
    for copy in share:
        copy.start()

    def lend(b):
        at = pl.ds(pl.multiple_of(((z & 1) ^ b) * half, half), half)
        return remote(wd_in.at[at], lent.at[at], lent_s.at[b], lent_r.at[b], across)

    def on_layer(layer, body):
        pl.when(sect == layer)(body)

    def lends(layer):
        return [b for b in range(2) if any(k & 1 == b for k in relayed(layer))]

    for layer in range(2):
        def body():
            for b in lends(layer):
                lend(b).start()

        on_layer(layer, body)

    zl = z & 1
    mine = [
        pltpu.make_async_copy(wq_in, wq.at[:, pl.ds(pl.multiple_of(z * deep, deep), deep)], own_sem.at[0]),
        pltpu.make_async_copy(wo_in, wo.at[z], own_sem.at[1]),
        pltpu.make_async_copy(
            wu_in.at[:, pl.ds(pl.multiple_of(zl * half, half), half)],
            wu.at[pl.ds(pl.multiple_of(z * deep, deep), deep)], own_sem.at[2]),
        pltpu.make_async_copy(
            wd_in.at[pl.ds(pl.multiple_of(zl * half, half), half)], wd.at[z], own_sem.at[3]),
    ]

    def slot(a, b):
        if a == 0:
            return wq.at[:, pl.ds(pl.multiple_of(b * deep, deep), deep)]
        return wo.at[b]

    def line(a, side, step, b):
        to = (sect, z + 1 - 2 * side, t)
        src = (wq_in, wo_in)[a] if step == 1 else slot(a, b)
        i = (a * 2 + side) * (n - 1) + step - 1
        return remote(src, slot(a, b), line_s.at[i], line_r.at[i], to)

    def line_send(a, side, step):
        b = z - (step - 1) if side == 0 else z + (step - 1)
        ok = (b >= 0) & (z < n - 1) if side == 0 else (b <= n - 1) & (z > 0)
        return ok, lambda: line(a, side, step, b)

    def line_recv(a, side, step):
        b = z - step if side == 0 else z + step
        ok = (b >= 0) if side == 0 else (b <= n - 1)
        return ok, lambda: line(a, side, step, b)

    def pair(a, k):
        h = (z ^ k) & 1
        to = (sect if a == 0 else 1 - sect, z ^ k, t)
        i = a * (n - 1) + k - 1
        if a == 0:
            src = wu_in.at[:, pl.ds(pl.multiple_of(h * half, half), half)]
            dst = wu.at[pl.ds(pl.multiple_of(z * deep, deep), deep)]
        else:
            src = lent.at[pl.ds(pl.multiple_of(h * half, half), half)]
            dst = wd.at[z]
        return remote(src, dst, pair_s.at[i], pair_r.at[i], to)

    def pair_recv(a, k):
        i = a * (n - 1) + k - 1
        if a == 0:
            src = wu_in.at[:, pl.ds(0, half)]
            dst = wu.at[pl.ds(pl.multiple_of((z ^ k) * deep, deep), deep)]
        else:
            src = wd_in.at[pl.ds(0, half)]
            dst = wd.at[z ^ k]
        return remote(src, dst, pair_s.at[i], pair_r.at[i], (sect, z ^ k, t))

    for a in range(2):
        for side in range(2):
            ok, make = line_send(a, side, 1)

            @pl.when(ok)
            def _():
                make().start()

    for copy in mine:
        copy.start()

    def vectors():
        for copy in share:
            copy.wait_recv()
        notes[0] = note[...]
        panel[...] = jnp.zeros_like(panel)
        me = z * 4 + t
        lane = D // (4 * n)
        for k in range(4 * n):
            panel[((me ^ k) * lane) // 128] += notes[k, 0:8, :]
        for j in range(D // 128):
            vec[:, j * 128 : (j + 1) * 128] = panel[j]
        low = notes[0, 8:32, :]
        for k in range(4, 4 * n, 4):
            low = low + notes[k, 8:32, :]
        qvb[...] = jnp.zeros_like(qvb)
        for h in range(heads):
            for c in range(2):
                qvb[2 * c : 2 * c + 1, h * size : (h + 1) * size] = low[c * heads + h : c * heads + h + 1, :]
        count = half // 128
        first = low[2 * heads : 2 * heads + count]
        later = low[2 * heads + count : 2 * heads + 2 * count]
        units = jnp.where(zl == 1, later, first)
        for j in range(count):
            upb[0:1, j * 128 : (j + 1) * 128] = units[j : j + 1, :]

    tile = 32

    def part_of_rows(h, size=R):
        return pl.ds(h * (size // 2), size // 2)

    def first_norm(h):
        def body(i):
            sl = rows_of(i, tile)
            v = hid[sl, :].astype(F32)
            nb[0, sl, :] = norm_rows(v, vec[0:1, :], vec[2:3, :]).astype(BF)

        half_tiles(R // tile, h, body)
        ag(1, h).start()
        ag(0, h).start()

    def ag(i, h):
        src, to = ((0, core), (0, chip), (2, core))[i]
        dst = (1, 2, 3)[i]
        at = part_of_rows(h)
        return remote(nb.at[src, at], nb.at[dst, at], ag_s.at[2 * i + h], ag_r.at[2 * i + h], to)

    def over(h):
        at = part_of_rows(h)
        return remote(carry_send.at[at], carry.at[at], carry_s.at[h], carry_r.at[h], across)

    def pass_on():
        for h in range(2):
            ag(1, h).wait_recv()
            ag(2, h).start()

    vectors()

    @pl.when(sect == 0)
    def _():
        hid[...] = x_in[...]
        first_norm(0)
        first_norm(1)
        pass_on()

    def direct(k):
        i = n - 1 + k - 1
        src = wd_in.at[pl.ds(pl.multiple_of(((z ^ k) & 1) * half, half), half)]
        return remote(src, wd.at[z], direct_s.at[k - 1], pair_r.at[i], (sect, z ^ k, t))

    def relay(layer):
        for b in lends(layer):
            lend(b).wait_recv()
        for k in relayed(layer):
            pair(1, k).start()

    def top(i):
        return remote(x_in, top_out.at[i], top_s.at[i], top_r.at[i], (core, chip, plane, diag)[i])

    def top_near(i):
        return remote(top_out.at[i], top_out.at[4 + i], near_s.at[i], near_r.at[i], core)

    top_own = pltpu.make_async_copy(x_in, top_out.at[0], own_sem.at[4])
    top_land = [remote(x_in, top_out.at[4], top_s.at[0], top_r.at[0], core)]

    @pl.when(sect == 1)
    def _():
        relay(0)

    for step in range(1, n):
        for a in range(2):
            for side in range(2):
                ok, make = line_recv(a, side, step)

                @pl.when(ok)
                def _():
                    make().wait_recv()

                if step < n - 1:
                    ok, make = line_send(a, side, step + 1)

                    @pl.when(ok)
                    def _():
                        make().start()

        if step == n - 2 or n == 2:
            for k in range(n - 1, 0, -1):
                pair(0, k).start()

    for layer in range(2):
        def body():
            for k in range(n - 1, 0, -1):
                if k not in relayed(layer):
                    direct(k).start()

        on_layer(layer, body)

    for copy in mine:
        copy.wait()
    load_q = pltpu.make_async_copy(wq, vq, load_sem.at[0])
    load_o = pltpu.make_async_copy(wo, vo, load_sem.at[1])
    load_q.start()
    load_o.start()

    @pl.when(sect == 1)
    def _():
        top_own.start()
        for i in (1, 2, 3):
            top(i).start()
        top_land[0].start()
        for h in range(2):
            over(h).wait_recv()
            hid[part_of_rows(h), :] = carry[part_of_rows(h), :]
            first_norm(h)

    load_q.wait()
    load_o.wait()
    ag(0, 0).wait_recv()
    ag(0, 1).wait_recv()
    keeps = []

    def keep(src, dst):
        copy = pltpu.make_async_copy(src, dst, keep_sem.at[len(keeps)])
        copy.start()
        keeps.append(copy)

    keep(hid, x_out)
    keep(vec, vec_out)

    tn = min(256, wide)

    def project_in(b):
        for c in range(3):
            def body(j):
                cols = rows_of(j, tn)
                lhs = jnp.concatenate([nb[2 * b], nb[2 * b + 1]], axis=0)
                got = dot(lhs, vq[c, :, cols]) + qvb[c : c + 1, cols]
                got = got.astype(BF)
                qkv[2 * b, :, pl.ds(pl.multiple_of(c * wide + j * tn, tn), tn)] = got[:R]
                qkv[2 * b + 1, :, pl.ds(pl.multiple_of(c * wide + j * tn, tn), tn)] = got[R:]

            tiles(wide // tn, body)

    project_in(0)

    @pl.when(sect == 1)
    def _():
        pass_on()

    ag(2, 0).wait_recv()
    ag(2, 1).wait_recv()
    project_in(1)
    keep(nb, nb_out)
    keep(qkv, qkv_out)

    def head(i):
        s = i // (heads // 2)
        both = [2 * lax.rem(i, heads // 2) + b for b in range(2)]
        pos = rows_of(s, rows)

        def part_of(c, h):
            cols = pl.ds(pl.multiple_of(c * wide + h * size, size), size)
            return jnp.concatenate([qkv[j, pos, cols] for j in range(4)], axis=0)

        raw = [dot(part_of(0, h), part_of(1, h), NT) for h in both]
        scores = [masked_scores(raw[b], slopes[both[b]], prefix[s], t, rows, size) for b in range(2)]
        expon = [jnp.exp(v - jnp.max(v, axis=-1, keepdims=True)) for v in scores]
        probs = [(v / jnp.sum(v, axis=-1, keepdims=True)).astype(BF) for v in expon]
        got = [dot(probs[b], part_of(2, both[b])).astype(BF) for b in range(2)]
        for b in range(2):
            for j in range(4):
                mix[j, pos, rows_of(both[b], size)] = got[b][j * rows : (j + 1) * rows]

    tiles(seqs * heads // 2, head)
    keep(mix, mix_out)

    def columns(c):
        return pl.ds(c * (D // 2), D // 2)

    def project(lhs_blocks, put, c):

        def body(i):
            lhs = jnp.concatenate([mix[lhs_blocks[0]], mix[lhs_blocks[1]]], axis=0)
            got = dot(lhs, vo[i])
            put(rows_of(i, deep), got)

        half_tiles(n, c, body)

    def put_send(cols, got):
        s1[0, :, cols] = got[:R].astype(BF)
        s1[1, :, cols] = got[R:].astype(BF)

    def put_part(cols, got):
        part[0, :, cols] = got[:R]
        part[1, :, cols] = got[R:]

    def to_core(c):
        at = columns(c)
        return remote(s1.at[:, :, at], r1.at[:, :, at], rs_s.at[c], rs_r.at[c], core)

    def to_chip(c):
        at = columns(c)
        return remote(sy.at[:, at], ry.at[:, at], rs_s.at[2 + c], rs_r.at[2 + c], chip)

    def add_chip(c):
        to_core(c).wait_recv()

        def body(i):
            sl = rows_of(i, tile)
            at = columns(c)
            sy[sl, at] = (part[0, sl, at] + r1[0, sl, at].astype(F32)).astype(BF)

        tiles(R // tile, body)
        to_chip(c).start()

    project((3, 1), put_send, 0)
    to_core(0).start()
    project((2, 0), put_part, 0)
    project((3, 1), put_send, 1)
    to_core(1).start()
    add_chip(0)
    project((2, 0), put_part, 1)
    add_chip(1)
    to_chip(0).wait_recv()
    to_chip(1).wait_recv()

    def middle_body(i):
        sl = rows_of(i, tile)
        v = hid[sl, :].astype(F32) + part[1, sl, :] + r1[1, sl, :].astype(F32)
        v = v + ry[sl, :].astype(F32) + vec[4:5, :]
        mid[sl, :] = v
        sec[0, sl, :] = norm_rows(v, vec[1:2, :], vec[3:4, :]).astype(BF)


    targets = (None, chip, plane, diag)

    def ag8(i, h):
        at = part_of_rows(h)
        return remote(sec.at[0, at], sec.at[i, at], ag8_s.at[2 * i + h], ag8_r.at[2 * i + h], targets[i])

    def corner8(i):
        at = pl.ds(i * (R // 2), R // 2)
        return remote(sec.at[2 - i, at], sec.at[3, at], cor_s.at[i], cor_r.at[i], (chip, plane)[i])

    def forward8(i):
        return remote(sec.at[i], sec.at[4 + i], f8_s.at[i], f8_r.at[i], core)

    def core8(i):
        return remote(sc.at[i], rc.at[i], c8_s.at[i], c8_r.at[i], core)

    def rs8(i):
        return remote(s8.at[i], r8.at[i], rs8_s.at[i], rs8_r.at[i], targets[i])

    order = (0, 2, 1, 3)
    for h in range(2):
        half_tiles(R // tile, h, middle_body)
        for i in order[1:3]:
            ag8(i, h).start()
    forward8(0).start()
    keep(mid, mid_out)

    def arrive():
        ag8(2, 0).wait_recv()
        corner8(0).start()
        ag8(2, 1).wait_recv()
        forward8(2).start()
        ag8(1, 0).wait_recv()
        ag8(1, 1).wait_recv()
        corner8(1).start()
        forward8(1).start()

    def arrive_corner():
        corner8(0).wait_recv()
        corner8(1).wait_recv()
        forward8(3).start()

    load_u = pltpu.make_async_copy(wu, vu, load_sem.at[2])
    load_d = pltpu.make_async_copy(wd, vd, load_sem.at[3])

    def weights_in(a):
        for k in range(n - 1, 0, -1):
            pair_recv(a, k).wait_recv()
        (load_u, load_d)[a].start()

    tu = min(256, half)

    def up_part(i):
        def up_body(j):
            cols = rows_of(j, tu)
            lhs = jnp.concatenate([sec[i], sec[4 + i]], axis=0)
            v = dot(lhs, vu[:, cols]) + upb[:, cols]
            g = (0.5 * v * (1.0 + gelu_parts(v))).astype(BF)
            up[i, :, cols] = v[:R]
            up[4 + i, :, cols] = v[R:]
            act[i, :, cols] = g[:R]
            act[4 + i, :, cols] = g[R:]

        tiles(half // tu, up_body)

    def down_part(i):
        def down_body(j):
            cols = rows_of(j, deep)
            lhs = jnp.concatenate([act[i], act[4 + i]], axis=0)
            got = dot(lhs, vd[j])
            part8[i, :, cols] = got[:R]
            sc[i, :, cols] = got[R:].astype(BF)

        tiles(n, down_body)
        core8(i).start()

    def reduce(i):
        core8(i).wait_recv()
        if i == 0:
            return

        def body(j):
            sl = rows_of(j, tile)
            s8[i, sl, :] = (part8[i, sl, :] + rc[i, sl, :].astype(F32)).astype(BF)

        tiles(R // tile, body)
        rs8(i).start()

    @pl.when(sect == 0)
    def _():
        arrive()
        arrive_corner()
        weights_in(0)
        weights_in(1)
        for i in range(4):
            forward8(i).wait_recv()
        load_u.wait()
        load_d.wait()
        for number, i in enumerate(order[::-1]):
            up_part(i)
            down_part(i)
            if number:
                reduce(order[4 - number])
        reduce(order[0])

    @pl.when(sect == 1)
    def _():
        weights_in(0)
        weights_in(1)
        load_u.wait()
        load_d.wait()
        for number, i in enumerate(order):
            if number == 1:
                arrive()
            if number == 3:
                arrive_corner()
            forward8(i).wait_recv()
            up_part(i)
            down_part(i)
            if number:
                reduce(order[number - 1])
        reduce(order[3])

    keep(sec, sec_out)
    keep(up, up_out)
    keep(act, act_out)
    for i in order[1:]:
        rs8(i).wait_recv()

    def out_body(j):
        sl = rows_of(j, tile)
        v = mid[sl, :] + part8[0, sl, :] + rc[0, sl, :].astype(F32)
        for i in (1, 2, 3):
            v = v + r8[i, sl, :].astype(F32)
        v = v + vec[5:6, :]
        outv[sl, :] = v
        carry_send[sl, :] = v.astype(BF)

    for h in range(2):
        half_tiles(R // tile, h, out_body)

        @pl.when(sect == 0)
        def _():
            over(h).start()

    @pl.when(sect == 0)
    def _():
        relay(1)

    keep(outv, out)

    for copy in share:
        copy.wait_send()
    for step in range(1, n):
        for a in range(2):
            for side in range(2):
                ok, make = line_send(a, side, step)

                @pl.when(ok)
                def _():
                    make().wait_send()

    for k in range(n - 1, 0, -1):
        pair(0, k).wait_send()
    for i in range(6):
        ag(i // 2, i % 2).wait_send()
    for c in range(2):
        to_core(c).wait_send()
        to_chip(c).wait_send()
    for i in range(4):
        if i in (1, 2):
            ag8(i, 0).wait_send()
            ag8(i, 1).wait_send()
            corner8(i - 1).wait_send()
        if i:
            rs8(i).wait_send()
        forward8(i).wait_send()
        core8(i).wait_send()

    for layer in range(2):
        def body():
            for b in lends(layer):
                lend(b).wait_send()
            for k in range(1, n):
                if k not in relayed(layer):
                    direct(k).wait_send()
            for k in relayed(1 - layer):
                pair(1, k).wait_send()

        on_layer(layer, body)

    @pl.when(sect == 0)
    def _():
        over(0).wait_send()
        over(1).wait_send()

    @pl.when(sect == 1)
    def _():
        for i in (1, 2, 3):
            top(i).wait_recv()
            top_near(i).start()
        top_land[0].wait_recv()
        for i in (1, 2, 3):
            top_near(i).wait_recv()
        top_own.wait()
        top_land[0].wait_send()
        for i in (1, 2, 3):
            top(i).wait_send()
            top_near(i).wait_send()

    for copy in keeps:
        copy.wait()


def run_forward(dims, x, note, prefix, slopes, wq, wo, wu, wd):
    n, seqs, heads, size, rows, deep, half = dims
    R, wide, D = seqs * rows, heads * size, n * deep
    V = lambda shape, dtype: pltpu.VMEM(shape, dtype)
    S = lambda *shape: jax.ShapeDtypeStruct(shape[:-1], shape[-1])
    any_ = pl.BlockSpec(memory_space=pl.ANY)
    vm = pl.BlockSpec(memory_space=pltpu.VMEM)
    sm = pl.BlockSpec(memory_space=pltpu.SMEM)
    dma = lambda k: pltpu.SemaphoreType.DMA((k,))
    outs = (
        S(R, D, F32), S(3, D, wide, BF), S(n, wide, deep, BF), S(D, half, BF), S(n, half, deep, BF),
        S(R, D, BF), S(R, D, F32), S(4, R, D, BF), S(4, R, 3 * wide, BF), S(4, R, wide, BF),
        S(8, R, D, BF), S(8, R, half, F32), S(8, R, half, BF), S(8, R, D, BF), S(2 * half, deep, BF), S(8, D, F32),
    )
    scratch = [
        V((4 * n, 32, 128), F32), V((D // 128, 8, 128), F32), V((8, D), F32), V((4, wide), F32), V((1, half), F32),
        dma(4 * n), dma(4 * n),
        V((R, D), BF), V((R, D), BF), V((R, D), BF), V((R, D), F32), V((4, R, D), BF), V((4, R, 3 * wide), BF),
        V((4, R, wide), BF), V((8, R, D), BF), V((8, R, half), F32), V((8, R, half), BF), V((R, D), F32),
        V((3, D, wide), BF), V((n, wide, deep), BF), V((D, half), BF), V((n, half, deep), BF),
        V((2, R, D), BF), V((2, R, D), BF), V((2, R, D), F32), V((R, D), BF), V((R, D), BF),
        V((4, R, D), F32), V((4, R, D), BF), V((4, R, D), BF), V((4, R, D), BF), V((4, R, D), BF),
        dma(4 * (n - 1)), dma(4 * (n - 1)), dma(2 * (n - 1)), dma(2 * (n - 1)), dma(5), dma(4), dma(10),
        dma(2), dma(2),
        dma(6), dma(6), dma(4), dma(4), dma(8), dma(8), dma(4), dma(4), dma(4), dma(4), dma(4), dma(4),
        dma(4), dma(4), dma(4), dma(4), dma(2), dma(2), dma(n - 1), dma(2), dma(2),
    ]
    return pl.pallas_call(
        functools.partial(forward_kernel, dims),
        out_shape=outs,
        in_specs=[vm, vm, sm, sm, any_, any_, any_, any_],
        out_specs=(any_,) * len(outs),
        scratch_shapes=scratch,
        compiler_params=pltpu.CompilerParams(
            collective_id=0, has_side_effects=True, vmem_limit_bytes=60 * 1024 * 1024
        ),
    )(x, note, prefix, slopes, wq, wo, wu, wd)


def backward_kernel(
    dims, top, vec, prefix, slopes, wq, wo, wu, wd, hid_in, mid_in, nb_in, qkv_in, mix_in, sec_in, up_in, act_in, top_in,
    dh_out, gq_out, go_out, gu_out, gd_out, sums_out, low_out, ru, rd, rq, ro, lent, lentq,
    carry, grad, mid, hid, dmid, gp, gm, gu, gd, gq, go, part, own8, sc, rc, s8, r8,
    s1, r1, sy, ry, sums, proj, ups, tmpq, tmpo, panel, low, notes, lows, sums_v, low_v, note_s, note_r, low_s, low_r,
    load_sem, up_sem, out_sem, carry_s, carry_r, ag8_s, ag8_r, f8_s, f8_r, c8_s, c8_r, rs8_s, rs8_r,
    ag_s, ag_r, rs_s, rs_r, ffn_s, ffn_r, att_s, att_r, lent_s, lent_r, lentq_s, lentq_r, over_s, cor_s, cor_r,
):
    n, seqs, heads, size, rows, deep, half = dims
    R = seqs * rows
    wide = heads * size
    D = n * deep
    sect, z, t = lax.axis_index("section"), lax.axis_index("dp"), lax.axis_index("tensor")
    core = (sect, z, t ^ 1)
    chip = (sect, z, t ^ 2)
    plane = (sect, z ^ 1, t)
    diag = (sect, z ^ 1, t ^ 2)
    across = (1 - sect, z, t)
    greet(peers_of(n) + [(1 - sect, z ^ k, t) for k in range(n)])
    zl = z & 1
    tile = 32
    order = (0, 2, 1, 3)
    targets = (None, chip, plane, diag)

    def part_of_rows(h):
        return pl.ds(h * (R // 2), R // 2)

    def ag8(i, h):
        at = part_of_rows(h)
        return remote(gp.at[0, at], gp.at[i, at], ag8_s.at[2 * i + h], ag8_r.at[2 * i + h], targets[i])

    def corner8(i):
        at = pl.ds(i * (R // 2), R // 2)
        return remote(gp.at[2 - i, at], gp.at[3, at], cor_s.at[i], cor_r.at[i], (chip, plane)[i])

    def forward8(i):
        return remote(gp.at[i], gp.at[4 + i], f8_s.at[i], f8_r.at[i], core)

    def core8(i):
        return remote(sc.at[i], rc.at[i], c8_s.at[i], c8_r.at[i], core)

    def rs8(i):
        return remote(s8.at[i - 1], r8.at[i - 1], rs8_s.at[i], rs8_r.at[i], targets[i])

    def load(src, dst, i):
        copy = pltpu.make_async_copy(src, dst, load_sem.at[i])
        copy.start()
        return copy

    load_mid, load_hid = load(mid_in, mid, 0), load(hid_in, hid, 1)
    sums[...] = jnp.zeros_like(sums)
    proj[...] = jnp.zeros_like(proj)
    ups[...] = jnp.zeros_like(ups)

    def over(h):
        at = part_of_rows(h)
        return remote(s1.at[0, at], carry.at[at], carry_s.at[h], carry_r.at[h], across)

    def col_sum(row, value):
        sums[row : row + 1, :] += jnp.sum(value, axis=0, keepdims=True)

    def ffn(a, k):
        i = a * (n - 1) + k - 1
        to = (sect if a == 0 else 1 - sect, z ^ k, t)
        src = gu.at[k] if a == 0 else lent.at[k - 1]
        return remote(src, (ru, rd)[a].at[k - 1], ffn_s.at[i], ffn_r.at[i], to)

    def direct(k):
        return remote(gd.at[k], rd.at[k - 1], lent_s.at[k - 1], ffn_r.at[n - 1 + k - 1], (sect, z ^ k, t))

    def lend(k):
        return remote(gd.at[k], lent.at[k - 1], lent_s.at[k - 1], lent_r.at[k - 1], across)

    def ffn_start(layer, k):
        (lend if k in GRADS_RELAYED[layer] else direct)(k).start()
        ffn(0, k).start()

    def relay(layer):
        for k in GRADS_RELAYED[layer]:
            lend(k).wait_recv()
            ffn(1, k).start()

    def feed(vu, vd, sec, act, dup, upb):
        load_d = pltpu.make_async_copy(wd, vd, load_sem.at[3])
        load_u = pltpu.make_async_copy(wu, vu, load_sem.at[2])
        later = [
            pltpu.make_async_copy(sec_in, sec, load_sem.at[4]),
            pltpu.make_async_copy(act_in, act, load_sem.at[5]),
        ]

        def up_load(number, turn):
            i, slot = turn[number], number % 2
            return [
                pltpu.make_async_copy(up_in.at[i + 4 * b], upb.at[slot, b], up_sem.at[2 * slot + b])
                for b in range(2)
            ]

        load_top = pltpu.make_async_copy(top_in, gp, load_sem.at[6])
        for layer in range(2):
            @pl.when(sect == layer)
            def _():
                for number in range(2):
                    for copy in up_load(number, order[:: 1 - 2 * layer]):
                        copy.start()

        load_d.start()

        @pl.when(sect == 1)
        def _():
            load_top.start()
            load_u.start()
            grad[...] = top[...]
            load_top.wait()

        @pl.when(sect == 0)
        def _():
            load_u.start()
            relay(1)
            for h in range(2):
                over(h).wait_recv()
                value = carry[part_of_rows(h), :]
                grad[part_of_rows(h), :] = value
                gp[0, part_of_rows(h), :] = value
                for i in order[1:3]:
                    ag8(i, h).start()
            forward8(0).start()

        def bias_body(j):
            col_sum(5, grad[rows_of(j, tile), :].astype(F32))

        tiles(R // tile, bias_body)
        load_d.wait()
        tu = min(256, half)
        td = min(256, D)

        def group(number, turn, arriving):
            i, slot = turn[number], number % 2
            if arriving:
                if number == 1:
                    ag8(2, 0).wait_recv()
                    corner8(0).start()
                    ag8(2, 1).wait_recv()
                    forward8(2).start()
                    ag8(1, 0).wait_recv()
                    ag8(1, 1).wait_recv()
                    corner8(1).start()
                    forward8(1).start()
                if i == 3:
                    corner8(0).wait_recv()
                    corner8(1).wait_recv()
                    forward8(3).start()
                forward8(i).wait_recv()
            for copy in up_load(number, turn):
                copy.wait()

            def up_body(j):
                cols = rows_of(j, tu)
                got = None
                for b in range(n):
                    at = pl.ds(b * deep, deep)
                    lhs = jnp.concatenate([gp[i, :, at], gp[4 + i, :, at]], axis=0)
                    term = dot(lhs, vd[b, cols, :], NT)
                    got = term if got is None else got + term
                v = jnp.concatenate([upb[slot, 0, :, cols], upb[slot, 1, :, cols]], axis=0)
                th = gelu_parts(v)
                slope = 0.5 * (1.0 + th) + 0.5 * v * (1.0 - th * th) * np.float32(np.sqrt(2 / np.pi)) * (
                    1.0 + np.float32(3 * 0.044715) * v * v
                )
                low = (got * slope).astype(BF)
                dup[i, :, cols] = low[:R]
                dup[4 + i, :, cols] = low[R:]
                ups[0:1, cols] += jnp.sum(low.astype(F32), axis=0, keepdims=True)

            tiles(half // tu, up_body)
            if number + 2 < 4:
                for copy in up_load(number + 2, turn):
                    copy.start()

            if number == 0:
                load_u.wait()
                for copy in later:
                    copy.start()

            def second_body(j):
                cols = rows_of(j, td)
                lhs = jnp.concatenate([dup[i], dup[4 + i]], axis=0)
                got = dot(lhs, vu[cols, :], NT)
                if i == 0:
                    own8[:, cols] = got[:R]
                else:
                    part[slot, :, cols] = got[:R]
                sc[i, :, cols] = got[R:].astype(BF)

            tiles(D // td, second_body)
            core8(i).start()

        def reduce(number, turn):
            i, slot = turn[number], number % 2
            core8(i).wait_recv()
            if i == 0:
                return

            def body(j):
                sl = rows_of(j, tile)
                s8[i - 1, sl, :] = (part[slot, sl, :] + rc[i, sl, :].astype(F32)).astype(BF)

            tiles(R // tile, body)
            rs8(i).start()

        def every(turn, arriving):
            for number in range(4):
                group(number, turn, arriving)
                if number:
                    reduce(number - 1, turn)
            reduce(3, turn)

        @pl.when(sect == 0)
        def _():
            every(order, True)

        @pl.when(sect == 1)
        def _():
            every(order[::-1], False)

        for copy in later:
            copy.wait()

        th_ = min(256, half)
        for k in list(range(n - 1, 0, -1)) + [0]:
            def down_body(j):
                cols = rows_of(j, th_)
                lhs = act[:, :, cols].reshape(8 * R, th_)
                at = pl.ds(pl.multiple_of((z ^ k) * deep, deep), deep)
                gd[k, cols, :] = dot(lhs, gp[:, :, at].reshape(8 * R, deep), TN).astype(BF)

            tiles(half // th_, down_body)
            dd = min(256, deep)

            def up_body(j):
                at = pl.ds(pl.multiple_of((z ^ k) * deep + j * dd, dd), dd)
                lhs = sec[:, :, at].reshape(8 * R, dd)
                gu[k, rows_of(j, dd), :] = dot(lhs, dup[...].reshape(8 * R, half), TN).astype(BF)

            tiles(deep // dd, up_body)
            if EARLY and k:
                @pl.when(sect == 0)
                def _():
                    ffn_start(0, k)

    pl.run_scoped(
        feed,
        pltpu.VMEM((D, half), BF), pltpu.VMEM((n, half, deep), BF), pltpu.VMEM((8, R, D), BF),
        pltpu.VMEM((8, R, half), BF), pltpu.VMEM((8, R, half), BF), pltpu.VMEM((2, 2, R, half), F32),
    )
    for i in order[1:]:
        rs8(i).wait_recv()
    for layer in range(1 if EARLY else 0, 2):
        @pl.when(sect == layer)
        def _():
            for k in range(n - 1, 0, -1):
                ffn_start(layer, k)

    load_mid.wait()
    load_hid.wait()

    def norm_back(value, gain, dy):
        centre = value - jnp.mean(value, axis=-1, keepdims=True)
        spread = jnp.mean(centre * centre, axis=-1, keepdims=True)
        scale = lax.rsqrt(spread + 1e-05)
        unit = centre * scale
        scaled = dy * gain
        inner = jnp.mean(scaled * unit, axis=-1, keepdims=True)
        return (scaled - jnp.mean(scaled, axis=-1, keepdims=True) - unit * inner) * scale, unit

    def mid_body(j):
        sl = rows_of(j, tile)
        dy = own8[sl, :] + rc[0, sl, :].astype(F32)
        for i in (1, 2, 3):
            dy = dy + r8[i - 1, sl, :].astype(F32)
        back, unit = norm_back(mid[sl, :], vec[1:2, :], dy)
        total = grad[sl, :].astype(F32) + back
        dmid[sl, :] = total
        gm[0, sl, :] = total.astype(BF)
        col_sum(1, dy * unit)
        col_sum(3, dy)
        col_sum(4, total)

    def ag(i, h):
        src, to = ((0, core), (0, chip), (2, core))[i]
        dst = (1, 2, 3)[i]
        at = part_of_rows(h)
        return remote(gm.at[src, at], gm.at[dst, at], ag_s.at[2 * i + h], ag_r.at[2 * i + h], to)

    for h in range(2):
        half_tiles(R // tile, h, mid_body)
        ag(1, h).start()
        ag(0, h).start()
    def columns(c):
        return pl.ds(c * (D // 2), D // 2)

    def to_core(c):
        at = columns(c)
        return remote(s1.at[:, :, at], r1.at[:, :, at], rs_s.at[c], rs_r.at[c], core)

    def to_chip(c):
        at = columns(c)
        return remote(sy.at[:, at], ry.at[:, at], rs_s.at[2 + c], rs_r.at[2 + c], chip)

    def add_chip(c):
        to_core(c).wait_recv()

        def body(i):
            sl = rows_of(i, tile)
            at = columns(c)
            sy[sl, at] = (part[0, sl, at] + r1[0, sl, at].astype(F32)).astype(BF)

        tiles(R // tile, body)
        to_chip(c).start()


    def low_bit(k):
        return k & -k

    def att(k, c):
        i = (k - 1) * 4 + c
        src, dst = (gq.at[k, c], rq.at[k - 1, c]) if c < 3 else (go.at[k], ro.at[k - 1])
        return remote(src, dst, att_s.at[i], att_r.at[i], (sect, z ^ low_bit(k), t))

    def att_lend(k, c):
        i = (k - 1) * 4 + c
        return remote(gq.at[k, c], lentq.at[k - 1, c], lentq_s.at[i], lentq_r.at[i], across)

    def att_relay(k, c):
        i = (k - 1) * 4 + c
        to = (1 - sect, z ^ low_bit(k), t)
        return remote(lentq.at[k - 1, c], rq.at[k - 1, c], over_s.at[i], att_r.at[i], to)

    def att_start(k, c):
        if c not in ATT_RELAYED:
            att(k, c).start()
            return

        @pl.when(sect == 0)
        def _():
            att_lend(k, c).start()

        @pl.when(sect == 1)
        def _():
            att(k, c).start()

    def at_once(k):
        return k > 1 and low_bit(k) == 1

    att_order = [k for k in range(n - 1, 1, -1) if k & 1]
    att_order += sorted((k for k in range(2, n, 2)), key=lambda k: (low_bit(k), -k)) + [1]
    send_order = sorted(range(1, n), key=lambda k: (low_bit(k), -k))

    def attention(vq, vo, nb, qkv, mix, dmix, dqkv):
        loads = [load(wo, vo, 2), load(qkv_in, qkv, 3), load(mix_in, mix, 4), load(nb_in, nb, 5), load(wq, vq, 6)]
        loads[0].wait()
        ag(0, 0).wait_recv()
        ag(0, 1).wait_recv()

        def mixed(b):
            if b == 1:
                for h in range(2):
                    ag(1, h).wait_recv()
                    ag(2, h).start()
                for copy in loads[1:]:
                    copy.wait()
                ag(2, 0).wait_recv()
                ag(2, 1).wait_recv()
            tw = min(256, wide)

            def body(j):
                cols = rows_of(j, tw)
                got = None
                for p in range(n):
                    at = pl.ds(p * deep, deep)
                    lhs = jnp.concatenate([gm[2 * b, :, at], gm[2 * b + 1, :, at]], axis=0)
                    term = dot(lhs, vo[p, cols, :], NT)
                    got = term if got is None else got + term
                low = got.astype(BF)
                dmix[2 * b, :, cols] = low[:R]
                dmix[2 * b + 1, :, cols] = low[R:]

            tiles(wide // tw, body)

        mixed(0)
        mixed(1)
        tw = min(256, wide)
        for k in send_order + [0]:
            at = pl.ds(pl.multiple_of((z ^ k) * deep, deep), deep)

            def out_body(j):
                cols = rows_of(j, tw)
                lhs = mix[:, :, cols].reshape(4 * R, tw)
                go[k, cols, :] = dot(lhs, gm[:, :, at].reshape(4 * R, deep), TN).astype(BF)

            tiles(wide // tw, out_body)
            if at_once(k):
                att_start(k, 3)

        def head(i):
            s = i // (heads // 2)
            pos = rows_of(s, rows)

            def part_of(ref, c, h):
                cols = pl.ds(pl.multiple_of(c * wide + h * size, size), size)
                return jnp.concatenate([ref[j, pos, cols] for j in range(4)], axis=0)

            def one(h):
                q, k, v, dm = part_of(qkv, 0, h), part_of(qkv, 1, h), part_of(qkv, 2, h), part_of(dmix, 0, h)
                scores = masked_scores(dot(q, k, NT), slopes[h], prefix[s], t, rows, size)
                dp = dot(dm, v, NT)
                expon = jnp.exp(scores - jnp.max(scores, axis=-1, keepdims=True))
                probs = expon / jnp.sum(expon, axis=-1, keepdims=True)
                inner = jnp.sum(probs * dp, axis=-1, keepdims=True)
                raw = (probs * (dp - inner) * np.float32(size ** (-0.5))).astype(BF)
                return [g.astype(BF) for g in (dot(raw, k), dot(raw, q, TN), dot(probs.astype(BF), dm, TN))]

            both = [2 * lax.rem(i, heads // 2) + b for b in range(2)]
            results = [one(h) for h in both]
            for h, result in zip(both, results):
                for c, low in enumerate(result):
                    cols = pl.ds(pl.multiple_of(c * wide + h * size, size), size)
                    proj[0:1, cols] += jnp.sum(low.astype(F32), axis=0, keepdims=True)
                    for j in range(4):
                        dqkv[j, pos, cols] = low[j * rows : (j + 1) * rows]

        tiles(seqs * heads // 2, head)

        def normed(blocks, put, c_half):
            td = min(256, D)

            def body(j):
                cols = rows_of(j, td)
                got = None
                for c in range(3):
                    lhs = jnp.concatenate([dqkv[b, :, c * wide : (c + 1) * wide] for b in blocks], axis=0)
                    term = dot(lhs, vq[c, cols, :], NT)
                    got = term if got is None else got + term
                put(cols, got)

            half_tiles(D // td, c_half, body)

        def put_send(cols, got):
            s1[0, :, cols] = got[:R].astype(BF)
            s1[1, :, cols] = got[R:].astype(BF)

        def put_part(cols, got):
            part[0, :, cols] = got[:R]
            part[1, :, cols] = got[R:]

        def normed_all():
            normed((3, 1), put_send, 0)
            to_core(0).start()
            normed((2, 0), put_part, 0)
            normed((3, 1), put_send, 1)
            to_core(1).start()
            add_chip(0)
            normed((2, 0), put_part, 1)
            add_chip(1)

        def grads_q():
            for k in send_order + [0]:
                at = pl.ds(pl.multiple_of((z ^ k) * deep, deep), deep)
                for c in range(3):
                    def body(j):
                        cols = rows_of(j, tw)
                        rhs = dqkv[:, :, pl.ds(pl.multiple_of(c * wide + j * tw, tw), tw)].reshape(4 * R, tw)
                        gq[k, c, :, cols] = dot(nb[:, :, at].reshape(4 * R, deep), rhs, TN).astype(BF)

                    tiles(wide // tw, body)
                    if at_once(k):
                        att_start(k, c)

        @pl.when(sect == 0)
        def _():
            grads_q()
            normed_all()

        @pl.when(sect == 1)
        def _():
            normed_all()
            grads_q()

    pl.run_scoped(
        attention,
        pltpu.VMEM((3, D, wide), BF), pltpu.VMEM((n, wide, deep), BF), pltpu.VMEM((4, R, D), BF),
        pltpu.VMEM((4, R, 3 * wide), BF), pltpu.VMEM((4, R, wide), BF), pltpu.VMEM((4, R, wide), BF),
        pltpu.VMEM((4, R, 3 * wide), BF),
    )
    for c in range(2):
        to_chip(c).wait_recv()
        to_core(c).wait_send()

    def low_body(j):
        sl = rows_of(j, tile)
        dy = part[1, sl, :] + r1[1, sl, :].astype(F32) + ry[sl, :].astype(F32)
        back, unit = norm_back(hid[sl, :].astype(F32), vec[0:1, :], dy)
        total = dmid[sl, :] + back
        dmid[sl, :] = total
        s1[0, sl, :] = total.astype(BF)
        col_sum(0, dy * unit)
        col_sum(2, dy)

    for h in range(2):
        half_tiles(R // tile, h, low_body)

        @pl.when(sect == 1)
        def _():
            over(h).start()

    outs = []

    def put(src, dst):
        copy = pltpu.make_async_copy(src, dst, out_sem.at[len(outs)])
        copy.start()
        outs.append(copy)

    put(dmid, dh_out)

    lane = D // (4 * n)
    for j in range(D // 128):
        panel[j] = sums[:, j * 128 : (j + 1) * 128]
    for h in range(heads):
        for c in range(2):
            at = 2 * c * wide + h * size
            low[c * heads + h : c * heads + h + 1, :] = proj[0:1, at : at + size]
    count = half // 128
    for j in range(count):
        row = ups[0:1, j * 128 : (j + 1) * 128]
        at = 2 * heads + j
        low[at : at + 1, :] = jnp.where(zl == 0, row, 0.0)
        low[at + count : at + count + 1, :] = jnp.where(zl == 1, row, 0.0)
    me = z * 4 + t
    share = []
    for k in range(1, 4 * n):
        to = peers_of(n)[k - 1]
        share.append(
            remote(panel.at[((me ^ k) * lane) // 128], notes.at[k], note_s.at[k], note_r.at[k], to))
        if k % 4 == 0:
            share.append(remote(low, lows.at[k // 4], low_s.at[k // 4], low_r.at[k // 4], to))
    for copy in share:
        copy.start()

    for k in send_order:
        if low_bit(k) == 1:
            continue
        for child in send_order:
            if child ^ low_bit(child) != k:
                continue
            for c in range(4):
                att(child, c).wait_recv()
                src = rq.at[child - 1, c] if c < 3 else ro.at[child - 1]
                dst = tmpq if c < 3 else tmpo
                copy = pltpu.make_async_copy(src, dst, load_sem.at[7])
                copy.start()
                copy.wait()
                if c < 3:
                    gq[k, c] = (gq[k, c].astype(F32) + tmpq[...].astype(F32)).astype(BF)
                else:
                    go[k] = (go[k].astype(F32) + tmpo[...].astype(F32)).astype(BF)
                if child == [j for j in send_order if j ^ low_bit(j) == k][-1]:
                    att_start(k, c)

    for c in range(4):
        att_start(1, c)

    @pl.when(sect == 1)
    def _():
        relay(0)
        for k in att_order:
            for c in ATT_RELAYED:
                att_lend(k, c).wait_recv()
                att_relay(k, c).start()

    for copy in share:
        copy.wait_recv()
    total = panel[(me * lane) // 128]
    for k in range(1, 4 * n):
        total = total + notes[k]
    sums_v[...] = total
    total = low[...]
    for k in range(1, n):
        total = total + lows[k]
    low_v[...] = total
    put(sums_v, sums_out)
    put(low_v, low_out)

    def final_feed(bu, bd, fu, fd):
        stores = []
        turn = [1] + list(range(n - 1, 1, -1))
        for k in turn:
            for a in (1, 0):
                own, got, buf, total = ((gu, ru, bu, fu), (gd, rd, bd, fd))[a]
                ffn(a, k).wait_recv()
                copy = load(got.at[k - 1], buf.at[k - 1], 2 + a)
                copy.wait()
                b = k & 1
                same = [other for other in turn if other & 1 == b]
                step = min(64, deep)

                def body(j):
                    sl = rows_of(j, step)
                    value = buf[k - 1, sl, :].astype(F32)
                    if k != same[0]:
                        value = value + total[b, sl, :]
                    elif b == 0:
                        value = value + own[0, sl, :].astype(F32)
                    total[b, sl, :] = value

                tiles(total.shape[1] // step, body)
                if k == same[-1]:
                    at = pl.ds(pl.multiple_of((zl ^ b) * half, half), half)
                    dst = gu_out.at[:, at] if a == 0 else gd_out.at[at, :]
                    stores.append(pltpu.make_async_copy(total.at[b], dst, load_sem.at[4 + 2 * a + b]))
                    stores[-1].start()
        for copy in stores:
            copy.wait()

    pl.run_scoped(
        final_feed,
        pltpu.VMEM((n - 1, deep, half), BF), pltpu.VMEM((n - 1, half, deep), BF),
        pltpu.VMEM((2, deep, half), F32), pltpu.VMEM((2, half, deep), F32),
    )

    def final_attention(bq, bo, fq, fo):
        last = [k for k in range(1, n) if k == low_bit(k)]
        stores = []
        for k in last:
            for c in (3, 0, 1, 2):
                att(k, c).wait_recv()
                src, buf = (rq.at[k - 1, c], bq.at[k - 1, c]) if c < 3 else (ro.at[k - 1], bo.at[k - 1])
                copy = load(src, buf, 2)
                copy.wait()
                step = min(64, deep)

                def body(j):
                    sl = rows_of(j, step)
                    if c < 3:
                        first = gq[0, c, sl, :].astype(F32) if k == 1 else fq[c, sl, :]
                        fq[c, sl, :] = first + bq[k - 1, c, sl, :].astype(F32)
                    else:
                        first = go[0, sl, :].astype(F32) if k == 1 else fo[sl, :]
                        fo[sl, :] = first + bo[k - 1, sl, :].astype(F32)

                tiles((deep if c < 3 else wide) // step, body)
                if k == last[-1]:
                    src, dst = (fq.at[c], gq_out.at[c]) if c < 3 else (fo, go_out)
                    stores.append(pltpu.make_async_copy(src, dst, load_sem.at[4 + c]))
                    stores[-1].start()
        for copy in stores:
            copy.wait()

    pl.run_scoped(
        final_attention,
        pltpu.VMEM((n - 1, 3, deep, wide), BF), pltpu.VMEM((n - 1, wide, deep), BF),
        pltpu.VMEM((3, deep, wide), F32), pltpu.VMEM((wide, deep), F32),
    )

    for i in range(4):
        @pl.when(sect == 0)
        def _():
            if i in (1, 2):
                ag8(i, 0).wait_send()
                ag8(i, 1).wait_send()
                corner8(i - 1).wait_send()
            forward8(i).wait_send()

        if i:
            rs8(i).wait_send()
        core8(i).wait_send()
    for i in range(6):
        ag(i // 2, i % 2).wait_send()
    to_chip(0).wait_send()
    to_chip(1).wait_send()
    for layer in range(2):
        @pl.when(sect == layer)
        def _():
            for k in range(1, n):
                ffn(0, k).wait_send()
                (lend if k in GRADS_RELAYED[layer] else direct)(k).wait_send()
            for k in GRADS_RELAYED[1 - layer]:
                ffn(1, k).wait_send()

    for k in range(1, n):
        for c in range(4):
            if c not in ATT_RELAYED:
                att(k, c).wait_send()
                continue

            @pl.when(sect == 0)
            def _():
                att_lend(k, c).wait_send()

            @pl.when(sect == 1)
            def _():
                att(k, c).wait_send()
                att_relay(k, c).wait_send()


    @pl.when(sect == 1)
    def _():
        over(0).wait_send()
        over(1).wait_send()

    for copy in share:
        copy.wait_send()
    for copy in outs:
        copy.wait()


def run_backward(dims, top, vec, prefix, slopes, weights, kept):
    n, seqs, heads, size, rows, deep, half = dims
    R, wide, D = seqs * rows, heads * size, n * deep
    V = lambda shape, dtype: pltpu.VMEM(shape, dtype)
    S = lambda *shape: jax.ShapeDtypeStruct(shape[:-1], shape[-1])
    any_ = pl.BlockSpec(memory_space=pl.ANY)
    vm = pl.BlockSpec(memory_space=pltpu.VMEM)
    sm = pl.BlockSpec(memory_space=pltpu.SMEM)
    dma = lambda k: pltpu.SemaphoreType.DMA((k,))
    outs = (
        S(R, D, F32), S(3, deep, wide, F32), S(wide, deep, F32), S(deep, 2 * half, F32), S(2 * half, deep, F32),
        S(8, 128, F32), S(24, 128, F32),
        S(n - 1, deep, half, BF), S(n - 1, half, deep, BF), S(n - 1, 3, deep, wide, BF), S(n - 1, wide, deep, BF),
        S(n - 1, half, deep, BF), S(n - 1, 3, deep, wide, BF),
    )
    scratch = [
        V((R, D), BF), V((R, D), BF), V((R, D), F32), V((R, D), BF), V((R, D), F32),
        V((8, R, D), BF), V((4, R, D), BF),
        V((n, deep, half), BF), V((n, half, deep), BF), V((n, 3, deep, wide), BF), V((n, wide, deep), BF),
        V((2, R, D), F32), V((R, D), F32), V((4, R, D), BF), V((4, R, D), BF), V((3, R, D), BF), V((3, R, D), BF),
        V((2, R, D), BF), V((2, R, D), BF), V((R, D), BF), V((R, D), BF),
        V((8, D), F32), V((1, 3 * wide), F32), V((1, half), F32), V((deep, wide), BF), V((wide, deep), BF),
        V((D // 128, 8, 128), F32), V((24, 128), F32), V((4 * n, 8, 128), F32), V((n, 24, 128), F32),
        V((8, 128), F32), V((24, 128), F32), dma(4 * n), dma(4 * n), dma(n), dma(n),
        dma(8), dma(4), dma(4), dma(2), dma(2),
        dma(8), dma(8), dma(4), dma(4), dma(4), dma(4), dma(4), dma(4),
        dma(6), dma(6), dma(4), dma(4), dma(2 * (n - 1)), dma(2 * (n - 1)), dma(4 * (n - 1)), dma(4 * (n - 1)), dma(n - 1), dma(n - 1),
        dma(4 * (n - 1)), dma(4 * (n - 1)), dma(4 * (n - 1)), dma(2), dma(2),
    ]
    return pl.pallas_call(
        functools.partial(backward_kernel, dims),
        out_shape=outs,
        in_specs=[vm, vm, sm, sm] + [any_] * 13,
        out_specs=(any_,) * len(outs),
        scratch_shapes=scratch,
        compiler_params=pltpu.CompilerParams(
            collective_id=1, has_side_effects=True, vmem_limit_bytes=62 * 1024 * 1024
        ),
    )(top, vec, prefix, slopes, *weights, *kept)


def on_device(activations, ln_gains, biases, w_qkv, qv_bias, w_out, w_up, up_bias, w_down, prefix):
    is_first = lax.axis_index("section") == 0
    plane = lax.axis_index("dp")
    place = lax.axis_index("tensor")
    planes = lax.axis_size("dp")
    tensors = lax.axis_size("tensor")
    seqs, rows, width = activations.shape[1:]
    heads, part = qv_bias.shape[2:]
    size = part * planes
    deep = w_qkv.shape[1]
    units = w_up.shape[2]
    lane = width // (planes * tensors)
    own = activations[0].reshape(seqs * rows, width)
    spot = (plane * tensors + place) * lane % 128

    def placed(block, start):
        length = block.shape[1]
        wide_block = jnp.tile(block.astype(F32), (1, 128 // length))
        lanes = jnp.arange(128)
        return jnp.where((lanes >= start) & (lanes < start + length), wide_block, 0.0)

    features = placed(jnp.concatenate([ln_gains[0], biases[0]]), spot)
    note = jnp.concatenate([
        features, jnp.zeros((2, 128), F32), placed(qv_bias[0].reshape(2 * heads, part), plane * part),
        placed(up_bias[0], plane * part),
    ])
    head_ids = place * heads + jnp.arange(heads)
    slopes = jnp.exp2(-8.0 * (head_ids.astype(F32) + 1.0) / (heads * tensors))
    dims = (planes, seqs, heads, size, rows, deep, units // 2)
    got = run_forward(
        dims, own, note, prefix, slopes, w_qkv[0].transpose(1, 0, 2), w_out[0], w_up[0], w_down[0]
    )
    output, weights, kept, vec = got[0], got[1:5], got[5:14], got[15]
    back = run_backward(dims, own, vec, prefix, slopes, weights, kept)
    grad_low, grad_q, grad_o, grad_u, grad_d, sums, low = back[:7]
    sums = lax.dynamic_slice_in_dim(sums, spot, lane, 1)
    low = lax.dynamic_slice_in_dim(low, plane * part, part, 1)
    ends = jnp.where(is_first, grad_low, output).reshape(seqs, rows, width)
    return (
        ends[None],
        sums[None, 0:2],
        sums[None, 2:6],
        grad_q.transpose(1, 0, 2)[None],
        low[: 2 * heads].reshape(1, 2, heads, part),
        grad_o[None],
        grad_u[None],
        low[2 * heads :][None],
        grad_d[None],
    )


def solution(mesh):
    in_specs = (
        P("section", "dp", "tensor", None),
        P("section", None, ("dp", "tensor")),
        P("section", None, ("dp", "tensor")),
        P("section", "dp", None, "tensor"),
        P("section", None, "tensor", "dp"),
        P("section", "tensor", "dp"),
        P("section", "dp", "tensor"),
        P("section", "tensor", "dp"),
        P("section", "tensor", "dp"),
        P("dp"),
    )
    out_specs = (
        P("section", "dp", "tensor", None),
        P("section", None, ("dp", "tensor")),
        P("section", None, ("dp", "tensor")),
        P("section", "dp", None, "tensor"),
        P("section", None, "tensor", "dp"),
        P("section", "tensor", "dp"),
        P("section", "dp", "tensor"),
        P("section", "tensor", "dp"),
        P("section", "tensor", "dp"),
    )
    return jax.shard_map(
        on_device, mesh=mesh, in_specs=in_specs, out_specs=out_specs, check_vma=False
    )
```

```python
import functools

import jax
import jax.numpy as jnp
import numpy as np
from jax import lax
from jax.experimental import pallas as pl
from jax.experimental.pallas import tpu as pltpu
from jax.sharding import PartitionSpec as P

BF = jnp.bfloat16
F32 = jnp.float32


MESH = pl.DeviceIdType.MESH
EARLY = True
RELAYED = ((3,), ())
GRADS_RELAYED = ((3,), (3, 2,1))
ATT_RELAYED = (0, 1)
NT = (((1,), (1,)), ((), ()))
TN = (((0,), (0,)), ((), ()))


def dot(a, b, dims=(((1,), (0,)), ((), ()))):
    return lax.dot_general(a, b, dims, preferred_element_type=F32)


def remote(src, dst, send_sem, recv_sem, device):
    return pltpu.make_async_remote_copy(
        src_ref=src, dst_ref=dst, send_sem=send_sem, recv_sem=recv_sem, device_id=device, device_id_type=MESH
    )


def when(condition):
    return True if condition is True else condition


def greet(devices):
    barrier = pltpu.get_barrier_semaphore()
    for device in devices:
        pl.semaphore_signal(barrier, inc=1, device_id=device, device_id_type=MESH)
    pl.semaphore_wait(barrier, len(devices))


def tiles(count, body):
    def step(i, carry):
        body(i)
        return carry

    lax.fori_loop(0, count, step, 0)


def half_tiles(count, part, body):
    tiles(count // 2, lambda i: body(i + part * (count // 2)))


def rows_of(i, size):
    return pl.ds(pl.multiple_of(i * size, size), size)


def norm_rows(value, gain, shift_vec):
    centre = value - jnp.mean(value, axis=-1, keepdims=True)
    spread = jnp.mean(centre * centre, axis=-1, keepdims=True)
    return centre * lax.rsqrt(spread + 1e-05) * gain + shift_vec


def spots(base, shape, dim, rows):
    index = lax.broadcasted_iota(jnp.int32, shape, dim)
    return ((index // rows) ^ base) * rows + lax.rem(index, rows)


def gelu_parts(v):
    cube = v * v * v
    inner = np.float32(np.sqrt(2 / np.pi)) * (v + 0.044715 * cube)
    return jnp.tanh(inner)


def masked_scores(raw, slope, length, place, rows, size):
    gap = spots(place, raw.shape, 0, rows) - spots(place, raw.shape, 1, rows)
    open_ = (gap >= 0) | (spots(place, raw.shape, 1, rows) < length)
    scores = raw * np.float32(size ** (-0.5)) - slope * gap.astype(F32)
    return jnp.where(open_, scores, -1e30)


def relayed(layer):
    return [k for k in RELAYED[layer]]


def peers_of(n):
    sect, z, t = lax.axis_index("section"), lax.axis_index("dp"), lax.axis_index("tensor")
    return [(sect, z ^ (k // 4), t ^ (k % 4)) for k in range(1, 4 * n)]


def note_copy(n, k, src, dst, send_sem, recv_sem):
    return remote(src, dst.at[k], send_sem.at[k], recv_sem.at[k], peers_of(n)[k - 1])


def forward_kernel(
    dims, x_in, note, prefix, slopes, wq_in, wo_in, wu_in, wd_in,
    out, wq, wo, wu, wd, x_out, mid_out, nb_out, qkv_out, mix_out, sec_out, up_out, act_out, top_out, lent, vec_out,
    notes, panel, vec, qvb, upb, note_s, note_r,
    carry, carry_send, hid, mid, nb, qkv, mix, sec, up, act, outv,
    vq, vo, vu, vd, s1, r1, part, sy, ry, part8, sc, rc, s8, r8,
    line_s, line_r, pair_s, pair_r, own_sem, load_sem, keep_sem, carry_s, carry_r,
    ag_s, ag_r, rs_s, rs_r, ag8_s, ag8_r, f8_s, f8_r, c8_s, c8_r, rs8_s, rs8_r,
    top_s, top_r, near_s, near_r, lent_s, lent_r, direct_s, cor_s, cor_r,
):
    n, seqs, heads, size, rows, deep, half = dims
    R = seqs * rows
    wide = heads * size
    D = n * deep
    sect, z, t = lax.axis_index("section"), lax.axis_index("dp"), lax.axis_index("tensor")
    me = (sect, z, t)
    core = (sect, z, t ^ 1)
    chip = (sect, z, t ^ 2)
    plane = (sect, z ^ 1, t)
    diag = (sect, z ^ 1, t ^ 2)
    across = (1 - sect, z, t)
    greet(peers_of(n) + [(1 - sect, z ^ k, t) for k in range(n)])
    share = [note_copy(n, k, note, notes, note_s, note_r) for k in range(1, 4 * n)]
    for copy in share:
        copy.start()

    def lend(b):
        at = pl.ds(pl.multiple_of(((z & 1) ^ b) * half, half), half)
        return remote(wd_in.at[at], lent.at[at], lent_s.at[b], lent_r.at[b], across)

    def on_layer(layer, body):
        pl.when(sect == layer)(body)

    def lends(layer):
        return [b for b in range(2) if any(k & 1 == b for k in relayed(layer))]

    for layer in range(2):
        def body():
            for b in lends(layer):
                lend(b).start()

        on_layer(layer, body)

    zl = z & 1
    mine = [
        pltpu.make_async_copy(wq_in, wq.at[:, pl.ds(pl.multiple_of(z * deep, deep), deep)], own_sem.at[0]),
        pltpu.make_async_copy(wo_in, wo.at[z], own_sem.at[1]),
        pltpu.make_async_copy(
            wu_in.at[:, pl.ds(pl.multiple_of(zl * half, half), half)],
            wu.at[pl.ds(pl.multiple_of(z * deep, deep), deep)], own_sem.at[2]),
        pltpu.make_async_copy(
            wd_in.at[pl.ds(pl.multiple_of(zl * half, half), half)], wd.at[z], own_sem.at[3]),
    ]

    def slot(a, b):
        if a == 0:
            return wq.at[:, pl.ds(pl.multiple_of(b * deep, deep), deep)]
        return wo.at[b]

    def line(a, side, step, b):
        to = (sect, z + 1 - 2 * side, t)
        src = (wq_in, wo_in)[a] if step == 1 else slot(a, b)
        i = (a * 2 + side) * (n - 1) + step - 1
        return remote(src, slot(a, b), line_s.at[i], line_r.at[i], to)

    def line_send(a, side, step):
        b = z - (step - 1) if side == 0 else z + (step - 1)
        ok = (b >= 0) & (z < n - 1) if side == 0 else (b <= n - 1) & (z > 0)
        return ok, lambda: line(a, side, step, b)

    def line_recv(a, side, step):
        b = z - step if side == 0 else z + step
        ok = (b >= 0) if side == 0 else (b <= n - 1)
        return ok, lambda: line(a, side, step, b)

    def pair(a, k):
        h = (z ^ k) & 1
        to = (sect if a == 0 else 1 - sect, z ^ k, t)
        i = a * (n - 1) + k - 1
        if a == 0:
            src = wu_in.at[:, pl.ds(pl.multiple_of(h * half, half), half)]
            dst = wu.at[pl.ds(pl.multiple_of(z * deep, deep), deep)]
        else:
            src = lent.at[pl.ds(pl.multiple_of(h * half, half), half)]
            dst = wd.at[z]
        return remote(src, dst, pair_s.at[i], pair_r.at[i], to)

    def pair_recv(a, k):
        i = a * (n - 1) + k - 1
        if a == 0:
            src = wu_in.at[:, pl.ds(0, half)]
            dst = wu.at[pl.ds(pl.multiple_of((z ^ k) * deep, deep), deep)]
        else:
            src = wd_in.at[pl.ds(0, half)]
            dst = wd.at[z ^ k]
        return remote(src, dst, pair_s.at[i], pair_r.at[i], (sect, z ^ k, t))

    for a in range(2):
        for side in range(2):
            ok, make = line_send(a, side, 1)

            @pl.when(ok)
            def _():
                make().start()

    for copy in mine:
        copy.start()

    def vectors():
        for copy in share:
            copy.wait_recv()
        notes[0] = note[...]
        panel[...] = jnp.zeros_like(panel)
        me = z * 4 + t
        lane = D // (4 * n)
        for k in range(4 * n):
            panel[((me ^ k) * lane) // 128] += notes[k, 0:8, :]
        for j in range(D // 128):
            vec[:, j * 128 : (j + 1) * 128] = panel[j]
        low = notes[0, 8:32, :]
        for k in range(4, 4 * n, 4):
            low = low + notes[k, 8:32, :]
        qvb[...] = jnp.zeros_like(qvb)
        for h in range(heads):
            for c in range(2):
                qvb[2 * c : 2 * c + 1, h * size : (h + 1) * size] = low[c * heads + h : c * heads + h + 1, :]
        count = half // 128
        first = low[2 * heads : 2 * heads + count]
        later = low[2 * heads + count : 2 * heads + 2 * count]
        units = jnp.where(zl == 1, later, first)
        for j in range(count):
            upb[0:1, j * 128 : (j + 1) * 128] = units[j : j + 1, :]

    tile = 32

    def part_of_rows(h, size=R):
        return pl.ds(h * (size // 2), size // 2)

    def first_norm(h):
        def body(i):
            sl = rows_of(i, tile)
            v = hid[sl, :].astype(F32)
            nb[0, sl, :] = norm_rows(v, vec[0:1, :], vec[2:3, :]).astype(BF)

        half_tiles(R // tile, h, body)
        ag(1, h).start()
        ag(0, h).start()

    def ag(i, h):
        src, to = ((0, core), (0, chip), (2, core))[i]
        dst = (1, 2, 3)[i]
        at = part_of_rows(h)
        return remote(nb.at[src, at], nb.at[dst, at], ag_s.at[2 * i + h], ag_r.at[2 * i + h], to)

    def over(h):
        at = part_of_rows(h)
        return remote(carry_send.at[at], carry.at[at], carry_s.at[h], carry_r.at[h], across)

    def pass_on():
        for h in range(2):
            ag(1, h).wait_recv()
            ag(2, h).start()

    vectors()

    @pl.when(sect == 0)
    def _():
        hid[...] = x_in[...]
        first_norm(0)
        first_norm(1)
        pass_on()

    def direct(k):
        i = n - 1 + k - 1
        src = wd_in.at[pl.ds(pl.multiple_of(((z ^ k) & 1) * half, half), half)]
        return remote(src, wd.at[z], direct_s.at[k - 1], pair_r.at[i], (sect, z ^ k, t))

    def relay(layer):
        for b in lends(layer):
            lend(b).wait_recv()
        for k in relayed(layer):
            pair(1, k).start()

    def top(i):
        return remote(x_in, top_out.at[i], top_s.at[i], top_r.at[i], (core, chip, plane, diag)[i])

    def top_near(i):
        return remote(top_out.at[i], top_out.at[4 + i], near_s.at[i], near_r.at[i], core)

    top_own = pltpu.make_async_copy(x_in, top_out.at[0], own_sem.at[4])
    top_land = [remote(x_in, top_out.at[4], top_s.at[0], top_r.at[0], core)]

    @pl.when(sect == 1)
    def _():
        relay(0)

    for step in range(1, n):
        for a in range(2):
            for side in range(2):
                ok, make = line_recv(a, side, step)

                @pl.when(ok)
                def _():
                    make().wait_recv()

                if step < n - 1:
                    ok, make = line_send(a, side, step + 1)

                    @pl.when(ok)
                    def _():
                        make().start()

        if step == n - 2 or n == 2:
            for k in range(n - 1, 0, -1):
                pair(0, k).start()

    for layer in range(2):
        def body():
            for k in range(n - 1, 0, -1):
                if k not in relayed(layer):
                    direct(k).start()

        on_layer(layer, body)

    for copy in mine:
        copy.wait()
    load_q = pltpu.make_async_copy(wq, vq, load_sem.at[0])
    load_o = pltpu.make_async_copy(wo, vo, load_sem.at[1])
    load_q.start()
    load_o.start()

    @pl.when(sect == 1)
    def _():
        top_own.start()
        for i in (1, 2, 3):
            top(i).start()
        top_land[0].start()
        for h in range(2):
            over(h).wait_recv()
            hid[part_of_rows(h), :] = carry[part_of_rows(h), :]
            first_norm(h)

    load_q.wait()
    load_o.wait()
    ag(0, 0).wait_recv()
    ag(0, 1).wait_recv()
    keeps = []

    def keep(src, dst):
        copy = pltpu.make_async_copy(src, dst, keep_sem.at[len(keeps)])
        copy.start()
        keeps.append(copy)

    keep(hid, x_out)
    keep(vec, vec_out)

    tn = min(256, wide)

    def project_in(b):
        for c in range(3):
            def body(j):
                cols = rows_of(j, tn)
                lhs = jnp.concatenate([nb[2 * b], nb[2 * b + 1]], axis=0)
                got = dot(lhs, vq[c, :, cols]) + qvb[c : c + 1, cols]
                got = got.astype(BF)
                qkv[2 * b, :, pl.ds(pl.multiple_of(c * wide + j * tn, tn), tn)] = got[:R]
                qkv[2 * b + 1, :, pl.ds(pl.multiple_of(c * wide + j * tn, tn), tn)] = got[R:]

            tiles(wide // tn, body)

    project_in(0)

    @pl.when(sect == 1)
    def _():
        pass_on()

    ag(2, 0).wait_recv()
    ag(2, 1).wait_recv()
    project_in(1)
    keep(nb, nb_out)
    keep(qkv, qkv_out)

    def head(i):
        s = i // (heads // 2)
        both = [2 * lax.rem(i, heads // 2) + b for b in range(2)]
        pos = rows_of(s, rows)

        def part_of(c, h):
            cols = pl.ds(pl.multiple_of(c * wide + h * size, size), size)
            return jnp.concatenate([qkv[j, pos, cols] for j in range(4)], axis=0)

        raw = [dot(part_of(0, h), part_of(1, h), NT) for h in both]
        scores = [masked_scores(raw[b], slopes[both[b]], prefix[s], t, rows, size) for b in range(2)]
        expon = [jnp.exp(v - jnp.max(v, axis=-1, keepdims=True)) for v in scores]
        probs = [(v / jnp.sum(v, axis=-1, keepdims=True)).astype(BF) for v in expon]
        got = [dot(probs[b], part_of(2, both[b])).astype(BF) for b in range(2)]
        for b in range(2):
            for j in range(4):
                mix[j, pos, rows_of(both[b], size)] = got[b][j * rows : (j + 1) * rows]

    tiles(seqs * heads // 2, head)
    keep(mix, mix_out)

    def columns(c):
        return pl.ds(c * (D // 2), D // 2)

    def project(lhs_blocks, put, c):

        def body(i):
            lhs = jnp.concatenate([mix[lhs_blocks[0]], mix[lhs_blocks[1]]], axis=0)
            got = dot(lhs, vo[i])
            put(rows_of(i, deep), got)

        half_tiles(n, c, body)

    def put_send(cols, got):
        s1[0, :, cols] = got[:R].astype(BF)
        s1[1, :, cols] = got[R:].astype(BF)

    def put_part(cols, got):
        part[0, :, cols] = got[:R]
        part[1, :, cols] = got[R:]

    def to_core(c):
        at = columns(c)
        return remote(s1.at[:, :, at], r1.at[:, :, at], rs_s.at[c], rs_r.at[c], core)

    def to_chip(c):
        at = columns(c)
        return remote(sy.at[:, at], ry.at[:, at], rs_s.at[2 + c], rs_r.at[2 + c], chip)

    def add_chip(c):
        to_core(c).wait_recv()

        def body(i):
            sl = rows_of(i, tile)
            at = columns(c)
            sy[sl, at] = (part[0, sl, at] + r1[0, sl, at].astype(F32)).astype(BF)

        tiles(R // tile, body)
        to_chip(c).start()

    project((3, 1), put_send, 0)
    to_core(0).start()
    project((2, 0), put_part, 0)
    project((3, 1), put_send, 1)
    to_core(1).start()
    add_chip(0)
    project((2, 0), put_part, 1)
    add_chip(1)
    to_chip(0).wait_recv()
    to_chip(1).wait_recv()

    def middle_body(i):
        sl = rows_of(i, tile)
        v = hid[sl, :].astype(F32) + part[1, sl, :] + r1[1, sl, :].astype(F32)
        v = v + ry[sl, :].astype(F32) + vec[4:5, :]
        mid[sl, :] = v
        sec[0, sl, :] = norm_rows(v, vec[1:2, :], vec[3:4, :]).astype(BF)


    targets = (None, chip, plane, diag)

    def ag8(i, h):
        at = part_of_rows(h)
        return remote(sec.at[0, at], sec.at[i, at], ag8_s.at[2 * i + h], ag8_r.at[2 * i + h], targets[i])

    def corner8(i):
        at = pl.ds(i * (R // 2), R // 2)
        return remote(sec.at[2 - i, at], sec.at[3, at], cor_s.at[i], cor_r.at[i], (chip, plane)[i])

    def forward8(i):
        return remote(sec.at[i], sec.at[4 + i], f8_s.at[i], f8_r.at[i], core)

    def core8(i):
        return remote(sc.at[i], rc.at[i], c8_s.at[i], c8_r.at[i], core)

    def rs8(i):
        return remote(s8.at[i], r8.at[i], rs8_s.at[i], rs8_r.at[i], targets[i])

    order = (0, 2, 1, 3)
    for h in range(2):
        half_tiles(R // tile, h, middle_body)
        for i in order[1:3]:
            ag8(i, h).start()
    forward8(0).start()
    keep(mid, mid_out)

    def arrive():
        ag8(2, 0).wait_recv()
        corner8(0).start()
        ag8(2, 1).wait_recv()
        forward8(2).start()
        ag8(1, 0).wait_recv()
        ag8(1, 1).wait_recv()
        corner8(1).start()
        forward8(1).start()

    def arrive_corner():
        corner8(0).wait_recv()
        corner8(1).wait_recv()
        forward8(3).start()

    load_u = pltpu.make_async_copy(wu, vu, load_sem.at[2])
    load_d = pltpu.make_async_copy(wd, vd, load_sem.at[3])

    def weights_in(a):
        for k in range(n - 1, 0, -1):
            pair_recv(a, k).wait_recv()
        (load_u, load_d)[a].start()

    tu = min(256, half)

    def up_part(i):
        def up_body(j):
            cols = rows_of(j, tu)
            lhs = jnp.concatenate([sec[i], sec[4 + i]], axis=0)
            v = dot(lhs, vu[:, cols]) + upb[:, cols]
            g = (0.5 * v * (1.0 + gelu_parts(v))).astype(BF)
            up[i, :, cols] = v[:R]
            up[4 + i, :, cols] = v[R:]
            act[i, :, cols] = g[:R]
            act[4 + i, :, cols] = g[R:]

        tiles(half // tu, up_body)

    def down_part(i):
        def down_body(j):
            cols = rows_of(j, deep)
            lhs = jnp.concatenate([act[i], act[4 + i]], axis=0)
            got = dot(lhs, vd[j])
            part8[i, :, cols] = got[:R]
            sc[i, :, cols] = got[R:].astype(BF)

        tiles(n, down_body)
        core8(i).start()

    def reduce(i):
        core8(i).wait_recv()
        if i == 0:
            return

        def body(j):
            sl = rows_of(j, tile)
            s8[i, sl, :] = (part8[i, sl, :] + rc[i, sl, :].astype(F32)).astype(BF)

        tiles(R // tile, body)
        rs8(i).start()

    @pl.when(sect == 0)
    def _():
        arrive()
        arrive_corner()
        weights_in(0)
        weights_in(1)
        for i in range(4):
            forward8(i).wait_recv()
        load_u.wait()
        load_d.wait()
        for number, i in enumerate(order[::-1]):
            up_part(i)
            down_part(i)
            if number:
                reduce(order[4 - number])
        reduce(order[0])

    @pl.when(sect == 1)
    def _():
        weights_in(0)
        weights_in(1)
        load_u.wait()
        load_d.wait()
        for number, i in enumerate(order):
            if number == 1:
                arrive()
            if number == 3:
                arrive_corner()
            forward8(i).wait_recv()
            up_part(i)
            down_part(i)
            if number:
                reduce(order[number - 1])
        reduce(order[3])

    keep(sec, sec_out)
    keep(up, up_out)
    keep(act, act_out)
    for i in order[1:]:
        rs8(i).wait_recv()

    def out_body(j):
        sl = rows_of(j, tile)
        v = mid[sl, :] + part8[0, sl, :] + rc[0, sl, :].astype(F32)
        for i in (1, 2, 3):
            v = v + r8[i, sl, :].astype(F32)
        v = v + vec[5:6, :]
        outv[sl, :] = v
        carry_send[sl, :] = v.astype(BF)

    for h in range(2):
        half_tiles(R // tile, h, out_body)

        @pl.when(sect == 0)
        def _():
            over(h).start()

    @pl.when(sect == 0)
    def _():
        relay(1)

    keep(outv, out)

    for copy in share:
        copy.wait_send()
    for step in range(1, n):
        for a in range(2):
            for side in range(2):
                ok, make = line_send(a, side, step)

                @pl.when(ok)
                def _():
                    make().wait_send()

    for k in range(n - 1, 0, -1):
        pair(0, k).wait_send()
    for i in range(6):
        ag(i // 2, i % 2).wait_send()
    for c in range(2):
        to_core(c).wait_send()
        to_chip(c).wait_send()
    for i in range(4):
        if i in (1, 2):
            ag8(i, 0).wait_send()
            ag8(i, 1).wait_send()
            corner8(i - 1).wait_send()
        if i:
            rs8(i).wait_send()
        forward8(i).wait_send()
        core8(i).wait_send()

    for layer in range(2):
        def body():
            for b in lends(layer):
                lend(b).wait_send()
            for k in range(1, n):
                if k not in relayed(layer):
                    direct(k).wait_send()
            for k in relayed(1 - layer):
                pair(1, k).wait_send()

        on_layer(layer, body)

    @pl.when(sect == 0)
    def _():
        over(0).wait_send()
        over(1).wait_send()

    @pl.when(sect == 1)
    def _():
        for i in (1, 2, 3):
            top(i).wait_recv()
            top_near(i).start()
        top_land[0].wait_recv()
        for i in (1, 2, 3):
            top_near(i).wait_recv()
        top_own.wait()
        top_land[0].wait_send()
        for i in (1, 2, 3):
            top(i).wait_send()
            top_near(i).wait_send()

    for copy in keeps:
        copy.wait()


def run_forward(dims, x, note, prefix, slopes, wq, wo, wu, wd):
    n, seqs, heads, size, rows, deep, half = dims
    R, wide, D = seqs * rows, heads * size, n * deep
    V = lambda shape, dtype: pltpu.VMEM(shape, dtype)
    S = lambda *shape: jax.ShapeDtypeStruct(shape[:-1], shape[-1])
    any_ = pl.BlockSpec(memory_space=pl.ANY)
    vm = pl.BlockSpec(memory_space=pltpu.VMEM)
    sm = pl.BlockSpec(memory_space=pltpu.SMEM)
    dma = lambda k: pltpu.SemaphoreType.DMA((k,))
    outs = (
        S(R, D, F32), S(3, D, wide, BF), S(n, wide, deep, BF), S(D, half, BF), S(n, half, deep, BF),
        S(R, D, BF), S(R, D, F32), S(4, R, D, BF), S(4, R, 3 * wide, BF), S(4, R, wide, BF),
        S(8, R, D, BF), S(8, R, half, F32), S(8, R, half, BF), S(8, R, D, BF), S(2 * half, deep, BF), S(8, D, F32),
    )
    scratch = [
        V((4 * n, 32, 128), F32), V((D // 128, 8, 128), F32), V((8, D), F32), V((4, wide), F32), V((1, half), F32),
        dma(4 * n), dma(4 * n),
        V((R, D), BF), V((R, D), BF), V((R, D), BF), V((R, D), F32), V((4, R, D), BF), V((4, R, 3 * wide), BF),
        V((4, R, wide), BF), V((8, R, D), BF), V((8, R, half), F32), V((8, R, half), BF), V((R, D), F32),
        V((3, D, wide), BF), V((n, wide, deep), BF), V((D, half), BF), V((n, half, deep), BF),
        V((2, R, D), BF), V((2, R, D), BF), V((2, R, D), F32), V((R, D), BF), V((R, D), BF),
        V((4, R, D), F32), V((4, R, D), BF), V((4, R, D), BF), V((4, R, D), BF), V((4, R, D), BF),
        dma(4 * (n - 1)), dma(4 * (n - 1)), dma(2 * (n - 1)), dma(2 * (n - 1)), dma(5), dma(4), dma(10),
        dma(2), dma(2),
        dma(6), dma(6), dma(4), dma(4), dma(8), dma(8), dma(4), dma(4), dma(4), dma(4), dma(4), dma(4),
        dma(4), dma(4), dma(4), dma(4), dma(2), dma(2), dma(n - 1), dma(2), dma(2),
    ]
    return pl.pallas_call(
        functools.partial(forward_kernel, dims),
        out_shape=outs,
        in_specs=[vm, vm, sm, sm, any_, any_, any_, any_],
        out_specs=(any_,) * len(outs),
        scratch_shapes=scratch,
        compiler_params=pltpu.CompilerParams(
            collective_id=0, has_side_effects=True, vmem_limit_bytes=60 * 1024 * 1024
        ),
    )(x, note, prefix, slopes, wq, wo, wu, wd)


def backward_kernel(
    dims, top, vec, prefix, slopes, wq, wo, wu, wd, hid_in, mid_in, nb_in, qkv_in, mix_in, sec_in, up_in, act_in, top_in,
    dh_out, gq_out, go_out, gu_out, gd_out, sums_out, low_out, ru, rd, rq, ro, lent, lentq,
    carry, grad, mid, hid, dmid, gp, gm, gu, gd, gq, go, part, own8, sc, rc, s8, r8,
    s1, r1, sy, ry, sums, proj, ups, tmpq, tmpo, panel, low, notes, lows, sums_v, low_v, note_s, note_r, low_s, low_r,
    load_sem, up_sem, out_sem, carry_s, carry_r, ag8_s, ag8_r, f8_s, f8_r, c8_s, c8_r, rs8_s, rs8_r,
    ag_s, ag_r, rs_s, rs_r, ffn_s, ffn_r, att_s, att_r, lent_s, lent_r, lentq_s, lentq_r, over_s, cor_s, cor_r,
):
    n, seqs, heads, size, rows, deep, half = dims
    R = seqs * rows
    wide = heads * size
    D = n * deep
    sect, z, t = lax.axis_index("section"), lax.axis_index("dp"), lax.axis_index("tensor")
    core = (sect, z, t ^ 1)
    chip = (sect, z, t ^ 2)
    plane = (sect, z ^ 1, t)
    diag = (sect, z ^ 1, t ^ 2)
    across = (1 - sect, z, t)
    greet(peers_of(n) + [(1 - sect, z ^ k, t) for k in range(n)])
    zl = z & 1
    tile = 32
    order = (0, 2, 1, 3)
    targets = (None, chip, plane, diag)

    def part_of_rows(h):
        return pl.ds(h * (R // 2), R // 2)

    def ag8(i, h):
        at = part_of_rows(h)
        return remote(gp.at[0, at], gp.at[i, at], ag8_s.at[2 * i + h], ag8_r.at[2 * i + h], targets[i])

    def corner8(i):
        at = pl.ds(i * (R // 2), R // 2)
        return remote(gp.at[2 - i, at], gp.at[3, at], cor_s.at[i], cor_r.at[i], (chip, plane)[i])

    def forward8(i):
        return remote(gp.at[i], gp.at[4 + i], f8_s.at[i], f8_r.at[i], core)

    def core8(i):
        return remote(sc.at[i], rc.at[i], c8_s.at[i], c8_r.at[i], core)

    def rs8(i):
        return remote(s8.at[i - 1], r8.at[i - 1], rs8_s.at[i], rs8_r.at[i], targets[i])

    def load(src, dst, i):
        copy = pltpu.make_async_copy(src, dst, load_sem.at[i])
        copy.start()
        return copy

    load_mid, load_hid = load(mid_in, mid, 0), load(hid_in, hid, 1)
    sums[...] = jnp.zeros_like(sums)
    proj[...] = jnp.zeros_like(proj)
    ups[...] = jnp.zeros_like(ups)

    def over(h):
        at = part_of_rows(h)
        return remote(s1.at[0, at], carry.at[at], carry_s.at[h], carry_r.at[h], across)

    def col_sum(row, value):
        sums[row : row + 1, :] += jnp.sum(value, axis=0, keepdims=True)

    def ffn(a, k):
        i = a * (n - 1) + k - 1
        to = (sect if a == 0 else 1 - sect, z ^ k, t)
        src = gu.at[k] if a == 0 else lent.at[k - 1]
        return remote(src, (ru, rd)[a].at[k - 1], ffn_s.at[i], ffn_r.at[i], to)

    def direct(k):
        return remote(gd.at[k], rd.at[k - 1], lent_s.at[k - 1], ffn_r.at[n - 1 + k - 1], (sect, z ^ k, t))

    def lend(k):
        return remote(gd.at[k], lent.at[k - 1], lent_s.at[k - 1], lent_r.at[k - 1], across)

    def ffn_start(layer, k):
        if k not in GRADS_RELAYED[layer]:
            direct(k).start()
        elif layer == 0:
            lend(k).start()
        ffn(0, k).start()

    def relay(layer):
        for k in GRADS_RELAYED[layer]:
            lend(k).wait_recv()
            ffn(1, k).start()

    def feed(vu, vd, sec, act, dup, upb):
        load_d = pltpu.make_async_copy(wd, vd, load_sem.at[3])
        load_u = pltpu.make_async_copy(wu, vu, load_sem.at[2])
        load_a = pltpu.make_async_copy(act_in, act, load_sem.at[5])
        load_s = pltpu.make_async_copy(sec_in, sec, load_sem.at[4])
        th_ = min(256, half)

        def down_grad(k):
            def body(j):
                cols = rows_of(j, th_)
                lhs = act[:, :, cols].reshape(8 * R, th_)
                at = pl.ds(pl.multiple_of((z ^ k) * deep, deep), deep)
                gd[k, cols, :] = dot(lhs, gp[:, :, at].reshape(8 * R, deep), TN).astype(BF)

            tiles(half // th_, body)


        def up_load(number, turn):
            i, slot = turn[number], number % 2
            return [
                pltpu.make_async_copy(up_in.at[i + 4 * b], upb.at[slot, b], up_sem.at[2 * slot + b])
                for b in range(2)
            ]

        load_top = pltpu.make_async_copy(top_in, gp, load_sem.at[6])
        for layer in range(2):
            @pl.when(sect == layer)
            def _():
                for number in range(2):
                    for copy in up_load(number, order[:: 1 - 2 * layer]):
                        copy.start()

        load_d.start()

        @pl.when(sect == 1)
        def _():
            load_top.start()
            load_a.start()
            load_u.start()
            grad[...] = top[...]
            load_top.wait()
            load_a.wait()
            for k in GRADS_RELAYED[1]:
                down_grad(k)
                lend(k).start()

        @pl.when(sect == 0)
        def _():
            load_u.start()
            load_a.start()
            relay(1)
            for h in range(2):
                over(h).wait_recv()
                value = carry[part_of_rows(h), :]
                grad[part_of_rows(h), :] = value
                gp[0, part_of_rows(h), :] = value
                for i in order[1:3]:
                    ag8(i, h).start()
            forward8(0).start()

        def bias_body(j):
            col_sum(5, grad[rows_of(j, tile), :].astype(F32))

        tiles(R // tile, bias_body)
        load_d.wait()
        tu = min(256, half)
        td = min(256, D)

        def group(number, turn, arriving):
            i, slot = turn[number], number % 2
            if arriving:
                if number == 1:
                    ag8(2, 0).wait_recv()
                    corner8(0).start()
                    ag8(2, 1).wait_recv()
                    forward8(2).start()
                    ag8(1, 0).wait_recv()
                    ag8(1, 1).wait_recv()
                    corner8(1).start()
                    forward8(1).start()
                if i == 3:
                    corner8(0).wait_recv()
                    corner8(1).wait_recv()
                    forward8(3).start()
                forward8(i).wait_recv()
            for copy in up_load(number, turn):
                copy.wait()

            def up_body(j):
                cols = rows_of(j, tu)
                got = None
                for b in range(n):
                    at = pl.ds(b * deep, deep)
                    lhs = jnp.concatenate([gp[i, :, at], gp[4 + i, :, at]], axis=0)
                    term = dot(lhs, vd[b, cols, :], NT)
                    got = term if got is None else got + term
                v = jnp.concatenate([upb[slot, 0, :, cols], upb[slot, 1, :, cols]], axis=0)
                th = gelu_parts(v)
                slope = 0.5 * (1.0 + th) + 0.5 * v * (1.0 - th * th) * np.float32(np.sqrt(2 / np.pi)) * (
                    1.0 + np.float32(3 * 0.044715) * v * v
                )
                low = (got * slope).astype(BF)
                dup[i, :, cols] = low[:R]
                dup[4 + i, :, cols] = low[R:]
                ups[0:1, cols] += jnp.sum(low.astype(F32), axis=0, keepdims=True)

            tiles(half // tu, up_body)
            if number + 2 < 4:
                for copy in up_load(number + 2, turn):
                    copy.start()

            if number == 0:
                load_u.wait()
                load_s.start()

            def second_body(j):
                cols = rows_of(j, td)
                lhs = jnp.concatenate([dup[i], dup[4 + i]], axis=0)
                got = dot(lhs, vu[cols, :], NT)
                if i == 0:
                    own8[:, cols] = got[:R]
                else:
                    part[slot, :, cols] = got[:R]
                sc[i, :, cols] = got[R:].astype(BF)

            tiles(D // td, second_body)
            core8(i).start()

        def reduce(number, turn):
            i, slot = turn[number], number % 2
            core8(i).wait_recv()
            if i == 0:
                return

            def body(j):
                sl = rows_of(j, tile)
                s8[i - 1, sl, :] = (part[slot, sl, :] + rc[i, sl, :].astype(F32)).astype(BF)

            tiles(R // tile, body)
            rs8(i).start()

        def every(turn, arriving):
            for number in range(4):
                group(number, turn, arriving)
                if number:
                    reduce(number - 1, turn)
            reduce(3, turn)

        @pl.when(sect == 0)
        def _():
            every(order, True)

        @pl.when(sect == 1)
        def _():
            every(order[::-1], False)

        load_s.wait()

        @pl.when(sect == 0)
        def _():
            load_a.wait()

        for k in list(range(n - 1, 0, -1)) + [0]:
            if k in GRADS_RELAYED[1]:
                pl.when(sect == 0)(functools.partial(down_grad, k))
            else:
                down_grad(k)
            dd = min(256, deep)

            def up_body(j):
                at = pl.ds(pl.multiple_of((z ^ k) * deep + j * dd, dd), dd)
                lhs = sec[:, :, at].reshape(8 * R, dd)
                gu[k, rows_of(j, dd), :] = dot(lhs, dup[...].reshape(8 * R, half), TN).astype(BF)

            tiles(deep // dd, up_body)
            if EARLY and k:
                @pl.when(sect == 0)
                def _():
                    ffn_start(0, k)

    pl.run_scoped(
        feed,
        pltpu.VMEM((D, half), BF), pltpu.VMEM((n, half, deep), BF), pltpu.VMEM((8, R, D), BF),
        pltpu.VMEM((8, R, half), BF), pltpu.VMEM((8, R, half), BF), pltpu.VMEM((2, 2, R, half), F32),
    )
    for i in order[1:]:
        rs8(i).wait_recv()
    for layer in range(1 if EARLY else 0, 2):
        @pl.when(sect == layer)
        def _():
            for k in range(n - 1, 0, -1):
                ffn_start(layer, k)

    load_mid.wait()
    load_hid.wait()

    def norm_back(value, gain, dy):
        centre = value - jnp.mean(value, axis=-1, keepdims=True)
        spread = jnp.mean(centre * centre, axis=-1, keepdims=True)
        scale = lax.rsqrt(spread + 1e-05)
        unit = centre * scale
        scaled = dy * gain
        inner = jnp.mean(scaled * unit, axis=-1, keepdims=True)
        return (scaled - jnp.mean(scaled, axis=-1, keepdims=True) - unit * inner) * scale, unit

    def mid_body(j):
        sl = rows_of(j, tile)
        dy = own8[sl, :] + rc[0, sl, :].astype(F32)
        for i in (1, 2, 3):
            dy = dy + r8[i - 1, sl, :].astype(F32)
        back, unit = norm_back(mid[sl, :], vec[1:2, :], dy)
        total = grad[sl, :].astype(F32) + back
        dmid[sl, :] = total
        gm[0, sl, :] = total.astype(BF)
        col_sum(1, dy * unit)
        col_sum(3, dy)
        col_sum(4, total)

    def ag(i, h):
        src, to = ((0, core), (0, chip), (2, core))[i]
        dst = (1, 2, 3)[i]
        at = part_of_rows(h)
        return remote(gm.at[src, at], gm.at[dst, at], ag_s.at[2 * i + h], ag_r.at[2 * i + h], to)

    for h in range(2):
        half_tiles(R // tile, h, mid_body)
        ag(1, h).start()
        ag(0, h).start()
    def columns(c):
        return pl.ds(c * (D // 2), D // 2)

    def to_core(c):
        at = columns(c)
        return remote(s1.at[:, :, at], r1.at[:, :, at], rs_s.at[c], rs_r.at[c], core)

    def to_chip(c):
        at = columns(c)
        return remote(sy.at[:, at], ry.at[:, at], rs_s.at[2 + c], rs_r.at[2 + c], chip)

    def add_chip(c):
        to_core(c).wait_recv()

        def body(i):
            sl = rows_of(i, tile)
            at = columns(c)
            sy[sl, at] = (part[0, sl, at] + r1[0, sl, at].astype(F32)).astype(BF)

        tiles(R // tile, body)
        to_chip(c).start()


    def low_bit(k):
        return k & -k

    def att(k, c):
        i = (k - 1) * 4 + c
        src, dst = (gq.at[k, c], rq.at[k - 1, c]) if c < 3 else (go.at[k], ro.at[k - 1])
        return remote(src, dst, att_s.at[i], att_r.at[i], (sect, z ^ low_bit(k), t))

    def att_lend(k, c):
        i = (k - 1) * 4 + c
        return remote(gq.at[k, c], lentq.at[k - 1, c], lentq_s.at[i], lentq_r.at[i], across)

    def att_relay(k, c):
        i = (k - 1) * 4 + c
        to = (1 - sect, z ^ low_bit(k), t)
        return remote(lentq.at[k - 1, c], rq.at[k - 1, c], over_s.at[i], att_r.at[i], to)

    def att_start(k, c):
        if c not in ATT_RELAYED:
            att(k, c).start()
            return

        @pl.when(sect == 0)
        def _():
            att_lend(k, c).start()

        @pl.when(sect == 1)
        def _():
            att(k, c).start()

    def at_once(k):
        return k > 1 and low_bit(k) == 1

    att_order = [k for k in range(n - 1, 1, -1) if k & 1]
    att_order += sorted((k for k in range(2, n, 2)), key=lambda k: (low_bit(k), -k)) + [1]
    send_order = sorted(range(1, n), key=lambda k: (low_bit(k), -k))

    def attention(vq, vo, nb, qkv, mix, dmix, dqkv):
        loads = [load(wo, vo, 2), load(qkv_in, qkv, 3), load(mix_in, mix, 4), load(nb_in, nb, 5), load(wq, vq, 6)]
        loads[0].wait()
        ag(0, 0).wait_recv()
        ag(0, 1).wait_recv()

        def mixed(b):
            if b == 1:
                for h in range(2):
                    ag(1, h).wait_recv()
                    ag(2, h).start()
                for copy in loads[1:]:
                    copy.wait()
                ag(2, 0).wait_recv()
                ag(2, 1).wait_recv()
            tw = min(256, wide)

            def body(j):
                cols = rows_of(j, tw)
                got = None
                for p in range(n):
                    at = pl.ds(p * deep, deep)
                    lhs = jnp.concatenate([gm[2 * b, :, at], gm[2 * b + 1, :, at]], axis=0)
                    term = dot(lhs, vo[p, cols, :], NT)
                    got = term if got is None else got + term
                low = got.astype(BF)
                dmix[2 * b, :, cols] = low[:R]
                dmix[2 * b + 1, :, cols] = low[R:]

            tiles(wide // tw, body)

        mixed(0)
        mixed(1)
        tw = min(256, wide)
        for k in send_order + [0]:
            at = pl.ds(pl.multiple_of((z ^ k) * deep, deep), deep)

            def out_body(j):
                cols = rows_of(j, tw)
                lhs = mix[:, :, cols].reshape(4 * R, tw)
                go[k, cols, :] = dot(lhs, gm[:, :, at].reshape(4 * R, deep), TN).astype(BF)

            tiles(wide // tw, out_body)
            if at_once(k):
                att_start(k, 3)

        def head(i):
            s = i // (heads // 2)
            pos = rows_of(s, rows)

            def part_of(ref, c, h):
                cols = pl.ds(pl.multiple_of(c * wide + h * size, size), size)
                return jnp.concatenate([ref[j, pos, cols] for j in range(4)], axis=0)

            def one(h):
                q, k, v, dm = part_of(qkv, 0, h), part_of(qkv, 1, h), part_of(qkv, 2, h), part_of(dmix, 0, h)
                scores = masked_scores(dot(q, k, NT), slopes[h], prefix[s], t, rows, size)
                dp = dot(dm, v, NT)
                expon = jnp.exp(scores - jnp.max(scores, axis=-1, keepdims=True))
                probs = expon / jnp.sum(expon, axis=-1, keepdims=True)
                inner = jnp.sum(probs * dp, axis=-1, keepdims=True)
                raw = (probs * (dp - inner) * np.float32(size ** (-0.5))).astype(BF)
                return [g.astype(BF) for g in (dot(raw, k), dot(raw, q, TN), dot(probs.astype(BF), dm, TN))]

            both = [2 * lax.rem(i, heads // 2) + b for b in range(2)]
            results = [one(h) for h in both]
            for h, result in zip(both, results):
                for c, low in enumerate(result):
                    cols = pl.ds(pl.multiple_of(c * wide + h * size, size), size)
                    proj[0:1, cols] += jnp.sum(low.astype(F32), axis=0, keepdims=True)
                    for j in range(4):
                        dqkv[j, pos, cols] = low[j * rows : (j + 1) * rows]

        tiles(seqs * heads // 2, head)

        def normed(blocks, put, c_half):
            td = min(256, D)

            def body(j):
                cols = rows_of(j, td)
                got = None
                for c in range(3):
                    lhs = jnp.concatenate([dqkv[b, :, c * wide : (c + 1) * wide] for b in blocks], axis=0)
                    term = dot(lhs, vq[c, cols, :], NT)
                    got = term if got is None else got + term
                put(cols, got)

            half_tiles(D // td, c_half, body)

        def put_send(cols, got):
            s1[0, :, cols] = got[:R].astype(BF)
            s1[1, :, cols] = got[R:].astype(BF)

        def put_part(cols, got):
            part[0, :, cols] = got[:R]
            part[1, :, cols] = got[R:]

        def normed_all():
            normed((3, 1), put_send, 0)
            to_core(0).start()
            normed((2, 0), put_part, 0)
            normed((3, 1), put_send, 1)
            to_core(1).start()
            add_chip(0)
            normed((2, 0), put_part, 1)
            add_chip(1)

        def grads_q():
            for k in send_order + [0]:
                at = pl.ds(pl.multiple_of((z ^ k) * deep, deep), deep)
                for c in range(3):
                    def body(j):
                        cols = rows_of(j, tw)
                        rhs = dqkv[:, :, pl.ds(pl.multiple_of(c * wide + j * tw, tw), tw)].reshape(4 * R, tw)
                        gq[k, c, :, cols] = dot(nb[:, :, at].reshape(4 * R, deep), rhs, TN).astype(BF)

                    tiles(wide // tw, body)
                    if at_once(k):
                        att_start(k, c)

        @pl.when(sect == 0)
        def _():
            grads_q()
            normed_all()

        @pl.when(sect == 1)
        def _():
            normed_all()
            grads_q()

    pl.run_scoped(
        attention,
        pltpu.VMEM((3, D, wide), BF), pltpu.VMEM((n, wide, deep), BF), pltpu.VMEM((4, R, D), BF),
        pltpu.VMEM((4, R, 3 * wide), BF), pltpu.VMEM((4, R, wide), BF), pltpu.VMEM((4, R, wide), BF),
        pltpu.VMEM((4, R, 3 * wide), BF),
    )
    for c in range(2):
        to_chip(c).wait_recv()
        to_core(c).wait_send()

    def low_body(j):
        sl = rows_of(j, tile)
        dy = part[1, sl, :] + r1[1, sl, :].astype(F32) + ry[sl, :].astype(F32)
        back, unit = norm_back(hid[sl, :].astype(F32), vec[0:1, :], dy)
        total = dmid[sl, :] + back
        dmid[sl, :] = total
        s1[0, sl, :] = total.astype(BF)
        col_sum(0, dy * unit)
        col_sum(2, dy)

    for h in range(2):
        half_tiles(R // tile, h, low_body)

        @pl.when(sect == 1)
        def _():
            over(h).start()

    outs = []

    def put(src, dst):
        copy = pltpu.make_async_copy(src, dst, out_sem.at[len(outs)])
        copy.start()
        outs.append(copy)

    put(dmid, dh_out)

    lane = D // (4 * n)
    for j in range(D // 128):
        panel[j] = sums[:, j * 128 : (j + 1) * 128]
    for h in range(heads):
        for c in range(2):
            at = 2 * c * wide + h * size
            low[c * heads + h : c * heads + h + 1, :] = proj[0:1, at : at + size]
    count = half // 128
    for j in range(count):
        row = ups[0:1, j * 128 : (j + 1) * 128]
        at = 2 * heads + j
        low[at : at + 1, :] = jnp.where(zl == 0, row, 0.0)
        low[at + count : at + count + 1, :] = jnp.where(zl == 1, row, 0.0)
    me = z * 4 + t
    share = []
    for k in range(1, 4 * n):
        to = peers_of(n)[k - 1]
        share.append(
            remote(panel.at[((me ^ k) * lane) // 128], notes.at[k], note_s.at[k], note_r.at[k], to))
        if k % 4 == 0:
            share.append(remote(low, lows.at[k // 4], low_s.at[k // 4], low_r.at[k // 4], to))
    for copy in share:
        copy.start()

    for k in send_order:
        if low_bit(k) == 1:
            continue
        for child in send_order:
            if child ^ low_bit(child) != k:
                continue
            for c in range(4):
                att(child, c).wait_recv()
                src = rq.at[child - 1, c] if c < 3 else ro.at[child - 1]
                dst = tmpq if c < 3 else tmpo
                copy = pltpu.make_async_copy(src, dst, load_sem.at[7])
                copy.start()
                copy.wait()
                if c < 3:
                    gq[k, c] = (gq[k, c].astype(F32) + tmpq[...].astype(F32)).astype(BF)
                else:
                    go[k] = (go[k].astype(F32) + tmpo[...].astype(F32)).astype(BF)
                if child == [j for j in send_order if j ^ low_bit(j) == k][-1]:
                    att_start(k, c)

    for c in range(4):
        att_start(1, c)

    @pl.when(sect == 1)
    def _():
        relay(0)
        for k in att_order:
            for c in ATT_RELAYED:
                att_lend(k, c).wait_recv()
                att_relay(k, c).start()

    for copy in share:
        copy.wait_recv()
    total = panel[(me * lane) // 128]
    for k in range(1, 4 * n):
        total = total + notes[k]
    sums_v[...] = total
    total = low[...]
    for k in range(1, n):
        total = total + lows[k]
    low_v[...] = total
    put(sums_v, sums_out)
    put(low_v, low_out)

    def final_feed(bu, bd, fu, fd):
        stores = []
        turn = [1] + list(range(n - 1, 1, -1))
        for k in turn:
            for a in (1, 0):
                own, got, buf, total = ((gu, ru, bu, fu), (gd, rd, bd, fd))[a]
                ffn(a, k).wait_recv()
                copy = load(got.at[k - 1], buf.at[k - 1], 2 + a)
                copy.wait()
                b = k & 1
                same = [other for other in turn if other & 1 == b]
                step = min(64, deep)

                def body(j):
                    sl = rows_of(j, step)
                    value = buf[k - 1, sl, :].astype(F32)
                    if k != same[0]:
                        value = value + total[b, sl, :]
                    elif b == 0:
                        value = value + own[0, sl, :].astype(F32)
                    total[b, sl, :] = value

                tiles(total.shape[1] // step, body)
                if k == same[-1]:
                    at = pl.ds(pl.multiple_of((zl ^ b) * half, half), half)
                    dst = gu_out.at[:, at] if a == 0 else gd_out.at[at, :]
                    stores.append(pltpu.make_async_copy(total.at[b], dst, load_sem.at[4 + 2 * a + b]))
                    stores[-1].start()
        for copy in stores:
            copy.wait()

    pl.run_scoped(
        final_feed,
        pltpu.VMEM((n - 1, deep, half), BF), pltpu.VMEM((n - 1, half, deep), BF),
        pltpu.VMEM((2, deep, half), F32), pltpu.VMEM((2, half, deep), F32),
    )

    def final_attention(bq, bo, fq, fo):
        last = [k for k in range(1, n) if k == low_bit(k)]
        stores = []
        for k in last:
            for c in (3, 0, 1, 2):
                att(k, c).wait_recv()
                src, buf = (rq.at[k - 1, c], bq.at[k - 1, c]) if c < 3 else (ro.at[k - 1], bo.at[k - 1])
                copy = load(src, buf, 2)
                copy.wait()
                step = min(64, deep)

                def body(j):
                    sl = rows_of(j, step)
                    if c < 3:
                        first = gq[0, c, sl, :].astype(F32) if k == 1 else fq[c, sl, :]
                        fq[c, sl, :] = first + bq[k - 1, c, sl, :].astype(F32)
                    else:
                        first = go[0, sl, :].astype(F32) if k == 1 else fo[sl, :]
                        fo[sl, :] = first + bo[k - 1, sl, :].astype(F32)

                tiles((deep if c < 3 else wide) // step, body)
                if k == last[-1]:
                    src, dst = (fq.at[c], gq_out.at[c]) if c < 3 else (fo, go_out)
                    stores.append(pltpu.make_async_copy(src, dst, load_sem.at[4 + c]))
                    stores[-1].start()
        for copy in stores:
            copy.wait()

    pl.run_scoped(
        final_attention,
        pltpu.VMEM((n - 1, 3, deep, wide), BF), pltpu.VMEM((n - 1, wide, deep), BF),
        pltpu.VMEM((3, deep, wide), F32), pltpu.VMEM((wide, deep), F32),
    )

    for i in range(4):
        @pl.when(sect == 0)
        def _():
            if i in (1, 2):
                ag8(i, 0).wait_send()
                ag8(i, 1).wait_send()
                corner8(i - 1).wait_send()
            forward8(i).wait_send()

        if i:
            rs8(i).wait_send()
        core8(i).wait_send()
    for i in range(6):
        ag(i // 2, i % 2).wait_send()
    to_chip(0).wait_send()
    to_chip(1).wait_send()
    for layer in range(2):
        @pl.when(sect == layer)
        def _():
            for k in range(1, n):
                ffn(0, k).wait_send()
                (lend if k in GRADS_RELAYED[layer] else direct)(k).wait_send()
            for k in GRADS_RELAYED[1 - layer]:
                ffn(1, k).wait_send()

    for k in range(1, n):
        for c in range(4):
            if c not in ATT_RELAYED:
                att(k, c).wait_send()
                continue

            @pl.when(sect == 0)
            def _():
                att_lend(k, c).wait_send()

            @pl.when(sect == 1)
            def _():
                att(k, c).wait_send()
                att_relay(k, c).wait_send()


    @pl.when(sect == 1)
    def _():
        over(0).wait_send()
        over(1).wait_send()

    for copy in share:
        copy.wait_send()
    for copy in outs:
        copy.wait()


def run_backward(dims, top, vec, prefix, slopes, weights, kept):
    n, seqs, heads, size, rows, deep, half = dims
    R, wide, D = seqs * rows, heads * size, n * deep
    V = lambda shape, dtype: pltpu.VMEM(shape, dtype)
    S = lambda *shape: jax.ShapeDtypeStruct(shape[:-1], shape[-1])
    any_ = pl.BlockSpec(memory_space=pl.ANY)
    vm = pl.BlockSpec(memory_space=pltpu.VMEM)
    sm = pl.BlockSpec(memory_space=pltpu.SMEM)
    dma = lambda k: pltpu.SemaphoreType.DMA((k,))
    outs = (
        S(R, D, F32), S(3, deep, wide, F32), S(wide, deep, F32), S(deep, 2 * half, F32), S(2 * half, deep, F32),
        S(8, 128, F32), S(24, 128, F32),
        S(n - 1, deep, half, BF), S(n - 1, half, deep, BF), S(n - 1, 3, deep, wide, BF), S(n - 1, wide, deep, BF),
        S(n - 1, half, deep, BF), S(n - 1, 3, deep, wide, BF),
    )
    scratch = [
        V((R, D), BF), V((R, D), BF), V((R, D), F32), V((R, D), BF), V((R, D), F32),
        V((8, R, D), BF), V((4, R, D), BF),
        V((n, deep, half), BF), V((n, half, deep), BF), V((n, 3, deep, wide), BF), V((n, wide, deep), BF),
        V((2, R, D), F32), V((R, D), F32), V((4, R, D), BF), V((4, R, D), BF), V((3, R, D), BF), V((3, R, D), BF),
        V((2, R, D), BF), V((2, R, D), BF), V((R, D), BF), V((R, D), BF),
        V((8, D), F32), V((1, 3 * wide), F32), V((1, half), F32), V((deep, wide), BF), V((wide, deep), BF),
        V((D // 128, 8, 128), F32), V((24, 128), F32), V((4 * n, 8, 128), F32), V((n, 24, 128), F32),
        V((8, 128), F32), V((24, 128), F32), dma(4 * n), dma(4 * n), dma(n), dma(n),
        dma(8), dma(4), dma(4), dma(2), dma(2),
        dma(8), dma(8), dma(4), dma(4), dma(4), dma(4), dma(4), dma(4),
        dma(6), dma(6), dma(4), dma(4), dma(2 * (n - 1)), dma(2 * (n - 1)), dma(4 * (n - 1)), dma(4 * (n - 1)), dma(n - 1), dma(n - 1),
        dma(4 * (n - 1)), dma(4 * (n - 1)), dma(4 * (n - 1)), dma(2), dma(2),
    ]
    return pl.pallas_call(
        functools.partial(backward_kernel, dims),
        out_shape=outs,
        in_specs=[vm, vm, sm, sm] + [any_] * 13,
        out_specs=(any_,) * len(outs),
        scratch_shapes=scratch,
        compiler_params=pltpu.CompilerParams(
            collective_id=1, has_side_effects=True, vmem_limit_bytes=62 * 1024 * 1024
        ),
    )(top, vec, prefix, slopes, *weights, *kept)


def on_device(activations, ln_gains, biases, w_qkv, qv_bias, w_out, w_up, up_bias, w_down, prefix):
    is_first = lax.axis_index("section") == 0
    plane = lax.axis_index("dp")
    place = lax.axis_index("tensor")
    planes = lax.axis_size("dp")
    tensors = lax.axis_size("tensor")
    seqs, rows, width = activations.shape[1:]
    heads, part = qv_bias.shape[2:]
    size = part * planes
    deep = w_qkv.shape[1]
    units = w_up.shape[2]
    lane = width // (planes * tensors)
    own = activations[0].reshape(seqs * rows, width)
    spot = (plane * tensors + place) * lane % 128

    def placed(block, start):
        length = block.shape[1]
        wide_block = jnp.tile(block.astype(F32), (1, 128 // length))
        lanes = jnp.arange(128)
        return jnp.where((lanes >= start) & (lanes < start + length), wide_block, 0.0)

    features = placed(jnp.concatenate([ln_gains[0], biases[0]]), spot)
    note = jnp.concatenate([
        features, jnp.zeros((2, 128), F32), placed(qv_bias[0].reshape(2 * heads, part), plane * part),
        placed(up_bias[0], plane * part),
    ])
    head_ids = place * heads + jnp.arange(heads)
    slopes = jnp.exp2(-8.0 * (head_ids.astype(F32) + 1.0) / (heads * tensors))
    dims = (planes, seqs, heads, size, rows, deep, units // 2)
    got = run_forward(
        dims, own, note, prefix, slopes, w_qkv[0].transpose(1, 0, 2), w_out[0], w_up[0], w_down[0]
    )
    output, weights, kept, vec = got[0], got[1:5], got[5:14], got[15]
    back = run_backward(dims, own, vec, prefix, slopes, weights, kept)
    grad_low, grad_q, grad_o, grad_u, grad_d, sums, low = back[:7]
    sums = lax.dynamic_slice_in_dim(sums, spot, lane, 1)
    low = lax.dynamic_slice_in_dim(low, plane * part, part, 1)
    ends = jnp.where(is_first, grad_low, output).reshape(seqs, rows, width)
    return (
        ends[None],
        sums[None, 0:2],
        sums[None, 2:6],
        grad_q.transpose(1, 0, 2)[None],
        low[: 2 * heads].reshape(1, 2, heads, part),
        grad_o[None],
        grad_u[None],
        low[2 * heads :][None],
        grad_d[None],
    )


def solution(mesh):
    in_specs = (
        P("section", "dp", "tensor", None),
        P("section", None, ("dp", "tensor")),
        P("section", None, ("dp", "tensor")),
        P("section", "dp", None, "tensor"),
        P("section", None, "tensor", "dp"),
        P("section", "tensor", "dp"),
        P("section", "dp", "tensor"),
        P("section", "tensor", "dp"),
        P("section", "tensor", "dp"),
        P("dp"),
    )
    out_specs = (
        P("section", "dp", "tensor", None),
        P("section", None, ("dp", "tensor")),
        P("section", None, ("dp", "tensor")),
        P("section", "dp", None, "tensor"),
        P("section", None, "tensor", "dp"),
        P("section", "tensor", "dp"),
        P("section", "dp", "tensor"),
        P("section", "tensor", "dp"),
        P("section", "tensor", "dp"),
    )
    return jax.shard_map(
        on_device, mesh=mesh, in_specs=in_specs, out_specs=out_specs, check_vma=False
    )
```
